512 devices in a mesh: wave: 32 (over y, x), field: 16 (over z, core).
Axes of the slice: x: 4, y: 8, z: 8, core: 2. Of those that a mesh axis runs over, the one named last changes fastest.
Arguments:
- spectra: bfloat16 [384, 2, 640, 64], P('wave', None, None, 'field'), may hold values from -6 to 6
- legendre: bfloat16 [384, 640, 768], P('wave', None, 'field'), may hold values from -0.3125 to 0.3125
- lat_weight: float32 [768], P('field'), may hold values from 0.25 to 0.75
- wave_of_slot: int32 [384], replicated, may hold values from 0 to 639, as said below
- lat_of_row: int32 [1536], replicated, may hold values from 0 to 1535, as said below
- lon_count: int32 [768], replicated, may hold values from 16 to 3088
Outputs:
- grid_field: bfloat16 [1536, 64, 3200], P(('wave', 'field'))
- spectral_out: float32 [384, 2, 640, 64], P('wave', None, None, 'field')
The draws below stay inside these ranges and needn't reach their ends.
Inputs may be any that keep to these rules, and one draw needn't show every extreme that they name: `wave_of_slot`: the 384 wavenumbers are distinct. `lat_of_row`: each latitude stands in exactly one row; the latitude j of row r has min(j, 1535 - j) in the block of 48 hemisphere rows numbered (r // 3) mod (16).
All inputs are finite; a program needn't handle non-finite values.
Results may differ from the reference program's by a relative error of at most 0.0081.
Values may be sent and summed in bfloat16 or wider, within the bound.
No kernel may reach another device: no remote copies, remote signals or barrier semaphores. Data moves between devices by JAX's collectives and lax.ppermute only.
A program may use at most 128 MiB of HBM per device.

```python
import math
import jax
import jax.numpy as jnp
from jax import lax

NHALF = 768
NDEG = 640
MW = 384
FL = 64
NLAT = 1536
BAND = 48
ROWS_DEV = 3
LONPAD = 3200


def draw_wave_of_slot(key, part):
    key = jax.random.fold_in(key, 11)
    key_middle, key_order = jax.random.split(key)
    if MW >= 3:
        middle = 1 + jax.random.permutation(key_middle, NDEG - 2)
        chosen = jnp.concatenate([jnp.array([0, NDEG - 1], jnp.int32), middle[:MW - 2].astype(jnp.int32)])
    else:
        middle = 1 + jax.random.permutation(key_middle, NDEG - 1)
        chosen = jnp.concatenate([jnp.array([0], jnp.int32), middle[:MW - 1].astype(jnp.int32)])
    return chosen[jax.random.permutation(key_order, MW)]


def draw_lat_of_row(key, part):
    key = jax.random.fold_in(key, 23)
    blocks = NHALF // BAND
    split_keys = jax.random.split(key, blocks)
    starts = jnp.arange(blocks, dtype=jnp.int32)[:, None] * BAND
    within = jnp.arange(BAND, dtype=jnp.int32)[None, :]
    north_rows = starts + within
    south_rows = NLAT - 1 - north_rows
    band_lats = jnp.concatenate([north_rows, south_rows], axis=1)
    orders = jax.vmap(lambda single: jax.random.permutation(single, 2 * BAND))(split_keys)
    shuffled = jnp.take_along_axis(band_lats, orders.astype(jnp.int32), axis=1)
    wave_count = 2 * BAND // ROWS_DEV
    return shuffled.reshape(blocks, wave_count, ROWS_DEV).transpose(1, 0, 2).reshape(NLAT).astype(jnp.int32)


def draw_lon_count(key, part):
    key = jax.random.fold_in(key, 37)
    row_ids = jnp.arange(NHALF, dtype=jnp.int32)
    added_points = 4 * jax.random.randint(key, (NHALF,), 0, 2, dtype=jnp.int32)
    counts = 4 * row_ids + 16 + added_points
    counts = jnp.where(row_ids == 0, 16, counts)
    return jnp.where(row_ids == NHALF - 1, 4 * NHALF + 16, counts).astype(jnp.int32)


def shard_levels(key, dims, cuts, least, largest):
    gain = 1.0
    for axis_at, shards_of in cuts:
        draws = jax.random.uniform(jax.random.fold_in(jax.random.fold_in(key, 6), axis_at), (shards_of,), jnp.float32, least / len(cuts), largest / len(cuts))
        gain = gain * jnp.repeat(jnp.exp(draws), dims[axis_at] // shards_of).reshape((-1,) + (1,) * (len(dims) - 1 - axis_at))
    return gain


def centred(own_key, extent, width, most, cuts=(), kind=jnp.bfloat16):
    entries = jax.random.normal(own_key, extent, jnp.float32) * width
    if len(cuts) > 0:
        entries = shard_levels(own_key, extent, cuts, -0.22, 0.18) * entries
    return jnp.clip(entries, min=-most, max=most).astype(kind)


def setup_inputs(seed: int = 0) -> dict:
    key_of = jax.random.split(jax.random.key(seed), 7)
    return {
        "spectra": centred(key_of[0], (MW, 2, NDEG, FL), 1.0, 6.0, ((0, 32), (3, 16))),
        "legendre": centred(key_of[1], (MW, NDEG, NHALF), (NDEG // 2) ** -0.5, 0.3125, ((0, 32), (2, 16))),
        "lat_weight": jnp.clip(0.25 + 0.5 * jax.random.uniform(key_of[2], (NHALF,), jnp.float32) ** shard_levels(key_of[2], (NHALF,), ((0, 16),), -0.2, 0.2), 0.25, 0.75),
        "wave_of_slot": draw_wave_of_slot(jax.random.fold_in(key_of[6], 71), 0),
        "lat_of_row": draw_lat_of_row(jax.random.fold_in(key_of[6], 71), 0),
        "lon_count": draw_lon_count(jax.random.fold_in(key_of[6], 71), 0),
    }


def fourier_table(wavenumbers, lon_points, padded):
    columns = lax.broadcasted_iota(jnp.int32, (wavenumbers.shape[0], padded), 1)
    phase = wavenumbers[:, None] * columns % lon_points
    angle = phase.astype(jnp.float32) * (2.0 * math.pi / lon_points.astype(jnp.float32))
    inside = columns < lon_points
    cosine = jnp.where(inside, jnp.cos(angle), 0.0)
    sine = jnp.where(inside, -jnp.sin(angle), 0.0)
    return jnp.stack([cosine, sine], axis=1).astype(jnp.bfloat16)

def reference(spectra, legendre, lat_weight, wave_of_slot, lat_of_row, lon_count):
    half_deg = NDEG // 2
    parity_table = legendre.reshape(MW, half_deg, 2, NHALF).astype(jnp.float32)
    offsets = 2 * lax.broadcasted_iota(jnp.int32, (MW, half_deg, 2), 1) + lax.broadcasted_iota(jnp.int32, (MW, half_deg, 2), 2)
    valid_rows = offsets < (NDEG - wave_of_slot)[:, None, None]
    shaped = jnp.where(valid_rows[:, None, :, :, None], spectra.reshape(MW, 2, half_deg, 2, FL).astype(jnp.float32), 0.0)
    parity_sums = jnp.einsum('skph,sckpf->scphf', parity_table, shaped)
    northern = parity_sums[:, :, 0] + parity_sums[:, :, 1]
    southern = parity_sums[:, :, 0] - parity_sums[:, :, 1]
    latitudes = jnp.concatenate([northern, southern[:, :, ::-1]], axis=2).astype(jnp.bfloat16)
    wave_scale = 1.0 / math.sqrt(MW)

    def grid_row(latitude):
        hemisphere = jnp.minimum(latitude, NLAT - 1 - latitude)
        lon_points = lon_count[hemisphere]
        lon_table = fourier_table(wave_of_slot, lon_points, LONPAD).astype(jnp.float32)
        coefficients = lax.dynamic_index_in_dim(latitudes, latitude, 2, keepdims=False).astype(jnp.float32)
        grid_line = (jnp.einsum('mcf,mck->fk', coefficients, lon_table) * wave_scale).astype(jnp.bfloat16)
        partner = jnp.roll(grid_line, -1, axis=0)
        product = (grid_line.astype(jnp.float32) * partner.astype(jnp.float32)).astype(jnp.bfloat16)
        analysed = jnp.einsum('fk,mck->mcf', product.astype(jnp.float32), lon_table)
        return (grid_line, (analysed / jnp.sqrt(lon_points.astype(jnp.float32))).astype(jnp.bfloat16))
    grid_field, analysed_rows = lax.map(grid_row, lat_of_row)
    by_latitude = jnp.zeros((NLAT, MW, 2, FL), jnp.bfloat16).at[lat_of_row].set(analysed_rows)
    ordered = jnp.transpose(by_latitude, (1, 2, 0, 3)).astype(jnp.float32)
    north_part = ordered[:, :, :NHALF]
    south_part = ordered[:, :, NHALF:][:, :, ::-1]
    weights = lat_weight[None, None, :, None]
    weighted = jnp.stack([(north_part + south_part) * weights, (north_part - south_part) * weights], axis=2).astype(jnp.bfloat16)
    summed = jnp.einsum('skph,scphf->sckpf', parity_table, weighted.astype(jnp.float32)).reshape(MW, 2, NDEG, FL)
    kept_rows = valid_rows.reshape(MW, NDEG)[:, None, :, None]
    return (grid_field, jnp.where(kept_rows, summed, 0.0))
```

```python
import functools
import math

import jax
import jax.numpy as jnp
from jax import lax
from jax.experimental import pallas as pl
from jax.experimental.pallas import tpu as pltpu
from jax.sharding import PartitionSpec as P

LONPAD = 3200
LANES = 128
BLOCK = 256
BLOCKS = -(-LONPAD // BLOCK)
MESH_VMEM = 56 * 1024 * 1024

NT = (((1,), (1,)), ((), ()))
NN = (((1,), (0,)), ((), ()))
TN = (((0,), (0,)), ((), ()))


def dot(a, b, dims):
    return lax.dot_general(a, b, dims, preferred_element_type=jnp.float32)


def params():
    return pltpu.CompilerParams(vmem_limit_bytes=MESH_VMEM)


def cost(micros):
    return pl.CostEstimate(flops=0, bytes_accessed=int(micros * 3.7e6), transcendentals=0)


def smem():
    return pl.BlockSpec(memory_space=pltpu.SMEM)


def vmem():
    return pl.BlockSpec(memory_space=pltpu.VMEM)


def side_of(core):
    return 1 - 2 * core


def legendre_rows_kernel(wave_id, field_id, wave_of_slot, lat_of_row, legendre, out, pick, south, *, waves, fields):
    slots, band, degrees = legendre.shape
    rows = out.shape[1]
    row_count = rows // waves
    half = lat_of_row.shape[0] // 2
    own, field = wave_id[0], field_id[0]
    lane = lax.broadcasted_iota(jnp.int32, (1, LANES), 1)
    for row in range(rows):
        member, wave = divmod(row, waves)
        lat = lat_of_row[(wave * fields + field) * row_count + member]
        is_south = lat >= half
        hemi = jnp.where(is_south, 2 * half - 1 - lat, lat) - field * band
        pick[row : row + 1, :] = (lane == hemi).astype(jnp.float32)
        south[row : row + 1, :] = jnp.broadcast_to(is_south.astype(jnp.float32), (1, LANES))
    offsets = lax.broadcasted_iota(jnp.int32, (1, degrees), 1)
    odd = (offsets & 1).astype(jnp.float32)
    sign = 1.0 - 2.0 * (south[:, :1] * odd)
    chosen = pick[:, :band].astype(jnp.bfloat16)
    for slot in range(slots):
        table = dot(chosen, legendre[slot], NN) * sign
        live = offsets < degrees - wave_of_slot[own * slots + slot]
        out[slot] = jnp.where(live, table, 0.0).astype(jnp.bfloat16)


def sin_cos(phase, period):
    inverse = 1.0 / period
    turns = (phase - jnp.floor(phase * inverse + 0.5) * period) * inverse
    quarter = jnp.floor(4.0 * turns + 0.5)
    w = (2.0 * math.pi) * (turns - 0.25 * quarter)
    w2 = w * w
    sine = w * (1.0 + w2 * (-1.0 / 6 + w2 * (1.0 / 120 + w2 * (-1.0 / 5040 + w2 * (1.0 / 362880)))))
    cosine = 1.0 + w2 * (-0.5 + w2 * (1.0 / 24 + w2 * (-1.0 / 720 + w2 * (1.0 / 40320))))
    size = jnp.abs(quarter)
    odd = size == 1.0
    flipped = size >= 2.0
    cos_out = jnp.where(odd, sine, cosine)
    sin_out = jnp.where(odd, cosine, sine)
    cos_out = jnp.where(flipped | (quarter == 1.0), -cos_out, cos_out)
    sin_out = jnp.where(flipped | (quarter == -1.0), -sin_out, sin_out)
    return cos_out, sin_out


def fourier_tables_kernel(
    wave_id, field_id, lat_of_row, lon_count, lat_weight, waves_row,
    inner, inner_t, outer_fwd, outer_inv, place, *, fields, zs,
):
    row_count = inner.shape[0]
    band = lat_weight.shape[0]
    half = lon_count.shape[0]
    slots = waves_row.shape[1]
    steps = outer_fwd.shape[1]
    wave, field = wave_id[0], field_id[0]
    for member in range(row_count):
        lat = lat_of_row[(wave * fields + field) * row_count + member]
        hemi = jnp.where(lat >= half, 2 * half - 1 - lat, lat)
        points = lon_count[hemi].astype(jnp.float32)
        period = jnp.broadcast_to(points, (1, LANES))
        weight = lat_weight[hemi - field * band] / jnp.sqrt(period)
        for part in range(slots // LANES):
            m = waves_row[:, part * LANES : (part + 1) * LANES]
            at = part * 2 * LANES
            x = lax.broadcasted_iota(jnp.int32, (BLOCK, LANES), 0).astype(jnp.float32)
            cosine, sine = sin_cos(x * m, period)
            both = jnp.concatenate([cosine, -sine], axis=1)
            inner[member, :, at : at + 2 * LANES] = both.astype(jnp.bfloat16)
            inner_t[member, at : at + 2 * LANES, :] = both.T.astype(jnp.bfloat16)
            x = (BLOCK * lax.broadcasted_iota(jnp.int32, (steps, LANES), 0)).astype(jnp.float32)
            cosine, sine = sin_cos(x * m, period)
            both = jnp.concatenate([cosine, sine], axis=1)
            outer_fwd[member, :, at : at + 2 * LANES] = both * (1.0 / math.sqrt(slots))
            outer_inv[member, :, at : at + 2 * LANES] = both * jnp.concatenate([weight, weight], axis=1)
    at = lax.broadcasted_iota(jnp.int32, (LANES, LANES), 1)
    chunk, part, low = (at >> 3) & 7, (at >> 2) & 1, at & 3
    core = (field & 1) ^ (at >> 6)
    back = (chunk + 1) >> 1
    other = ((chunk & 1) ^ 1) & (chunk > 0).astype(jnp.int32)
    z = ((field >> 1) - side_of(core) * back + zs) & (zs - 1)
    target = part * 64 + (2 * z + (core ^ other)) * 4 + low
    place[...] = (lax.broadcasted_iota(jnp.int32, (LANES, LANES), 0) == target).astype(jnp.bfloat16)


def legendre_forward_kernel(own, one, two, three, four, table, *refs, second):
    swapped, out, held = (None,) * (3 - len(refs)) + refs
    slots, rows, degrees = table.shape
    waves = out.shape[0]
    row_count = rows // waves
    each = slots * row_count
    empty = jnp.zeros((64, degrees), jnp.float32)
    for pair in range(slots // 2):
        at = pl.ds(16 * pair, 16)
        both = [own[at, :]] + [piece[i, at, :] for piece in (one, two, three) for i in range(2)] + [four[at, :]]
        both = [b.astype(jnp.float32) for b in both]
        for half in range(2):
            slot = 2 * pair + half
            spec = [b[8 * half : 8 * half + 8] for b in both]
            spec = [empty] + spec if second else spec + [empty]
            sums = dot(table[slot], jnp.concatenate(spec, axis=0).astype(jnp.bfloat16), NT)
            for member in range(row_count):
                held[pl.ds(slot * row_count + member, waves, stride=each), :] = sums[
                    waves * member : waves * (member + 1)
                ]
    for wave in range(waves):
        lines = held[wave * each : (wave + 1) * each, :]
        if swapped is not None:
            lines = lines + swapped[wave].astype(jnp.float32)
        out[wave] = lines.astype(jnp.bfloat16)


def legendre_inverse_kernel(
    arrived, swapped, table, table_swapped, own, one, one_other, two, two_other, three, four, held, held_swapped
):
    slots, rows, degrees = table.shape
    waves = arrived.shape[0]
    row_count = rows // waves
    each = slots * row_count
    for wave in range(waves):
        held[wave * each : (wave + 1) * each, :] = arrived[wave].astype(jnp.float32)
        held_swapped[wave * each : (wave + 1) * each, :] = pltpu.roll(swapped[wave].astype(jnp.float32), 64, 1)

    def share(ref, slot, legendre):
        weighted = jnp.concatenate(
            [ref[pl.ds(slot * row_count + member, waves, stride=each), :] for member in range(row_count)], axis=0
        )
        return dot(weighted[:, :64].astype(jnp.bfloat16), legendre[slot], TN)

    for pair in range(slots // 2):
        at = pl.ds(16 * pair, 16)
        sums = [
            share(held, slot, table) + share(held_swapped, slot, table_swapped) for slot in (2 * pair, 2 * pair + 1)
        ]
        pieces = [jnp.concatenate([s[8 * chunk : 8 * chunk + 8] for s in sums], axis=0) for chunk in range(8)]
        own[at, :] = pieces[0]
        pieces = [piece.astype(jnp.bfloat16) for piece in pieces]
        one[at, :] = pieces[1]
        one_other[at, :] = pieces[2]
        two[at, :] = pieces[3]
        two_other[at, :] = pieces[4]
        three[0, at, :] = pieces[5]
        three[1, at, :] = pieces[6]
        four[at, :] = pieces[7]


def fourier_kernel(
    wave_id, field_id, lat_of_row, lon_count, arrived, inner, inner_t, outer_fwd, outer_inv, place,
    grid_out, sent, held, back, turned, products, *, fields,
):
    row_count = inner.shape[0]
    waves, each, _ = arrived.shape
    slots = waves * each // row_count
    parts = slots // LANES
    half = lon_count.shape[0]
    levels = grid_out.shape[1]
    wave, field = wave_id[0], field_id[0]
    for source in range(waves):
        held[source * each : (source + 1) * each, :] = arrived[source].astype(jnp.float32)
    for member in range(row_count):
        lat = lat_of_row[(wave * fields + field) * row_count + member]
        hemi = jnp.where(lat >= half, 2 * half - 1 - lat, lat)
        points = lon_count[hemi]
        lines = held[pl.ds(member, slots, stride=row_count), :].astype(jnp.bfloat16)
        coef = dot(place[...], lines, NT)
        for step in range(BLOCKS):
            rows = pl.ds(step * levels, levels)
            for part in range(parts):
                real = coef[:levels, part * LANES : (part + 1) * LANES]
                imag = coef[levels:, part * LANES : (part + 1) * LANES]
                at = part * 2 * LANES
                cosine = outer_fwd[member, step : step + 1, at : at + LANES]
                sine = outer_fwd[member, step : step + 1, at + LANES : at + 2 * LANES]
                turned[rows, at : at + LANES] = (real * cosine - imag * sine).astype(jnp.bfloat16)
                turned[rows, at + LANES : at + 2 * LANES] = (real * sine + imag * cosine).astype(jnp.bfloat16)
        values = dot(turned[...], inner_t[member], NN)
        for step in range(BLOCKS):
            width = min(BLOCK, LONPAD - step * BLOCK)
            line = values[step * levels : (step + 1) * levels]
            x = step * BLOCK + lax.broadcasted_iota(jnp.int32, (1, BLOCK), 1)
            line = jnp.where(x < points, line, 0.0).astype(jnp.bfloat16)
            grid_out[member, :, step * BLOCK : step * BLOCK + width] = line[:, :width]
            line = line.astype(jnp.float32)
            partner = pltpu.roll(line, levels - 1, 0)
            products[step * levels : (step + 1) * levels, :] = (line * partner).astype(jnp.bfloat16)
        reals, imags = [], []
        for part in range(parts):
            at = part * 2 * LANES
            sums = dot(products[...], inner[member, :, at : at + 2 * LANES], NN)
            real = jnp.zeros((levels, LANES), jnp.float32)
            imag = jnp.zeros((levels, LANES), jnp.float32)
            for step in range(BLOCKS):
                rows = slice(step * levels, (step + 1) * levels)
                cosine = outer_inv[member, step : step + 1, at : at + LANES]
                sine = outer_inv[member, step : step + 1, at + LANES : at + 2 * LANES]
                real += sums[rows, :LANES] * cosine + sums[rows, LANES:] * sine
                imag += sums[rows, LANES:] * cosine - sums[rows, :LANES] * sine
            reals.append(real)
            imags.append(imag)
        analysed = jnp.concatenate([jnp.concatenate(reals, axis=1), jnp.concatenate(imags, axis=1)], axis=0)
        back[pl.ds(member, slots, stride=row_count), :] = dot(
            analysed.T.astype(jnp.bfloat16), place[...], NN
        )
    for source in range(waves):
        sent[source] = back[source * each : (source + 1) * each, :].astype(jnp.bfloat16)


def shards(spectra, legendre, lat_weight, wave_of_slot, lat_of_row, lon_count):
    waves = lax.axis_size("wave")
    fields = lax.axis_size("field")
    zs = fields // 2
    wave_id = lax.axis_index("wave").astype(jnp.int32).reshape(1)
    field_id = lax.axis_index("field").astype(jnp.int32).reshape(1)
    slots, _, degrees, cols = spectra.shape
    band = legendre.shape[2]
    rows = 2 * band
    row_count = rows // waves
    all_slots = wave_of_slot.shape[0]
    levels = cols * fields
    each = row_count * slots
    coded = slots * 2 * cols

    def hop(x, by, cross=0):
        pairs = [
            (i, (2 * (i // 2 + side_of(i % 2) * by) + (i % 2 ^ cross)) % fields) for i in range(fields)
        ]
        return lax.ppermute(x, "field", pairs)

    def swap(x):
        return hop(x, 0, 1)

    own = jnp.transpose(spectra, (0, 1, 3, 2)).reshape(coded, degrees)
    four = hop(own, 4)
    legendre = jnp.transpose(legendre, (0, 2, 1))
    legendre_swapped = swap(legendre)
    partner, legendre = lax.optimization_barrier((swap(own), legendre))
    pair = jnp.stack([own, partner])
    two = hop(pair, 2)
    one = hop(pair, 1)
    def order_rows(values, band_of):
        return pl.pallas_call(
            functools.partial(legendre_rows_kernel, waves=waves, fields=fields),
            out_shape=jax.ShapeDtypeStruct((slots, rows, degrees), jnp.bfloat16),
            in_specs=[smem(), smem(), smem(), smem(), vmem()],
            out_specs=vmem(),
            scratch_shapes=[pltpu.VMEM((rows, LANES), jnp.float32)] * 2,
            compiler_params=params(),
            cost_estimate=cost(3),
            name="legendre_rows",
        )(wave_id, band_of, wave_of_slot, lat_of_row, values)

    two, table = lax.optimization_barrier((two, order_rows(legendre, field_id)))
    two, legendre_swapped = lax.optimization_barrier((two, legendre_swapped))
    three = hop(two, 1)
    table_swapped = order_rows(legendre_swapped, field_id ^ 1)

    def forward(legendre_table, second, *swapped):
        return pl.pallas_call(
            functools.partial(legendre_forward_kernel, second=second),
            out_shape=jax.ShapeDtypeStruct((waves, each, LANES), jnp.bfloat16),
            in_specs=[vmem()] * (6 + len(swapped)),
            out_specs=vmem(),
            scratch_shapes=[pltpu.VMEM((waves * each, LANES), jnp.float32)],
            compiler_params=params(),
            cost_estimate=cost(2),
            name="legendre_forward",
        )(own, one, two, three, four, legendre_table, *swapped)

    outgoing = forward(table, False, swap(forward(table_swapped, True)))
    outgoing, lat_weight = lax.optimization_barrier((outgoing, lat_weight))
    arrived = lax.all_to_all(outgoing, "wave", split_axis=0, concat_axis=0, tiled=True)

    steps = 16
    inner, inner_t, outer_fwd, outer_inv, place = pl.pallas_call(
        functools.partial(fourier_tables_kernel, fields=fields, zs=zs),
        out_shape=(
            jax.ShapeDtypeStruct((row_count, BLOCK, 2 * all_slots), jnp.bfloat16),
            jax.ShapeDtypeStruct((row_count, 2 * all_slots, BLOCK), jnp.bfloat16),
            jax.ShapeDtypeStruct((row_count, steps, 2 * all_slots), jnp.float32),
            jax.ShapeDtypeStruct((row_count, steps, 2 * all_slots), jnp.float32),
            jax.ShapeDtypeStruct((LANES, LANES), jnp.bfloat16),
        ),
        in_specs=[smem()] * 5 + [vmem()],
        out_specs=(vmem(),) * 5,
        compiler_params=params(),
        cost_estimate=cost(4),
        name="fourier_tables",
    )(
        wave_id, field_id, lat_of_row, lon_count, lat_weight,
        wave_of_slot.astype(jnp.float32).reshape(1, all_slots),
    )

    grid_field, sent = pl.pallas_call(
        functools.partial(fourier_kernel, fields=fields),
        out_shape=(
            jax.ShapeDtypeStruct((row_count, levels, LONPAD), jnp.bfloat16),
            jax.ShapeDtypeStruct((waves, each, LANES), jnp.bfloat16),
        ),
        in_specs=[smem()] * 4 + [vmem()] * 6,
        out_specs=(vmem(), vmem()),
        scratch_shapes=[
            pltpu.VMEM((waves * each, LANES), jnp.float32),
            pltpu.VMEM((waves * each, LANES), jnp.float32),
            pltpu.VMEM((BLOCKS * levels, 2 * all_slots), jnp.bfloat16),
            pltpu.VMEM((BLOCKS * levels, BLOCK), jnp.bfloat16),
        ],
        compiler_params=params(),
        cost_estimate=cost(7),
        name="fourier",
    )(wave_id, field_id, lat_of_row, lon_count, arrived, inner, inner_t, outer_fwd, outer_inv, place)

    returned = lax.all_to_all(sent, "wave", split_axis=0, concat_axis=0, tiled=True)

    half = jax.ShapeDtypeStruct((coded, degrees), jnp.bfloat16)
    total, one, one_other, two, two_other, three, four = pl.pallas_call(
        legendre_inverse_kernel,
        out_shape=(
            jax.ShapeDtypeStruct((coded, degrees), jnp.float32), half, half, half, half,
            jax.ShapeDtypeStruct((2, coded, degrees), jnp.bfloat16), half,
        ),
        in_specs=[vmem()] * 4,
        out_specs=(vmem(),) * 7,
        scratch_shapes=[pltpu.VMEM((waves * each, LANES), jnp.float32)] * 2,
        compiler_params=params(),
        cost_estimate=cost(3),
        name="legendre_inverse",
    )(returned, swap(returned), table, table_swapped)

    def add(a, b):
        return (a.astype(jnp.float32) + b.astype(jnp.float32)).astype(jnp.bfloat16)

    three = hop(three, -1)
    landed = [hop(four, -4), hop(one, -1), hop(one_other, -1, 1)]
    landed += [hop(add(two, three[0]), -2), hop(add(two_other, three[1]), -2, 1)]
    total = total + sum(x.astype(jnp.float32) for x in landed)
    spectral = jnp.transpose(total.reshape(slots, 2, cols, degrees), (0, 1, 3, 2))
    return grid_field, spectral


def solution(mesh):
    in_specs = (P("wave", None, None, "field"), P("wave", None, "field"), P("field"), P(), P(), P())
    out_specs = (P(("wave", "field"), None, None), P("wave", None, None, "field"))
    return jax.shard_map(shards, mesh=mesh, in_specs=in_specs, out_specs=out_specs, check_vma=False)
```

```python
import functools
import math

import jax
import jax.numpy as jnp
from jax import lax
from jax.experimental import pallas as pl
from jax.experimental.pallas import tpu as pltpu
from jax.sharding import PartitionSpec as P

LONPAD = 3200
LANES = 128
BLOCK = 256
BLOCKS = -(-LONPAD // BLOCK)

NT = (((1,), (1,)), ((), ()))
NN = (((1,), (0,)), ((), ()))
TN = (((0,), (0,)), ((), ()))


def dot(a, b, dims):
    return lax.dot_general(a, b, dims, preferred_element_type=jnp.float32)


def params(mebibytes):
    return pltpu.CompilerParams(vmem_limit_bytes=mebibytes * 1024 * 1024)


def cost(micros):
    return pl.CostEstimate(flops=0, bytes_accessed=int(micros * 3.7e6), transcendentals=0)


def smem():
    return pl.BlockSpec(memory_space=pltpu.SMEM)


def vmem():
    return pl.BlockSpec(memory_space=pltpu.VMEM)


def side_of(core):
    return 1 - 2 * core


def legendre_rows_kernel(wave_id, field_id, wave_of_slot, lat_of_row, legendre, out, pick, south, *, waves, fields):
    slots, band, degrees = legendre.shape
    rows = out.shape[1]
    row_count = rows // waves
    half = lat_of_row.shape[0] // 2
    own, field = wave_id[0], field_id[0]
    lane = lax.broadcasted_iota(jnp.int32, (1, LANES), 1)
    for row in range(rows):
        member, wave = divmod(row, waves)
        lat = lat_of_row[(wave * fields + field) * row_count + member]
        is_south = lat >= half
        hemi = jnp.where(is_south, 2 * half - 1 - lat, lat) - field * band
        pick[row : row + 1, :] = (lane == hemi).astype(jnp.float32)
        south[row : row + 1, :] = jnp.broadcast_to(is_south.astype(jnp.float32), (1, LANES))
    offsets = lax.broadcasted_iota(jnp.int32, (1, degrees), 1)
    odd = (offsets & 1).astype(jnp.float32)
    sign = 1.0 - 2.0 * (south[:, :1] * odd)
    chosen = pick[:, :band].astype(jnp.bfloat16)
    for slot in range(slots):
        table = dot(chosen, legendre[slot], NN) * sign
        live = offsets < degrees - wave_of_slot[own * slots + slot]
        out[slot] = jnp.where(live, table, 0.0).astype(jnp.bfloat16)


def sin_cos(phase, period):
    inverse = 1.0 / period
    turns = (phase - jnp.floor(phase * inverse + 0.5) * period) * inverse
    quarter = jnp.floor(4.0 * turns + 0.5)
    w = (2.0 * math.pi) * (turns - 0.25 * quarter)
    w2 = w * w
    sine = w * (1.0 + w2 * (-1.0 / 6 + w2 * (1.0 / 120 + w2 * (-1.0 / 5040 + w2 * (1.0 / 362880)))))
    cosine = 1.0 + w2 * (-0.5 + w2 * (1.0 / 24 + w2 * (-1.0 / 720 + w2 * (1.0 / 40320))))
    size = jnp.abs(quarter)
    odd = size == 1.0
    flipped = size >= 2.0
    cos_out = jnp.where(odd, sine, cosine)
    sin_out = jnp.where(odd, cosine, sine)
    cos_out = jnp.where(flipped | (quarter == 1.0), -cos_out, cos_out)
    sin_out = jnp.where(flipped | (quarter == -1.0), -sin_out, sin_out)
    return cos_out, sin_out


def fourier_tables_kernel(
    wave_id, field_id, lat_of_row, lon_count, lat_weight, waves_row,
    inner, inner_t, outer_fwd, outer_inv, place, *, fields, zs,
):
    row_count = inner.shape[0]
    band = lat_weight.shape[0]
    half = lon_count.shape[0]
    slots = waves_row.shape[1]
    steps = outer_fwd.shape[1]
    wave, field = wave_id[0], field_id[0]
    for member in range(row_count):
        lat = lat_of_row[(wave * fields + field) * row_count + member]
        hemi = jnp.where(lat >= half, 2 * half - 1 - lat, lat)
        points = lon_count[hemi].astype(jnp.float32)
        period = jnp.broadcast_to(points, (1, LANES))
        weight = lat_weight[hemi - field * band] / jnp.sqrt(period)
        for part in range(slots // LANES):
            m = waves_row[:, part * LANES : (part + 1) * LANES]
            at = part * 2 * LANES
            x = lax.broadcasted_iota(jnp.int32, (BLOCK, LANES), 0).astype(jnp.float32)
            cosine, sine = sin_cos(x * m, period)
            both = jnp.concatenate([cosine, -sine], axis=1)
            inner[member, :, at : at + 2 * LANES] = both.astype(jnp.bfloat16)
            inner_t[member, at : at + 2 * LANES, :] = both.T.astype(jnp.bfloat16)
            x = (BLOCK * lax.broadcasted_iota(jnp.int32, (steps, LANES), 0)).astype(jnp.float32)
            cosine, sine = sin_cos(x * m, period)
            both = jnp.concatenate([cosine, sine], axis=1)
            outer_fwd[member, :, at : at + 2 * LANES] = both * (1.0 / math.sqrt(slots))
            outer_inv[member, :, at : at + 2 * LANES] = both * jnp.concatenate([weight, weight], axis=1)
    at = lax.broadcasted_iota(jnp.int32, (LANES, LANES), 1)
    chunk, part, low = (at >> 3) & 7, (at >> 2) & 1, at & 3
    core = (field & 1) ^ (at >> 6)
    back = (chunk + 1) >> 1
    other = ((chunk & 1) ^ 1) & (chunk > 0).astype(jnp.int32)
    z = ((field >> 1) - side_of(core) * back + zs) & (zs - 1)
    target = part * 64 + (2 * z + (core ^ other)) * 4 + low
    place[...] = (lax.broadcasted_iota(jnp.int32, (LANES, LANES), 0) == target).astype(jnp.bfloat16)


def legendre_forward_kernel(*refs):
    pieces, (table, table_swapped, out, held) = refs[:-4], refs[-4:]
    slots, rows, degrees = table.shape
    waves = out.shape[0]
    row_count = rows // waves
    each = slots * row_count
    for pair in range(slots // 2):
        both = [piece[16 * pair : 16 * pair + 16, :].astype(jnp.float32) for piece in pieces]
        for half in range(2):
            slot = 2 * pair + half
            spec = jnp.concatenate([b[8 * half : 8 * half + 8] for b in both], axis=0).astype(jnp.bfloat16)
            sums = jnp.concatenate([dot(table[slot], spec, NT), dot(table_swapped[slot], spec, NT)], axis=1)
            for member in range(row_count):
                held[pl.ds(slot * row_count + member, waves, stride=each), :] = sums[
                    waves * member : waves * (member + 1)
                ]
    for wave in range(waves):
        out[wave] = held[wave * each : (wave + 1) * each, :].astype(jnp.bfloat16)


def legendre_inverse_kernel(
    arrived, swapped, table, table_swapped, own, one, one_other, two, two_other, three, four, held, held_swapped
):
    slots, rows, degrees = table.shape
    waves = arrived.shape[0]
    row_count = rows // waves
    each = slots * row_count
    for wave in range(waves):
        held[wave * each : (wave + 1) * each, :] = arrived[wave].astype(jnp.float32)
        held_swapped[wave * each : (wave + 1) * each, :] = pltpu.roll(swapped[wave].astype(jnp.float32), 64, 1)

    def share(ref, slot, legendre):
        weighted = jnp.concatenate(
            [ref[pl.ds(slot * row_count + member, waves, stride=each), :] for member in range(row_count)], axis=0
        )
        return dot(weighted[:, :64].astype(jnp.bfloat16), legendre[slot], TN)

    for pair in range(slots // 2):
        at = pl.ds(16 * pair, 16)
        sums = [
            share(held, slot, table) + share(held_swapped, slot, table_swapped) for slot in (2 * pair, 2 * pair + 1)
        ]
        pieces = [jnp.concatenate([s[8 * chunk : 8 * chunk + 8] for s in sums], axis=0) for chunk in range(8)]
        own[at, :] = pieces[0]
        pieces = [piece.astype(jnp.bfloat16) for piece in pieces]
        one[at, :] = pieces[1]
        one_other[at, :] = pieces[2]
        two[at, :] = pieces[3]
        two_other[at, :] = pieces[4]
        three[0, at, :] = pieces[5]
        three[1, at, :] = pieces[6]
        four[at, :] = pieces[7]


def fourier_kernel(
    wave_id, field_id, lat_of_row, lon_count, arrived, swapped, inner, inner_t, outer_fwd, outer_inv, place,
    grid_out, sent, held, back, turned, products, *, fields,
):
    row_count = inner.shape[0]
    waves, each, _ = arrived.shape
    slots = waves * each // row_count
    parts = slots // LANES
    half = lon_count.shape[0]
    levels = grid_out.shape[1]
    wave, field = wave_id[0], field_id[0]
    mine = lax.broadcasted_iota(jnp.int32, (1, LANES), 1) < 64
    for source in range(waves):
        held[source * each : (source + 1) * each, :] = jnp.where(
            mine, arrived[source].astype(jnp.float32), swapped[source].astype(jnp.float32)
        )
    for member in range(row_count):
        lat = lat_of_row[(wave * fields + field) * row_count + member]
        hemi = jnp.where(lat >= half, 2 * half - 1 - lat, lat)
        points = lon_count[hemi]
        lines = held[pl.ds(member, slots, stride=row_count), :].astype(jnp.bfloat16)
        coef = dot(place[...], lines, NT)
        for step in range(BLOCKS):
            rows = pl.ds(step * levels, levels)
            for part in range(parts):
                real = coef[:levels, part * LANES : (part + 1) * LANES]
                imag = coef[levels:, part * LANES : (part + 1) * LANES]
                at = part * 2 * LANES
                cosine = outer_fwd[member, step : step + 1, at : at + LANES]
                sine = outer_fwd[member, step : step + 1, at + LANES : at + 2 * LANES]
                turned[rows, at : at + LANES] = (real * cosine - imag * sine).astype(jnp.bfloat16)
                turned[rows, at + LANES : at + 2 * LANES] = (real * sine + imag * cosine).astype(jnp.bfloat16)
        values = dot(turned[...], inner_t[member], NN)
        for step in range(BLOCKS):
            width = min(BLOCK, LONPAD - step * BLOCK)
            line = values[step * levels : (step + 1) * levels]
            x = step * BLOCK + lax.broadcasted_iota(jnp.int32, (1, BLOCK), 1)
            line = jnp.where(x < points, line, 0.0).astype(jnp.bfloat16)
            grid_out[member, :, step * BLOCK : step * BLOCK + width] = line[:, :width]
            line = line.astype(jnp.float32)
            partner = pltpu.roll(line, levels - 1, 0)
            products[step * levels : (step + 1) * levels, :] = (line * partner).astype(jnp.bfloat16)
        reals, imags = [], []
        for part in range(parts):
            at = part * 2 * LANES
            sums = dot(products[...], inner[member, :, at : at + 2 * LANES], NN)
            real = jnp.zeros((levels, LANES), jnp.float32)
            imag = jnp.zeros((levels, LANES), jnp.float32)
            for step in range(BLOCKS):
                rows = slice(step * levels, (step + 1) * levels)
                cosine = outer_inv[member, step : step + 1, at : at + LANES]
                sine = outer_inv[member, step : step + 1, at + LANES : at + 2 * LANES]
                real += sums[rows, :LANES] * cosine + sums[rows, LANES:] * sine
                imag += sums[rows, LANES:] * cosine - sums[rows, :LANES] * sine
            reals.append(real)
            imags.append(imag)
        analysed = jnp.concatenate([jnp.concatenate(reals, axis=1), jnp.concatenate(imags, axis=1)], axis=0)
        back[pl.ds(member, slots, stride=row_count), :] = dot(
            analysed.T.astype(jnp.bfloat16), place[...], NN
        )
    for source in range(waves):
        sent[source] = back[source * each : (source + 1) * each, :].astype(jnp.bfloat16)


def shards(spectra, legendre, lat_weight, wave_of_slot, lat_of_row, lon_count):
    waves = lax.axis_size("wave")
    fields = lax.axis_size("field")
    zs = fields // 2
    wave_id = lax.axis_index("wave").astype(jnp.int32).reshape(1)
    field_id = lax.axis_index("field").astype(jnp.int32).reshape(1)
    slots, _, degrees, cols = spectra.shape
    band = legendre.shape[2]
    rows = 2 * band
    row_count = rows // waves
    all_slots = wave_of_slot.shape[0]
    levels = cols * fields
    each = row_count * slots
    coded = slots * 2 * cols

    def hop(x, by, cross=0):
        pairs = [
            (i, (2 * (i // 2 + side_of(i % 2) * by) + (i % 2 ^ cross)) % fields) for i in range(fields)
        ]
        return lax.ppermute(x, "field", pairs)

    def swap(x):
        return hop(x, 0, 1)

    own = jnp.transpose(spectra, (0, 1, 3, 2)).reshape(coded, degrees)
    two, two_x = hop(own, 2), hop(own, -2, 1)
    one, one_x = hop(own, 1), hop(own, -1, 1)
    legendre = jnp.transpose(legendre, (0, 2, 1))
    legendre_swapped = swap(legendre)

    def order_rows(values, band_of):
        return pl.pallas_call(
            functools.partial(legendre_rows_kernel, waves=waves, fields=fields),
            out_shape=jax.ShapeDtypeStruct((slots, rows, degrees), jnp.bfloat16),
            in_specs=[smem(), smem(), smem(), smem(), vmem()],
            out_specs=vmem(),
            scratch_shapes=[pltpu.VMEM((rows, LANES), jnp.float32)] * 2,
            compiler_params=params(8),
            cost_estimate=cost(3),
            name="legendre_rows",
        )(wave_id, band_of, wave_of_slot, lat_of_row, values)

    two, table = lax.optimization_barrier((two, order_rows(legendre, field_id)))
    two_x, legendre_swapped = lax.optimization_barrier((two_x, legendre_swapped))
    three, three_x = hop(two, 1), hop(two_x, 1)
    four = hop(two, 2)
    table_swapped = order_rows(legendre_swapped, field_id ^ 1)

    outgoing = pl.pallas_call(
        legendre_forward_kernel,
        out_shape=jax.ShapeDtypeStruct((waves, each, LANES), jnp.bfloat16),
        in_specs=[vmem()] * 10,
        out_specs=vmem(),
        scratch_shapes=[pltpu.VMEM((waves * each, LANES), jnp.float32)],
        compiler_params=params(16),
        cost_estimate=cost(4),
        name="legendre_forward",
    )(own, one, one_x, two, two_x, three, three_x, four, table, table_swapped)
    outgoing, lat_weight = lax.optimization_barrier((outgoing, lat_weight))
    arrived = lax.all_to_all(outgoing, "wave", split_axis=0, concat_axis=0, tiled=True)

    steps = 16
    inner, inner_t, outer_fwd, outer_inv, place = pl.pallas_call(
        functools.partial(fourier_tables_kernel, fields=fields, zs=zs),
        out_shape=(
            jax.ShapeDtypeStruct((row_count, BLOCK, 2 * all_slots), jnp.bfloat16),
            jax.ShapeDtypeStruct((row_count, 2 * all_slots, BLOCK), jnp.bfloat16),
            jax.ShapeDtypeStruct((row_count, steps, 2 * all_slots), jnp.float32),
            jax.ShapeDtypeStruct((row_count, steps, 2 * all_slots), jnp.float32),
            jax.ShapeDtypeStruct((LANES, LANES), jnp.bfloat16),
        ),
        in_specs=[smem()] * 5 + [vmem()],
        out_specs=(vmem(),) * 5,
        compiler_params=params(16),
        cost_estimate=cost(4),
        name="fourier_tables",
    )(
        wave_id, field_id, lat_of_row, lon_count, lat_weight,
        wave_of_slot.astype(jnp.float32).reshape(1, all_slots),
    )

    arrived, place = lax.optimization_barrier((arrived, place))
    grid_field, sent = pl.pallas_call(
        functools.partial(fourier_kernel, fields=fields),
        out_shape=(
            jax.ShapeDtypeStruct((row_count, levels, LONPAD), jnp.bfloat16),
            jax.ShapeDtypeStruct((waves, each, LANES), jnp.bfloat16),
        ),
        in_specs=[smem()] * 4 + [vmem()] * 7,
        out_specs=(vmem(), vmem()),
        scratch_shapes=[
            pltpu.VMEM((waves * each, LANES), jnp.float32),
            pltpu.VMEM((waves * each, LANES), jnp.float32),
            pltpu.VMEM((BLOCKS * levels, 2 * all_slots), jnp.bfloat16),
            pltpu.VMEM((BLOCKS * levels, BLOCK), jnp.bfloat16),
        ],
        compiler_params=params(24),
        cost_estimate=cost(7),
        name="fourier",
    )(wave_id, field_id, lat_of_row, lon_count, arrived, swap(arrived), inner, inner_t, outer_fwd, outer_inv, place)

    returned = lax.all_to_all(sent, "wave", split_axis=0, concat_axis=0, tiled=True)

    half = jax.ShapeDtypeStruct((coded, degrees), jnp.bfloat16)
    total, one, one_other, two, two_other, three, four = pl.pallas_call(
        legendre_inverse_kernel,
        out_shape=(
            jax.ShapeDtypeStruct((coded, degrees), jnp.float32), half, half, half, half,
            jax.ShapeDtypeStruct((2, coded, degrees), jnp.bfloat16), half,
        ),
        in_specs=[vmem()] * 4,
        out_specs=(vmem(),) * 7,
        scratch_shapes=[pltpu.VMEM((waves * each, LANES), jnp.float32)] * 2,
        compiler_params=params(16),
        cost_estimate=cost(3),
        name="legendre_inverse",
    )(returned, swap(returned), table, table_swapped)

    def add(*terms):
        return sum(x.astype(jnp.float32) for x in terms).astype(jnp.bfloat16)

    three, four = hop(three, -1), hop(four, -2)
    landed = [hop(one, -1), hop(one_other, -1, 1)]
    landed += [hop(add(two, three[0], four), -2), hop(add(two_other, three[1]), -2, 1)]
    total = total + sum(x.astype(jnp.float32) for x in landed)
    spectral = jnp.transpose(total.reshape(slots, 2, cols, degrees), (0, 1, 3, 2))
    return grid_field, spectral


def solution(mesh):
    in_specs = (P("wave", None, None, "field"), P("wave", None, "field"), P("field"), P(), P(), P())
    out_specs = (P(("wave", "field"), None, None), P("wave", None, None, "field"))
    return jax.shard_map(shards, mesh=mesh, in_specs=in_specs, out_specs=out_specs, check_vma=False)
```

```python
import functools
import math

import jax
import jax.numpy as jnp
from jax import lax
from jax.experimental import pallas as pl
from jax.experimental.pallas import tpu as pltpu
from jax.sharding import PartitionSpec as P

LONPAD = 3200
LANES = 128
BLOCK = 256
BLOCKS = -(-LONPAD // BLOCK)

NT = (((1,), (1,)), ((), ()))
NN = (((1,), (0,)), ((), ()))
TN = (((0,), (0,)), ((), ()))


def dot(a, b, dims):
    return lax.dot_general(a, b, dims, preferred_element_type=jnp.float32)


def params(mebibytes):
    return pltpu.CompilerParams(vmem_limit_bytes=mebibytes * 1024 * 1024)


def in_hbm(x):
    return pltpu.with_memory_space_constraint(x, pltpu.HBM)


def cost(micros):
    return pl.CostEstimate(flops=0, bytes_accessed=int(micros * 3.7e6), transcendentals=0)


def smem():
    return pl.BlockSpec(memory_space=pltpu.SMEM)


def vmem():
    return pl.BlockSpec(memory_space=pltpu.VMEM)


def hbm():
    return pl.BlockSpec(memory_space=pltpu.HBM)


def side_of(core):
    return 1 - 2 * core


def pair_kernel(own, partner, out, mine, held, sem):
    copy = pltpu.make_async_copy(own, mine, sem)
    copy.start()
    slots, parts, cols, _ = mine.shape
    for at, source in ((1, partner), (0, mine)):
        if at == 0:
            copy.wait()
        for slot in range(slots):
            for part in range(parts):
                row = (slot * parts + part) * cols
                held[row : row + cols, :] = source[slot, part].astype(jnp.float32)
        out[at] = held[...].astype(jnp.bfloat16)


def ordered_rows(chosen, south, live, legendre, out):
    slots, band, degrees = legendre.shape
    odd = (lax.broadcasted_iota(jnp.int32, (1, degrees), 1) & 1).astype(jnp.float32)
    sign = 1.0 - 2.0 * (south[:, :1] * odd)
    for slot in range(slots):
        table = dot(chosen[:, :band], legendre[slot], NN) * sign
        out[slot] = (table * live[slot : slot + 1, :]).astype(jnp.bfloat16)


def own_rows_kernel(
    wave_id, field_id, wave_of_slot, lat_of_row, legendre,
    out, chosen_x, south_x, live,
    slot_waves, row_lats, held, pick, south, sems, *, waves, fields,
):
    copies = [
        pltpu.make_async_copy(source, target, sems.at[i])
        for i, (source, target) in enumerate(((lat_of_row, row_lats), (wave_of_slot, slot_waves), (legendre, held)))
    ]
    for copy in copies:
        copy.start()
    slots, band, degrees = held.shape
    rows = out.shape[1]
    row_count = rows // waves
    half = row_lats.shape[0] // 2
    own, field = wave_id[0], field_id[0]
    lane = lax.broadcasted_iota(jnp.int32, (1, LANES), 1)
    copies[0].wait()
    for at in range(2):
        this = field ^ at
        for row in range(rows):
            member, wave = divmod(row, waves)
            lat = row_lats[(wave * fields + this) * row_count + member]
            is_south = lat >= half
            hemi = jnp.where(is_south, 2 * half - 1 - lat, lat) - this * band
            pick[at, row : row + 1, :] = (lane == hemi).astype(jnp.float32)
            south[at, row : row + 1, :] = jnp.broadcast_to(is_south.astype(jnp.float32), (1, LANES))
    chosen_x[...] = pick[1].astype(jnp.bfloat16)
    south_x[...] = south[1]
    offsets = lax.broadcasted_iota(jnp.int32, (1, degrees), 1)
    copies[1].wait()
    live[...] = jnp.zeros(live.shape, jnp.float32)
    for slot in range(slots):
        live[slot : slot + 1, :] = (offsets < degrees - slot_waves[own * slots + slot]).astype(jnp.float32)
    copies[2].wait()
    ordered_rows(pick[0].astype(jnp.bfloat16), south[0], live, held, out)


def partner_rows_kernel(chosen, south, live, legendre, out, held, sem):
    copy = pltpu.make_async_copy(legendre, held, sem)
    copy.start()
    copy.wait()
    ordered_rows(chosen[...], south[...], live, held, out)


def sin_cos(phase, period):
    inverse = 1.0 / period
    turns = (phase - jnp.floor(phase * inverse + 0.5) * period) * inverse
    quarter = jnp.floor(4.0 * turns + 0.5)
    w = (2.0 * math.pi) * (turns - 0.25 * quarter)
    w2 = w * w
    sine = w * (1.0 + w2 * (-1.0 / 6 + w2 * (1.0 / 120 + w2 * (-1.0 / 5040 + w2 * (1.0 / 362880)))))
    cosine = 1.0 + w2 * (-0.5 + w2 * (1.0 / 24 + w2 * (-1.0 / 720 + w2 * (1.0 / 40320))))
    size = jnp.abs(quarter)
    odd = size == 1.0
    flipped = size >= 2.0
    cos_out = jnp.where(odd, sine, cosine)
    sin_out = jnp.where(odd, cosine, sine)
    cos_out = jnp.where(flipped | (quarter == 1.0), -cos_out, cos_out)
    sin_out = jnp.where(flipped | (quarter == -1.0), -sin_out, sin_out)
    return cos_out, sin_out


def fourier_tables_kernel(
    wave_id, field_id, lat_of_row, lon_count, lat_weight, waves_row,
    inner_out, inner_t_out, outer_fwd_out, outer_inv_out, place_out, limits_out,
    inner, inner_t, outer_fwd, outer_inv, place, limits, sems, *, fields, zs,
):
    row_count = inner.shape[0]
    band = lat_weight.shape[0]
    half = lon_count.shape[0]
    slots = waves_row.shape[1]
    steps = outer_fwd.shape[1]
    wave, field = wave_id[0], field_id[0]
    for member in range(row_count):
        lat = lat_of_row[(wave * fields + field) * row_count + member]
        hemi = jnp.where(lat >= half, 2 * half - 1 - lat, lat)
        points = lon_count[hemi].astype(jnp.float32)
        period = jnp.broadcast_to(points, (1, LANES))
        limits[member] = jnp.broadcast_to(points, limits.shape[1:])
        weight = lat_weight[hemi - field * band] / jnp.sqrt(period)
        for part in range(slots // LANES):
            m = waves_row[:, part * LANES : (part + 1) * LANES]
            at = part * 2 * LANES
            x = lax.broadcasted_iota(jnp.int32, (BLOCK, LANES), 0).astype(jnp.float32)
            cosine, sine = sin_cos(x * m, period)
            both = jnp.concatenate([cosine, -sine], axis=1)
            inner[member, :, at : at + 2 * LANES] = both.astype(jnp.bfloat16)
            inner_t[member, at : at + 2 * LANES, :] = both.T.astype(jnp.bfloat16)
            x = (BLOCK * lax.broadcasted_iota(jnp.int32, (steps, LANES), 0)).astype(jnp.float32)
            cosine, sine = sin_cos(x * m, period)
            both = jnp.concatenate([cosine, sine], axis=1)
            outer_fwd[member, :, at : at + 2 * LANES] = both * (1.0 / math.sqrt(slots))
            outer_inv[member, :, at : at + 2 * LANES] = both * jnp.concatenate([weight, weight], axis=1)
    at = lax.broadcasted_iota(jnp.int32, (LANES, LANES), 1)
    chunk, part, low = (at >> 3) & 7, (at >> 2) & 1, at & 3
    core = (field & 1) ^ (at >> 6)
    back = (chunk + 1) >> 1
    other = ((chunk & 1) ^ 1) & (chunk > 0).astype(jnp.int32)
    z = ((field >> 1) - side_of(core) * back + zs) & (zs - 1)
    target = part * 64 + (2 * z + (core ^ other)) * 4 + low
    place[...] = (lax.broadcasted_iota(jnp.int32, (LANES, LANES), 0) == target).astype(jnp.bfloat16)
    results = (
        (inner, inner_out), (inner_t, inner_t_out), (outer_fwd, outer_fwd_out),
        (outer_inv, outer_inv_out), (place, place_out), (limits, limits_out),
    )
    copies = [pltpu.make_async_copy(source, target, sems.at[i]) for i, (source, target) in enumerate(results)]
    for copy in copies:
        copy.start()
    for copy in copies:
        copy.wait()


def legendre_forward_kernel(pair0, one, two, three, four, table, table_swapped, out, held):
    pieces = [pair0.at[0]] + [piece.at[i] for piece in (one, two, three) for i in range(2)] + [four]
    slots, rows, degrees = table.shape
    waves = out.shape[0]
    row_count = rows // waves
    each = slots * row_count
    for pair in range(slots // 2):
        both = [piece[16 * pair : 16 * pair + 16, :].astype(jnp.float32) for piece in pieces]
        for half in range(2):
            slot = 2 * pair + half
            spec = jnp.concatenate([b[8 * half : 8 * half + 8] for b in both], axis=0).astype(jnp.bfloat16)
            sums = jnp.concatenate([dot(table[slot], spec, NT), dot(table_swapped[slot], spec, NT)], axis=1)
            for member in range(row_count):
                held[pl.ds(slot * row_count + member, waves, stride=each), :] = sums[
                    waves * member : waves * (member + 1)
                ]
    for wave in range(waves):
        out[wave] = held[wave * each : (wave + 1) * each, :].astype(jnp.bfloat16)


def legendre_inverse_kernel(
    arrived, swapped, table, table_swapped, own, one, two, three, four, held, held_swapped
):
    slots, rows, degrees = table.shape
    waves = arrived.shape[0]
    row_count = rows // waves
    each = slots * row_count
    for wave in range(waves):
        held[wave * each : (wave + 1) * each, :] = arrived[wave].astype(jnp.float32)
        held_swapped[wave * each : (wave + 1) * each, :] = pltpu.roll(swapped[wave].astype(jnp.float32), 64, 1)

    def share(ref, slot, legendre):
        weighted = jnp.concatenate(
            [ref[pl.ds(slot * row_count + member, waves, stride=each), :] for member in range(row_count)], axis=0
        )
        return dot(weighted[:, :64].astype(jnp.bfloat16), legendre[slot], TN)

    for pair in range(slots // 2):
        at = pl.ds(16 * pair, 16)
        sums = [
            share(held, slot, table) + share(held_swapped, slot, table_swapped) for slot in (2 * pair, 2 * pair + 1)
        ]
        pieces = [jnp.concatenate([s[8 * chunk : 8 * chunk + 8] for s in sums], axis=0) for chunk in range(8)]
        own[at, :] = pieces[0]
        pieces = [piece.astype(jnp.bfloat16) for piece in pieces]
        for target, first in ((one, 1), (two, 3), (three, 5)):
            for i in range(2):
                target[i, at, :] = pieces[first + i]
        four[at, :] = pieces[7]


def fourier_kernel(
    arrived, swapped, inner_in, inner_t_in, outer_fwd_in, outer_inv_in, place_in, limits_in,
    grid_out, sent,
    inner, inner_t, outer_fwd, outer_inv, place, limits, held, back, turned, products, lines_out, sems, out_sems,
):
    inputs = (
        (place_in, place), (outer_fwd_in, outer_fwd), (limits_in, limits),
        (inner_t_in, inner_t), (inner_in, inner), (outer_inv_in, outer_inv),
    )
    copies = [pltpu.make_async_copy(source, target, sems.at[i]) for i, (source, target) in enumerate(inputs)]
    for copy in copies:
        copy.start()
    row_count = inner.shape[0]
    waves, each, _ = arrived.shape
    slots = waves * each // row_count
    parts = slots // LANES
    levels = grid_out.shape[1]
    mine = lax.broadcasted_iota(jnp.int32, (1, LANES), 1) < 64
    for source in range(waves):
        held[source * each : (source + 1) * each, :] = jnp.where(
            mine, arrived[source].astype(jnp.float32), swapped[source].astype(jnp.float32)
        )
    for copy in copies:
        copy.wait()
    column = lax.broadcasted_iota(jnp.int32, (1, BLOCK), 1).astype(jnp.float32)
    results = []
    for member in range(row_count):
        points = jnp.concatenate([limits[member, :1, :]] * (BLOCK // LANES), axis=1)
        lines = held[pl.ds(member, slots, stride=row_count), :].astype(jnp.bfloat16)
        coef = dot(place[...], lines, NT)
        for step in range(BLOCKS):
            rows = pl.ds(step * levels, levels)
            for part in range(parts):
                real = coef[:levels, part * LANES : (part + 1) * LANES]
                imag = coef[levels:, part * LANES : (part + 1) * LANES]
                at = part * 2 * LANES
                cosine = outer_fwd[member, step : step + 1, at : at + LANES]
                sine = outer_fwd[member, step : step + 1, at + LANES : at + 2 * LANES]
                turned[member, rows, at : at + LANES] = (real * cosine - imag * sine).astype(jnp.bfloat16)
                turned[member, rows, at + LANES : at + 2 * LANES] = (real * sine + imag * cosine).astype(jnp.bfloat16)
        values = dot(turned[member], inner_t[member], NN)
        for step in range(BLOCKS):
            width = min(BLOCK, LONPAD - step * BLOCK)
            line = values[step * levels : (step + 1) * levels]
            line = jnp.where(column + step * BLOCK < points, line, 0.0).astype(jnp.bfloat16)
            lines_out[member, :, step * BLOCK : step * BLOCK + width] = line[:, :width]
            line = line.astype(jnp.float32)
            partner = pltpu.roll(line, levels - 1, 0)
            products[member, step * levels : (step + 1) * levels, :] = (line * partner).astype(jnp.bfloat16)
        result = pltpu.make_async_copy(lines_out.at[member], grid_out.at[member], out_sems.at[member])
        result.start()
        results.append(result)
        reals, imags = [], []
        for part in range(parts):
            at = part * 2 * LANES
            sums = dot(products[member], inner[member, :, at : at + 2 * LANES], NN)
            real = jnp.zeros((levels, LANES), jnp.float32)
            imag = jnp.zeros((levels, LANES), jnp.float32)
            for step in range(BLOCKS):
                rows = slice(step * levels, (step + 1) * levels)
                cosine = outer_inv[member, step : step + 1, at : at + LANES]
                sine = outer_inv[member, step : step + 1, at + LANES : at + 2 * LANES]
                real += sums[rows, :LANES] * cosine + sums[rows, LANES:] * sine
                imag += sums[rows, LANES:] * cosine - sums[rows, :LANES] * sine
            reals.append(real)
            imags.append(imag)
        analysed = jnp.concatenate([jnp.concatenate(reals, axis=1), jnp.concatenate(imags, axis=1)], axis=0)
        back[pl.ds(member, slots, stride=row_count), :] = dot(
            analysed.T.astype(jnp.bfloat16), place[...], NN
        )
    for source in range(waves):
        sent[source] = back[source * each : (source + 1) * each, :].astype(jnp.bfloat16)
    for result in results:
        result.wait()


def add_three_kernel(two, three, four, out):
    out[0] = (
        two[0].astype(jnp.float32) + three[0].astype(jnp.float32) + four[...].astype(jnp.float32)
    ).astype(jnp.bfloat16)
    out[1] = (two[1].astype(jnp.float32) + three[1].astype(jnp.float32)).astype(jnp.bfloat16)


def add_two_kernel(one, two, out, out_other):
    for i, target in enumerate((out, out_other)):
        target[...] = (one[i].astype(jnp.float32) + two[i].astype(jnp.float32)).astype(jnp.bfloat16)


def add_own_kernel(own, one, one_other, out):
    total = own[...] + one[...].astype(jnp.float32) + one_other[...].astype(jnp.float32)
    groups, cols, _ = out.shape
    for group in range(groups):
        out[group] = total[group * cols : (group + 1) * cols]


def shards(spectra, legendre, lat_weight, wave_of_slot, lat_of_row, lon_count):
    waves = lax.axis_size("wave")
    fields = lax.axis_size("field")
    zs = fields // 2
    wave_id = lax.axis_index("wave").astype(jnp.int32).reshape(1)
    field_id = lax.axis_index("field").astype(jnp.int32).reshape(1)
    slots, _, degrees, cols = spectra.shape
    band = legendre.shape[2]
    rows = 2 * band
    row_count = rows // waves
    all_slots = wave_of_slot.shape[0]
    levels = cols * fields
    each = row_count * slots
    coded = slots * 2 * cols

    def hop(x, by, cross=0):
        pairs = [
            (i, (2 * (i // 2 + side_of(i % 2) * by) + (i % 2 ^ cross)) % fields) for i in range(fields)
        ]
        return lax.ppermute(x, "field", pairs)

    def swap(x):
        return hop(x, 0, 1)

    def local(kernel, out_shape, name, micros, mebibytes=8, in_specs=None, out_specs=None, scratch=()):
        if in_specs is None:
            in_specs = pl.BlockSpec(memory_space=pltpu.VMEM)
        return pl.pallas_call(
            kernel,
            out_shape=out_shape,
            in_specs=in_specs,
            out_specs=jax.tree.map(lambda _: vmem(), out_shape) if out_specs is None else out_specs,
            scratch_shapes=list(scratch),
            compiler_params=params(mebibytes),
            cost_estimate=cost(micros),
            name=name,
        )

    chunk = jax.ShapeDtypeStruct((coded, degrees), jnp.bfloat16)
    chunk_pair = jax.ShapeDtypeStruct((2, coded, degrees), jnp.bfloat16)
    row_table = jax.ShapeDtypeStruct((slots, rows, degrees), jnp.bfloat16)
    fourier_shape = jax.ShapeDtypeStruct((waves, each, LANES), jnp.bfloat16)
    float_rows = pltpu.VMEM((waves * each, LANES), jnp.float32)

    spectra = jnp.transpose(spectra, (0, 1, 3, 2))
    legendre = jnp.transpose(legendre, (0, 2, 1))
    pair = local(
        pair_kernel,
        chunk_pair,
        "pair",
        1,
        in_specs=[hbm(), vmem()],
        scratch=[
            pltpu.VMEM(spectra.shape, jnp.bfloat16),
            pltpu.VMEM((coded, degrees), jnp.float32),
            pltpu.SemaphoreType.DMA(()),
        ],
    )(in_hbm(spectra), swap(spectra))
    pair, legendre = lax.optimization_barrier((pair, legendre))
    legendre_x = swap(legendre)
    one = hop(pair, 1)
    table, chosen_x, south_x, live = local(
        functools.partial(own_rows_kernel, waves=waves, fields=fields),
        (
            row_table,
            jax.ShapeDtypeStruct((rows, LANES), jnp.bfloat16),
            jax.ShapeDtypeStruct((rows, LANES), jnp.float32),
            jax.ShapeDtypeStruct((-(-slots // 8) * 8, degrees), jnp.float32),
        ),
        "own_rows",
        2,
        in_specs=[smem(), smem(), hbm(), hbm(), hbm()],
        scratch=[
            pltpu.SMEM(wave_of_slot.shape, jnp.int32),
            pltpu.SMEM(lat_of_row.shape, jnp.int32),
            pltpu.VMEM((slots, band, degrees), jnp.bfloat16),
            pltpu.VMEM((2, rows, LANES), jnp.float32),
            pltpu.VMEM((2, rows, LANES), jnp.float32),
            pltpu.SemaphoreType.DMA((3,)),
        ],
    )(wave_id, field_id, in_hbm(wave_of_slot), in_hbm(lat_of_row), in_hbm(legendre))
    one, legendre_x, table = lax.optimization_barrier((one, legendre_x, table))
    two = hop(one, 1)
    table_x = local(
        partner_rows_kernel,
        row_table,
        "partner_rows",
        2,
        in_specs=[vmem(), vmem(), vmem(), hbm()],
        scratch=[pltpu.VMEM((slots, band, degrees), jnp.bfloat16), pltpu.SemaphoreType.DMA(())],
    )(chosen_x, south_x, live, in_hbm(legendre_x))
    two, table_x = lax.optimization_barrier((two, table_x))
    three = hop(two, 1)
    four = hop(three[0], 1)

    outgoing = local(
        legendre_forward_kernel, fourier_shape, "legendre_forward", 4, 16, in_specs=[vmem()] * 7, scratch=[float_rows]
    )(pair, one, two, three, four, table, table_x)
    outgoing, lat_weight = lax.optimization_barrier((outgoing, lat_weight))
    arrived = lax.all_to_all(outgoing, "wave", split_axis=0, concat_axis=0, tiled=True)

    tables = (
        ((row_count, BLOCK, 2 * all_slots), jnp.bfloat16),
        ((row_count, 2 * all_slots, BLOCK), jnp.bfloat16),
        ((row_count, 16, 2 * all_slots), jnp.float32),
        ((row_count, 16, 2 * all_slots), jnp.float32),
        ((LANES, LANES), jnp.bfloat16),
        ((row_count, 8, LANES), jnp.float32),
    )
    tables_vmem = [pltpu.VMEM(shape, kind) for shape, kind in tables]
    prepared = local(
        functools.partial(fourier_tables_kernel, fields=fields, zs=zs),
        [pltpu.HBM(shape, kind) for shape, kind in tables],
        "fourier_tables",
        4,
        16,
        in_specs=[smem()] * 5 + [vmem()],
        out_specs=[hbm()] * 6,
        scratch=tables_vmem + [pltpu.SemaphoreType.DMA((6,))],
    )(
        wave_id, field_id, lat_of_row, lon_count, lat_weight,
        wave_of_slot.astype(jnp.float32).reshape(1, all_slots),
    )
    arrived, prepared = lax.optimization_barrier((arrived, prepared))
    prepared = [in_hbm(x) for x in prepared]

    grid_field, sent = local(
        fourier_kernel,
        (jax.ShapeDtypeStruct((row_count, levels, LONPAD), jnp.bfloat16), fourier_shape),
        "fourier",
        6,
        32,
        in_specs=[vmem()] * 2 + [hbm()] * 6,
        out_specs=(hbm(), vmem()),
        scratch=tables_vmem + [
            float_rows,
            float_rows,
            pltpu.VMEM((row_count, BLOCKS * levels, 2 * all_slots), jnp.bfloat16),
            pltpu.VMEM((row_count, BLOCKS * levels, BLOCK), jnp.bfloat16),
            pltpu.VMEM((row_count, levels, LONPAD), jnp.bfloat16),
            pltpu.SemaphoreType.DMA((6,)),
            pltpu.SemaphoreType.DMA((row_count,)),
        ],
    )(arrived, swap(arrived), *prepared)

    returned = lax.all_to_all(sent, "wave", split_axis=0, concat_axis=0, tiled=True)

    own, one, two, three, four = local(
        legendre_inverse_kernel,
        (jax.ShapeDtypeStruct((coded, degrees), jnp.float32), chunk_pair, chunk_pair, chunk_pair, chunk),
        "legendre_inverse",
        2,
        16,
        in_specs=[vmem()] * 4,
        scratch=[float_rows, float_rows],
    )(returned, swap(returned), table, table_x)
    three, four = hop(three, -1), hop(four, -2)
    two = local(add_three_kernel, chunk_pair, "add_three", 1, in_specs=[vmem()] * 3)(two, three, four)
    one, one_other = local(add_two_kernel, (chunk, chunk), "add_two", 1, in_specs=[vmem()] * 2)(one, hop(two, -1))
    total = local(
        add_own_kernel,
        jax.ShapeDtypeStruct((2 * slots, cols, degrees), jnp.float32),
        "add_own",
        1,
        in_specs=[vmem()] * 3,
    )(own, hop(one, -1), hop(one_other, -1, 1))
    spectral = jnp.transpose(total.reshape(slots, 2, cols, degrees), (0, 1, 3, 2))
    return grid_field, spectral


def solution(mesh):
    in_specs = (P("wave", None, None, "field"), P("wave", None, "field"), P("field"), P(), P(), P())
    out_specs = (P(("wave", "field"), None, None), P("wave", None, None, "field"))
    return jax.shard_map(shards, mesh=mesh, in_specs=in_specs, out_specs=out_specs, check_vma=False)
```

```python
import functools
import math

import jax
import jax.numpy as jnp
from jax import lax
from jax.experimental import pallas as pl
from jax.experimental.pallas import tpu as pltpu
from jax.sharding import PartitionSpec as P

LONPAD = 3200
LANES = 128
BLOCK = 256
BLOCKS = -(-LONPAD // BLOCK)

NT = (((1,), (1,)), ((), ()))
NN = (((1,), (0,)), ((), ()))
TN = (((0,), (0,)), ((), ()))


def dot(a, b, dims):
    return lax.dot_general(a, b, dims, preferred_element_type=jnp.float32)


def params(mebibytes):
    return pltpu.CompilerParams(vmem_limit_bytes=mebibytes * 1024 * 1024)


def in_hbm(x):
    return pltpu.with_memory_space_constraint(x, pltpu.HBM)


def cost(micros):
    return pl.CostEstimate(flops=0, bytes_accessed=int(micros * 3.7e6), transcendentals=0)


def smem():
    return pl.BlockSpec(memory_space=pltpu.SMEM)


def vmem():
    return pl.BlockSpec(memory_space=pltpu.VMEM)


def hbm():
    return pl.BlockSpec(memory_space=pltpu.HBM)


def ordered_rows(chosen, south, live, legendre, out):
    slots, band, degrees = legendre.shape
    odd = (lax.broadcasted_iota(jnp.int32, (1, degrees), 1) & 1).astype(jnp.float32)
    sign = 1.0 - 2.0 * (south[:, :1] * odd)
    for slot in range(slots):
        table = dot(chosen[:, :band], legendre[slot], NN) * sign
        out[slot] = (table * live[slot : slot + 1, :]).astype(jnp.bfloat16)


def own_rows_kernel(
    wave_id, field_id, wave_of_slot, lat_of_row, legendre,
    out, chosen_x, south_x, live,
    slot_waves, row_lats, held, pick, south, sems, *, waves, fields,
):
    copies = [
        pltpu.make_async_copy(source, target, sems.at[i])
        for i, (source, target) in enumerate(((lat_of_row, row_lats), (wave_of_slot, slot_waves), (legendre, held)))
    ]
    for copy in copies:
        copy.start()
    slots, band, degrees = held.shape
    rows = out.shape[1]
    row_count = rows // waves
    half = row_lats.shape[0] // 2
    own, field = wave_id[0], field_id[0]
    lane = lax.broadcasted_iota(jnp.int32, (1, LANES), 1)
    copies[0].wait()
    for at in range(2):
        this = field ^ at
        for row in range(rows):
            member, wave = divmod(row, waves)
            lat = row_lats[(wave * fields + this) * row_count + member]
            is_south = lat >= half
            hemi = jnp.where(is_south, 2 * half - 1 - lat, lat) - this * band
            pick[at, row : row + 1, :] = (lane == hemi).astype(jnp.float32)
            south[at, row : row + 1, :] = jnp.broadcast_to(is_south.astype(jnp.float32), (1, LANES))
    chosen_x[...] = pick[1].astype(jnp.bfloat16)
    south_x[...] = south[1]
    offsets = lax.broadcasted_iota(jnp.int32, (1, degrees), 1)
    copies[1].wait()
    live[...] = jnp.zeros(live.shape, jnp.float32)
    for slot in range(slots):
        live[slot : slot + 1, :] = (offsets < degrees - slot_waves[own * slots + slot]).astype(jnp.float32)
    copies[2].wait()
    ordered_rows(pick[0].astype(jnp.bfloat16), south[0], live, held, out)


def partner_rows_kernel(chosen, south, live, legendre, out, held, sem):
    copy = pltpu.make_async_copy(legendre, held, sem)
    copy.start()
    copy.wait()
    ordered_rows(chosen[...], south[...], live, held, out)


def sin_cos(phase, period):
    inverse = 1.0 / period
    turns = (phase - jnp.floor(phase * inverse + 0.5) * period) * inverse
    quarter = jnp.floor(4.0 * turns + 0.5)
    w = (2.0 * math.pi) * (turns - 0.25 * quarter)
    w2 = w * w
    sine = w * (1.0 + w2 * (-1.0 / 6 + w2 * (1.0 / 120 + w2 * (-1.0 / 5040 + w2 * (1.0 / 362880)))))
    cosine = 1.0 + w2 * (-0.5 + w2 * (1.0 / 24 + w2 * (-1.0 / 720 + w2 * (1.0 / 40320))))
    size = jnp.abs(quarter)
    odd = size == 1.0
    flipped = size >= 2.0
    cos_out = jnp.where(odd, sine, cosine)
    sin_out = jnp.where(odd, cosine, sine)
    cos_out = jnp.where(flipped | (quarter == 1.0), -cos_out, cos_out)
    sin_out = jnp.where(flipped | (quarter == -1.0), -sin_out, sin_out)
    return cos_out, sin_out


def fourier_tables_kernel(
    wave_id, field_id, lat_of_row, lon_count, lat_weight, waves_row,
    inner_out, inner_t_out, outer_fwd_out, outer_inv_out, place_out, limits_out,
    inner, inner_t, outer_fwd, outer_inv, place, limits, sems, *, fields,
):
    row_count = inner.shape[0]
    band = lat_weight.shape[0]
    half = lon_count.shape[0]
    slots = waves_row.shape[1]
    steps = outer_fwd.shape[1]
    wave, field = wave_id[0], field_id[0]
    for member in range(row_count):
        lat = lat_of_row[(wave * fields + field) * row_count + member]
        hemi = jnp.where(lat >= half, 2 * half - 1 - lat, lat)
        points = lon_count[hemi].astype(jnp.float32)
        period = jnp.broadcast_to(points, (1, LANES))
        limits[member] = jnp.broadcast_to(points, limits.shape[1:])
        weight = lat_weight[hemi - field * band] / jnp.sqrt(period)
        for part in range(slots // LANES):
            m = waves_row[:, part * LANES : (part + 1) * LANES]
            at = part * 2 * LANES
            x = lax.broadcasted_iota(jnp.int32, (BLOCK, LANES), 0).astype(jnp.float32)
            cosine, sine = sin_cos(x * m, period)
            both = jnp.concatenate([cosine, -sine], axis=1)
            inner[member, :, at : at + 2 * LANES] = both.astype(jnp.bfloat16)
            inner_t[member, at : at + 2 * LANES, :] = both.T.astype(jnp.bfloat16)
            x = (BLOCK * lax.broadcasted_iota(jnp.int32, (steps, LANES), 0)).astype(jnp.float32)
            cosine, sine = sin_cos(x * m, period)
            both = jnp.concatenate([cosine, sine], axis=1)
            outer_fwd[member, :, at : at + 2 * LANES] = both * (1.0 / math.sqrt(slots))
            outer_inv[member, :, at : at + 2 * LANES] = both * jnp.concatenate([weight, weight], axis=1)
    at = lax.broadcasted_iota(jnp.int32, (LANES, LANES), 1)
    core, z, part, low = (field & 1) ^ (at >> 6), (at >> 3) & 7, (at >> 2) & 1, at & 3
    target = part * 64 + (2 * z + core) * 4 + low
    place[...] = (lax.broadcasted_iota(jnp.int32, (LANES, LANES), 0) == target).astype(jnp.bfloat16)
    results = (
        (inner, inner_out), (inner_t, inner_t_out), (outer_fwd, outer_fwd_out),
        (outer_inv, outer_inv_out), (place, place_out), (limits, limits_out),
    )
    copies = [pltpu.make_async_copy(source, target, sems.at[i]) for i, (source, target) in enumerate(results)]
    for copy in copies:
        copy.start()
    for copy in copies:
        copy.wait()


def legendre_forward_kernel(gathered, table, table_swapped, out, held):
    slots, rows, degrees = table.shape
    waves = out.shape[0]
    row_count = rows // waves
    each = slots * row_count
    for pair in range(slots // 2):
        both = [gathered[z, 16 * pair : 16 * pair + 16, :].astype(jnp.float32) for z in range(gathered.shape[0])]
        for half in range(2):
            slot = 2 * pair + half
            spec = jnp.concatenate([b[8 * half : 8 * half + 8] for b in both], axis=0).astype(jnp.bfloat16)
            sums = jnp.concatenate([dot(table[slot], spec, NT), dot(table_swapped[slot], spec, NT)], axis=1)
            for member in range(row_count):
                held[pl.ds(slot * row_count + member, waves, stride=each), :] = sums[
                    waves * member : waves * (member + 1)
                ]
    for wave in range(waves):
        out[wave] = held[wave * each : (wave + 1) * each, :].astype(jnp.bfloat16)


def legendre_inverse_kernel(
    arrived, swapped, table, table_swapped, out, held, held_swapped
):
    slots, rows, degrees = table.shape
    waves = arrived.shape[0]
    row_count = rows // waves
    each = slots * row_count
    for wave in range(waves):
        held[wave * each : (wave + 1) * each, :] = arrived[wave].astype(jnp.float32)
        held_swapped[wave * each : (wave + 1) * each, :] = pltpu.roll(swapped[wave].astype(jnp.float32), 64, 1)

    def share(ref, slot, legendre):
        weighted = jnp.concatenate(
            [ref[pl.ds(slot * row_count + member, waves, stride=each), :] for member in range(row_count)], axis=0
        )
        return dot(weighted[:, :64].astype(jnp.bfloat16), legendre[slot], TN)

    for pair in range(slots // 2):
        at = pl.ds(16 * pair, 16)
        sums = [
            share(held, slot, table) + share(held_swapped, slot, table_swapped) for slot in (2 * pair, 2 * pair + 1)
        ]
        for z in range(out.shape[0]):
            piece = jnp.concatenate([s[8 * z : 8 * z + 8] for s in sums], axis=0)
            out[z, at, :] = piece.astype(jnp.bfloat16)


def fourier_kernel(
    arrived, swapped, inner_in, inner_t_in, outer_fwd_in, outer_inv_in, place_in, limits_in,
    grid_out, sent,
    inner, inner_t, outer_fwd, outer_inv, place, limits, held, back, turned, products, lines_out, sems, out_sems,
):
    inputs = (
        (place_in, place), (outer_fwd_in, outer_fwd), (limits_in, limits),
        (inner_t_in, inner_t), (inner_in, inner), (outer_inv_in, outer_inv),
    )
    copies = [pltpu.make_async_copy(source, target, sems.at[i]) for i, (source, target) in enumerate(inputs)]
    for copy in copies:
        copy.start()
    row_count = inner.shape[0]
    waves, each, _ = arrived.shape
    slots = waves * each // row_count
    parts = slots // LANES
    levels = grid_out.shape[1]
    mine = lax.broadcasted_iota(jnp.int32, (1, LANES), 1) < 64
    for source in range(waves):
        held[source * each : (source + 1) * each, :] = jnp.where(
            mine, arrived[source].astype(jnp.float32), swapped[source].astype(jnp.float32)
        )
    for copy in copies:
        copy.wait()
    column = lax.broadcasted_iota(jnp.int32, (1, BLOCK), 1).astype(jnp.float32)
    results = []
    for member in range(row_count):
        points = jnp.concatenate([limits[member, :1, :]] * (BLOCK // LANES), axis=1)
        lines = held[pl.ds(member, slots, stride=row_count), :].astype(jnp.bfloat16)
        coef = dot(place[...], lines, NT)
        for step in range(BLOCKS):
            rows = pl.ds(step * levels, levels)
            for part in range(parts):
                real = coef[:levels, part * LANES : (part + 1) * LANES]
                imag = coef[levels:, part * LANES : (part + 1) * LANES]
                at = part * 2 * LANES
                cosine = outer_fwd[member, step : step + 1, at : at + LANES]
                sine = outer_fwd[member, step : step + 1, at + LANES : at + 2 * LANES]
                turned[member, rows, at : at + LANES] = (real * cosine - imag * sine).astype(jnp.bfloat16)
                turned[member, rows, at + LANES : at + 2 * LANES] = (real * sine + imag * cosine).astype(jnp.bfloat16)
        values = dot(turned[member], inner_t[member], NN)
        for step in range(BLOCKS):
            width = min(BLOCK, LONPAD - step * BLOCK)
            line = values[step * levels : (step + 1) * levels]
            line = jnp.where(column + step * BLOCK < points, line, 0.0).astype(jnp.bfloat16)
            lines_out[member, :, step * BLOCK : step * BLOCK + width] = line[:, :width]
            line = line.astype(jnp.float32)
            partner = pltpu.roll(line, levels - 1, 0)
            products[member, step * levels : (step + 1) * levels, :] = (line * partner).astype(jnp.bfloat16)
        result = pltpu.make_async_copy(lines_out.at[member], grid_out.at[member], out_sems.at[member])
        result.start()
        results.append(result)
        reals, imags = [], []
        for part in range(parts):
            at = part * 2 * LANES
            sums = dot(products[member], inner[member, :, at : at + 2 * LANES], NN)
            real = jnp.zeros((levels, LANES), jnp.float32)
            imag = jnp.zeros((levels, LANES), jnp.float32)
            for step in range(BLOCKS):
                rows = slice(step * levels, (step + 1) * levels)
                cosine = outer_inv[member, step : step + 1, at : at + LANES]
                sine = outer_inv[member, step : step + 1, at + LANES : at + 2 * LANES]
                real += sums[rows, :LANES] * cosine + sums[rows, LANES:] * sine
                imag += sums[rows, LANES:] * cosine - sums[rows, :LANES] * sine
            reals.append(real)
            imags.append(imag)
        analysed = jnp.concatenate([jnp.concatenate(reals, axis=1), jnp.concatenate(imags, axis=1)], axis=0)
        back[pl.ds(member, slots, stride=row_count), :] = dot(
            analysed.T.astype(jnp.bfloat16), place[...], NN
        )
    for source in range(waves):
        sent[source] = back[source * each : (source + 1) * each, :].astype(jnp.bfloat16)
    for result in results:
        result.wait()


def finish_kernel(summed, out):
    total = summed[...].astype(jnp.float32)
    groups, cols, _ = out.shape
    for group in range(groups):
        out[group] = total[group * cols : (group + 1) * cols]


def shards(spectra, legendre, lat_weight, wave_of_slot, lat_of_row, lon_count):
    waves = lax.axis_size("wave")
    fields = lax.axis_size("field")
    zs = fields // 2
    wave_id = lax.axis_index("wave").astype(jnp.int32).reshape(1)
    field_id = lax.axis_index("field").astype(jnp.int32).reshape(1)
    slots, _, degrees, cols = spectra.shape
    band = legendre.shape[2]
    rows = 2 * band
    row_count = rows // waves
    all_slots = wave_of_slot.shape[0]
    levels = cols * fields
    each = row_count * slots
    coded = slots * 2 * cols

    like_cores = [list(range(core, fields, 2)) for core in range(2)]

    def swap(x):
        return lax.ppermute(x, "field", [(i, i ^ 1) for i in range(fields)])

    def local(kernel, out_shape, name, micros, mebibytes=8, in_specs=None, out_specs=None, scratch=()):
        if in_specs is None:
            in_specs = pl.BlockSpec(memory_space=pltpu.VMEM)
        return pl.pallas_call(
            kernel,
            out_shape=out_shape,
            in_specs=in_specs,
            out_specs=jax.tree.map(lambda _: vmem(), out_shape) if out_specs is None else out_specs,
            scratch_shapes=list(scratch),
            compiler_params=params(mebibytes),
            cost_estimate=cost(micros),
            name=name,
        )

    row_table = jax.ShapeDtypeStruct((slots, rows, degrees), jnp.bfloat16)
    fourier_shape = jax.ShapeDtypeStruct((waves, each, LANES), jnp.bfloat16)
    float_rows = pltpu.VMEM((waves * each, LANES), jnp.float32)

    own = jnp.transpose(spectra, (0, 1, 3, 2)).reshape(coded, degrees)
    own, legendre = lax.optimization_barrier((own, jnp.transpose(legendre, (0, 2, 1))))
    gathered = lax.all_gather(own, "field", axis_index_groups=like_cores)
    legendre_x = swap(legendre)
    table, chosen_x, south_x, live = local(
        functools.partial(own_rows_kernel, waves=waves, fields=fields),
        (
            row_table,
            jax.ShapeDtypeStruct((rows, LANES), jnp.bfloat16),
            jax.ShapeDtypeStruct((rows, LANES), jnp.float32),
            jax.ShapeDtypeStruct((-(-slots // 8) * 8, degrees), jnp.float32),
        ),
        "own_rows",
        2,
        in_specs=[smem(), smem(), hbm(), hbm(), hbm()],
        scratch=[
            pltpu.SMEM(wave_of_slot.shape, jnp.int32),
            pltpu.SMEM(lat_of_row.shape, jnp.int32),
            pltpu.VMEM((slots, band, degrees), jnp.bfloat16),
            pltpu.VMEM((2, rows, LANES), jnp.float32),
            pltpu.VMEM((2, rows, LANES), jnp.float32),
            pltpu.SemaphoreType.DMA((3,)),
        ],
    )(wave_id, field_id, in_hbm(wave_of_slot), in_hbm(lat_of_row), in_hbm(legendre))
    table_x = local(
        partner_rows_kernel,
        row_table,
        "partner_rows",
        2,
        in_specs=[vmem(), vmem(), vmem(), hbm()],
        scratch=[pltpu.VMEM((slots, band, degrees), jnp.bfloat16), pltpu.SemaphoreType.DMA(())],
    )(chosen_x, south_x, live, in_hbm(legendre_x))
    outgoing = local(
        legendre_forward_kernel, fourier_shape, "legendre_forward", 4, 16, in_specs=[vmem()] * 3, scratch=[float_rows]
    )(gathered, table, table_x)
    outgoing, lat_weight = lax.optimization_barrier((outgoing, lat_weight))
    arrived = lax.all_to_all(outgoing, "wave", split_axis=0, concat_axis=0, tiled=True)

    tables = (
        ((row_count, BLOCK, 2 * all_slots), jnp.bfloat16),
        ((row_count, 2 * all_slots, BLOCK), jnp.bfloat16),
        ((row_count, 16, 2 * all_slots), jnp.float32),
        ((row_count, 16, 2 * all_slots), jnp.float32),
        ((LANES, LANES), jnp.bfloat16),
        ((row_count, 8, LANES), jnp.float32),
    )
    tables_vmem = [pltpu.VMEM(shape, kind) for shape, kind in tables]
    prepared = local(
        functools.partial(fourier_tables_kernel, fields=fields),
        [pltpu.HBM(shape, kind) for shape, kind in tables],
        "fourier_tables",
        4,
        16,
        in_specs=[smem()] * 5 + [vmem()],
        out_specs=[hbm()] * 6,
        scratch=tables_vmem + [pltpu.SemaphoreType.DMA((6,))],
    )(
        wave_id, field_id, lat_of_row, lon_count, lat_weight,
        wave_of_slot.astype(jnp.float32).reshape(1, all_slots),
    )
    arrived, prepared = lax.optimization_barrier((arrived, prepared))
    prepared = [in_hbm(x) for x in prepared]

    grid_field, sent = local(
        fourier_kernel,
        (jax.ShapeDtypeStruct((row_count, levels, LONPAD), jnp.bfloat16), fourier_shape),
        "fourier",
        6,
        32,
        in_specs=[vmem()] * 2 + [hbm()] * 6,
        out_specs=(hbm(), vmem()),
        scratch=tables_vmem + [
            float_rows,
            float_rows,
            pltpu.VMEM((row_count, BLOCKS * levels, 2 * all_slots), jnp.bfloat16),
            pltpu.VMEM((row_count, BLOCKS * levels, BLOCK), jnp.bfloat16),
            pltpu.VMEM((row_count, levels, LONPAD), jnp.bfloat16),
            pltpu.SemaphoreType.DMA((6,)),
            pltpu.SemaphoreType.DMA((row_count,)),
        ],
    )(arrived, swap(arrived), *prepared)

    returned = lax.all_to_all(sent, "wave", split_axis=0, concat_axis=0, tiled=True)

    partial = local(
        legendre_inverse_kernel,
        jax.ShapeDtypeStruct((zs, coded, degrees), jnp.bfloat16),
        "legendre_inverse",
        2,
        16,
        in_specs=[vmem()] * 4,
        scratch=[float_rows, float_rows],
    )(returned, swap(returned), table, table_x)
    summed = lax.psum_scatter(
        partial.reshape(zs * coded, degrees),
        "field",
        scatter_dimension=0,
        axis_index_groups=like_cores,
        tiled=True,
    )
    total = local(
        finish_kernel,
        jax.ShapeDtypeStruct((2 * slots, cols, degrees), jnp.float32),
        "finish",
        1,
        in_specs=[vmem()],
    )(summed)
    spectral = jnp.transpose(total.reshape(slots, 2, cols, degrees), (0, 1, 3, 2))
    return grid_field, spectral


def solution(mesh):
    in_specs = (P("wave", None, None, "field"), P("wave", None, "field"), P("field"), P(), P(), P())
    out_specs = (P(("wave", "field"), None, None), P("wave", None, None, "field"))
    return jax.shard_map(shards, mesh=mesh, in_specs=in_specs, out_specs=out_specs, check_vma=False)
```

```python
import functools
import math

import jax
import jax.numpy as jnp
from jax import lax
from jax.experimental import pallas as pl
from jax.experimental.pallas import tpu as pltpu
from jax.sharding import PartitionSpec as P

LONPAD = 3200
LANES = 128
BLOCK = 256
BLOCKS = -(-LONPAD // BLOCK)

NT = (((1,), (1,)), ((), ()))
NN = (((1,), (0,)), ((), ()))
TN = (((0,), (0,)), ((), ()))


def dot(a, b, dims):
    return lax.dot_general(a, b, dims, preferred_element_type=jnp.float32)


def params(mebibytes):
    return pltpu.CompilerParams(vmem_limit_bytes=mebibytes * 1024 * 1024)


def in_hbm(x):
    return pltpu.with_memory_space_constraint(x, pltpu.HBM)


def cost(micros):
    return pl.CostEstimate(flops=0, bytes_accessed=int(micros * 3.7e6), transcendentals=0)


def smem():
    return pl.BlockSpec(memory_space=pltpu.SMEM)


def vmem():
    return pl.BlockSpec(memory_space=pltpu.VMEM)


def hbm():
    return pl.BlockSpec(memory_space=pltpu.HBM)


def side_of(core):
    return 1 - 2 * core


def ordered_rows(chosen, south, live, legendre, out):
    slots, band, degrees = legendre.shape
    odd = (lax.broadcasted_iota(jnp.int32, (1, degrees), 1) & 1).astype(jnp.float32)
    sign = 1.0 - 2.0 * (south[:, :1] * odd)
    for slot in range(slots):
        table = dot(chosen[:, :band], legendre[slot], NN) * sign
        out[slot] = (table * live[slot : slot + 1, :]).astype(jnp.bfloat16)


def own_rows_kernel(
    wave_id, field_id, wave_of_slot, lat_of_row, legendre,
    out, chosen_x, south_x, live,
    slot_waves, row_lats, held, pick, south, sems, *, waves, fields,
):
    copies = [
        pltpu.make_async_copy(source, target, sems.at[i])
        for i, (source, target) in enumerate(((lat_of_row, row_lats), (wave_of_slot, slot_waves), (legendre, held)))
    ]
    for copy in copies:
        copy.start()
    slots, band, degrees = held.shape
    rows = out.shape[1]
    row_count = rows // waves
    half = row_lats.shape[0] // 2
    own, field = wave_id[0], field_id[0]
    lane = lax.broadcasted_iota(jnp.int32, (1, LANES), 1)
    copies[0].wait()
    for at in range(2):
        this = field ^ at
        for row in range(rows):
            member, wave = divmod(row, waves)
            lat = row_lats[(wave * fields + this) * row_count + member]
            is_south = lat >= half
            hemi = jnp.where(is_south, 2 * half - 1 - lat, lat) - this * band
            pick[at, row : row + 1, :] = (lane == hemi).astype(jnp.float32)
            south[at, row : row + 1, :] = jnp.broadcast_to(is_south.astype(jnp.float32), (1, LANES))
    chosen_x[...] = pick[1].astype(jnp.bfloat16)
    south_x[...] = south[1]
    offsets = lax.broadcasted_iota(jnp.int32, (1, degrees), 1)
    copies[1].wait()
    live[...] = jnp.zeros(live.shape, jnp.float32)
    for slot in range(slots):
        live[slot : slot + 1, :] = (offsets < degrees - slot_waves[own * slots + slot]).astype(jnp.float32)
    copies[2].wait()
    ordered_rows(pick[0].astype(jnp.bfloat16), south[0], live, held, out)


def partner_rows_kernel(chosen, south, live, legendre, out, held, sem):
    copy = pltpu.make_async_copy(legendre, held, sem)
    copy.start()
    copy.wait()
    ordered_rows(chosen[...], south[...], live, held, out)


def sin_cos(phase, period):
    inverse = 1.0 / period
    turns = (phase - jnp.floor(phase * inverse + 0.5) * period) * inverse
    quarter = jnp.floor(4.0 * turns + 0.5)
    w = (2.0 * math.pi) * (turns - 0.25 * quarter)
    w2 = w * w
    sine = w * (1.0 + w2 * (-1.0 / 6 + w2 * (1.0 / 120 + w2 * (-1.0 / 5040 + w2 * (1.0 / 362880)))))
    cosine = 1.0 + w2 * (-0.5 + w2 * (1.0 / 24 + w2 * (-1.0 / 720 + w2 * (1.0 / 40320))))
    size = jnp.abs(quarter)
    odd = size == 1.0
    flipped = size >= 2.0
    cos_out = jnp.where(odd, sine, cosine)
    sin_out = jnp.where(odd, cosine, sine)
    cos_out = jnp.where(flipped | (quarter == 1.0), -cos_out, cos_out)
    sin_out = jnp.where(flipped | (quarter == -1.0), -sin_out, sin_out)
    return cos_out, sin_out


def fourier_tables_kernel(
    wave_id, field_id, lat_of_row, lon_count, lat_weight, waves_row,
    inner_out, inner_t_out, outer_fwd_out, outer_inv_out, place_out, limits_out,
    inner, inner_t, outer_fwd, outer_inv, place, limits, sems, *, fields, zs,
):
    row_count = inner.shape[0]
    band = lat_weight.shape[0]
    half = lon_count.shape[0]
    slots = waves_row.shape[1]
    steps = outer_fwd.shape[1]
    wave, field = wave_id[0], field_id[0]
    for member in range(row_count):
        lat = lat_of_row[(wave * fields + field) * row_count + member]
        hemi = jnp.where(lat >= half, 2 * half - 1 - lat, lat)
        points = lon_count[hemi].astype(jnp.float32)
        period = jnp.broadcast_to(points, (1, LANES))
        limits[member] = jnp.broadcast_to(points, limits.shape[1:])
        weight = lat_weight[hemi - field * band] / jnp.sqrt(period)
        for part in range(slots // LANES):
            m = waves_row[:, part * LANES : (part + 1) * LANES]
            at = part * 2 * LANES
            x = lax.broadcasted_iota(jnp.int32, (BLOCK, LANES), 0).astype(jnp.float32)
            cosine, sine = sin_cos(x * m, period)
            both = jnp.concatenate([cosine, -sine], axis=1)
            inner[member, :, at : at + 2 * LANES] = both.astype(jnp.bfloat16)
            inner_t[member, at : at + 2 * LANES, :] = both.T.astype(jnp.bfloat16)
            x = (BLOCK * lax.broadcasted_iota(jnp.int32, (steps, LANES), 0)).astype(jnp.float32)
            cosine, sine = sin_cos(x * m, period)
            both = jnp.concatenate([cosine, sine], axis=1)
            outer_fwd[member, :, at : at + 2 * LANES] = both * (1.0 / math.sqrt(slots))
            outer_inv[member, :, at : at + 2 * LANES] = both * jnp.concatenate([weight, weight], axis=1)
    at = lax.broadcasted_iota(jnp.int32, (LANES, LANES), 1)
    core, chunk, part, low = (field & 1) ^ (at >> 6), (at >> 3) & 7, (at >> 2) & 1, at & 3
    away = (chunk + 1) >> 1
    cross = ((chunk & 1) ^ 1) & (chunk > 0).astype(jnp.int32)
    z = ((field >> 1) - side_of(core) * away + zs) & (zs - 1)
    row = lax.broadcasted_iota(jnp.int32, (LANES, LANES), 0)
    for way, shard in enumerate((2 * chunk + core, 2 * z + (core ^ cross))):
        place[way] = (row == part * 64 + shard * 4 + low).astype(jnp.bfloat16)
    results = (
        (inner, inner_out), (inner_t, inner_t_out), (outer_fwd, outer_fwd_out),
        (outer_inv, outer_inv_out), (place, place_out), (limits, limits_out),
    )
    copies = [pltpu.make_async_copy(source, target, sems.at[i]) for i, (source, target) in enumerate(results)]
    for copy in copies:
        copy.start()
    for copy in copies:
        copy.wait()


def legendre_forward_kernel(gathered, table, table_swapped, out, held):
    slots, rows, degrees = table.shape
    waves = out.shape[0]
    row_count = rows // waves
    each = slots * row_count
    for pair in range(slots // 2):
        both = [gathered[z, 16 * pair : 16 * pair + 16, :].astype(jnp.float32) for z in range(gathered.shape[0])]
        for half in range(2):
            slot = 2 * pair + half
            spec = jnp.concatenate([b[8 * half : 8 * half + 8] for b in both], axis=0).astype(jnp.bfloat16)
            sums = jnp.concatenate([dot(table[slot], spec, NT), dot(table_swapped[slot], spec, NT)], axis=1)
            for member in range(row_count):
                held[pl.ds(slot * row_count + member, waves, stride=each), :] = sums[
                    waves * member : waves * (member + 1)
                ]
    for wave in range(waves):
        out[wave] = held[wave * each : (wave + 1) * each, :].astype(jnp.bfloat16)


def legendre_inverse_kernel(
    arrived, swapped, table, table_swapped, own, one, one_x, two, two_x, three, four, held, held_swapped
):
    slots, rows, degrees = table.shape
    waves = arrived.shape[0]
    row_count = rows // waves
    each = slots * row_count
    for wave in range(waves):
        held[wave * each : (wave + 1) * each, :] = arrived[wave].astype(jnp.float32)
        held_swapped[wave * each : (wave + 1) * each, :] = pltpu.roll(swapped[wave].astype(jnp.float32), 64, 1)

    def share(ref, slot, legendre):
        weighted = jnp.concatenate(
            [ref[pl.ds(slot * row_count + member, waves, stride=each), :] for member in range(row_count)], axis=0
        )
        return dot(weighted[:, :64].astype(jnp.bfloat16), legendre[slot], TN)

    for pair in range(slots // 2):
        at = pl.ds(16 * pair, 16)
        sums = [
            share(held, slot, table) + share(held_swapped, slot, table_swapped) for slot in (2 * pair, 2 * pair + 1)
        ]
        pieces = [jnp.concatenate([s[8 * chunk : 8 * chunk + 8] for s in sums], axis=0) for chunk in range(8)]
        own[at, :] = pieces[0]
        targets = (one, one_x, two, two_x, three.at[0], three.at[1], four)
        for target, piece in zip(targets, pieces[1:]):
            target[at, :] = piece.astype(jnp.bfloat16)


def fourier_kernel(
    arrived, swapped, inner_in, inner_t_in, outer_fwd_in, outer_inv_in, place_in, limits_in,
    grid_out, sent,
    inner, inner_t, outer_fwd, outer_inv, place, limits, held, back, turned, products, lines_out, sems, out_sems,
):
    inputs = (
        (place_in, place), (outer_fwd_in, outer_fwd), (limits_in, limits),
        (inner_t_in, inner_t), (inner_in, inner), (outer_inv_in, outer_inv),
    )
    copies = [pltpu.make_async_copy(source, target, sems.at[i]) for i, (source, target) in enumerate(inputs)]
    for copy in copies:
        copy.start()
    row_count = inner.shape[0]
    waves, each, _ = arrived.shape
    slots = waves * each // row_count
    parts = slots // LANES
    levels = grid_out.shape[1]
    mine = lax.broadcasted_iota(jnp.int32, (1, LANES), 1) < 64
    for source in range(waves):
        held[source * each : (source + 1) * each, :] = jnp.where(
            mine, arrived[source].astype(jnp.float32), swapped[source].astype(jnp.float32)
        )
    for copy in copies:
        copy.wait()
    column = lax.broadcasted_iota(jnp.int32, (1, BLOCK), 1).astype(jnp.float32)
    results = []
    for member in range(row_count):
        points = jnp.concatenate([limits[member, :1, :]] * (BLOCK // LANES), axis=1)
        lines = held[pl.ds(member, slots, stride=row_count), :].astype(jnp.bfloat16)
        coef = dot(place[0], lines, NT)
        for step in range(BLOCKS):
            rows = pl.ds(step * levels, levels)
            for part in range(parts):
                real = coef[:levels, part * LANES : (part + 1) * LANES]
                imag = coef[levels:, part * LANES : (part + 1) * LANES]
                at = part * 2 * LANES
                cosine = outer_fwd[member, step : step + 1, at : at + LANES]
                sine = outer_fwd[member, step : step + 1, at + LANES : at + 2 * LANES]
                turned[member, rows, at : at + LANES] = (real * cosine - imag * sine).astype(jnp.bfloat16)
                turned[member, rows, at + LANES : at + 2 * LANES] = (real * sine + imag * cosine).astype(jnp.bfloat16)
        values = dot(turned[member], inner_t[member], NN)
        for step in range(BLOCKS):
            width = min(BLOCK, LONPAD - step * BLOCK)
            line = values[step * levels : (step + 1) * levels]
            line = jnp.where(column + step * BLOCK < points, line, 0.0).astype(jnp.bfloat16)
            lines_out[member, :, step * BLOCK : step * BLOCK + width] = line[:, :width]
            line = line.astype(jnp.float32)
            partner = pltpu.roll(line, levels - 1, 0)
            products[member, step * levels : (step + 1) * levels, :] = (line * partner).astype(jnp.bfloat16)
        result = pltpu.make_async_copy(lines_out.at[member], grid_out.at[member], out_sems.at[member])
        result.start()
        results.append(result)
        reals, imags = [], []
        for part in range(parts):
            at = part * 2 * LANES
            sums = dot(products[member], inner[member, :, at : at + 2 * LANES], NN)
            real = jnp.zeros((levels, LANES), jnp.float32)
            imag = jnp.zeros((levels, LANES), jnp.float32)
            for step in range(BLOCKS):
                rows = slice(step * levels, (step + 1) * levels)
                cosine = outer_inv[member, step : step + 1, at : at + LANES]
                sine = outer_inv[member, step : step + 1, at + LANES : at + 2 * LANES]
                real += sums[rows, :LANES] * cosine + sums[rows, LANES:] * sine
                imag += sums[rows, LANES:] * cosine - sums[rows, :LANES] * sine
            reals.append(real)
            imags.append(imag)
        analysed = jnp.concatenate([jnp.concatenate(reals, axis=1), jnp.concatenate(imags, axis=1)], axis=0)
        back[pl.ds(member, slots, stride=row_count), :] = dot(
            analysed.T.astype(jnp.bfloat16), place[1], NN
        )
    for source in range(waves):
        sent[source] = back[source * each : (source + 1) * each, :].astype(jnp.bfloat16)
    for result in results:
        result.wait()


def add_three_kernel(two, two_x, three, four, out, out_x):
    out[...] = (
        two[...].astype(jnp.float32) + three[0].astype(jnp.float32) + four[...].astype(jnp.float32)
    ).astype(jnp.bfloat16)
    out_x[...] = (two_x[...].astype(jnp.float32) + three[1].astype(jnp.float32)).astype(jnp.bfloat16)


def add_own_kernel(own, one, one_x, two, two_x, out):
    total = own[...]
    for landed in (one, one_x, two, two_x):
        total = total + landed[...].astype(jnp.float32)
    groups, cols, _ = out.shape
    for group in range(groups):
        out[group] = total[group * cols : (group + 1) * cols]


def shards(spectra, legendre, lat_weight, wave_of_slot, lat_of_row, lon_count):
    waves = lax.axis_size("wave")
    fields = lax.axis_size("field")
    zs = fields // 2
    wave_id = lax.axis_index("wave").astype(jnp.int32).reshape(1)
    field_id = lax.axis_index("field").astype(jnp.int32).reshape(1)
    slots, _, degrees, cols = spectra.shape
    band = legendre.shape[2]
    rows = 2 * band
    row_count = rows // waves
    all_slots = wave_of_slot.shape[0]
    levels = cols * fields
    each = row_count * slots
    coded = slots * 2 * cols

    like_cores = [list(range(core, fields, 2)) for core in range(2)]

    def hop(x, by, cross=0):
        pairs = [
            (i, (2 * (i // 2 + side_of(i % 2) * by) + (i % 2 ^ cross)) % fields) for i in range(fields)
        ]
        return lax.ppermute(x, "field", pairs)

    def swap(x):
        return hop(x, 0, 1)

    def local(kernel, out_shape, name, micros, mebibytes=8, in_specs=None, out_specs=None, scratch=()):
        if in_specs is None:
            in_specs = pl.BlockSpec(memory_space=pltpu.VMEM)
        return pl.pallas_call(
            kernel,
            out_shape=out_shape,
            in_specs=in_specs,
            out_specs=jax.tree.map(lambda _: vmem(), out_shape) if out_specs is None else out_specs,
            scratch_shapes=list(scratch),
            compiler_params=params(mebibytes),
            cost_estimate=cost(micros),
            name=name,
        )

    row_table = jax.ShapeDtypeStruct((slots, rows, degrees), jnp.bfloat16)
    fourier_shape = jax.ShapeDtypeStruct((waves, each, LANES), jnp.bfloat16)
    float_rows = pltpu.VMEM((waves * each, LANES), jnp.float32)

    own = jnp.transpose(spectra, (0, 1, 3, 2)).reshape(coded, degrees)
    own, legendre = lax.optimization_barrier((own, jnp.transpose(legendre, (0, 2, 1))))
    gathered = lax.all_gather(own, "field", axis_index_groups=like_cores)
    legendre_x = swap(legendre)
    table, chosen_x, south_x, live = local(
        functools.partial(own_rows_kernel, waves=waves, fields=fields),
        (
            row_table,
            jax.ShapeDtypeStruct((rows, LANES), jnp.bfloat16),
            jax.ShapeDtypeStruct((rows, LANES), jnp.float32),
            jax.ShapeDtypeStruct((-(-slots // 8) * 8, degrees), jnp.float32),
        ),
        "own_rows",
        2,
        in_specs=[smem(), smem(), hbm(), hbm(), hbm()],
        scratch=[
            pltpu.SMEM(wave_of_slot.shape, jnp.int32),
            pltpu.SMEM(lat_of_row.shape, jnp.int32),
            pltpu.VMEM((slots, band, degrees), jnp.bfloat16),
            pltpu.VMEM((2, rows, LANES), jnp.float32),
            pltpu.VMEM((2, rows, LANES), jnp.float32),
            pltpu.SemaphoreType.DMA((3,)),
        ],
    )(wave_id, field_id, in_hbm(wave_of_slot), in_hbm(lat_of_row), in_hbm(legendre))
    table_x = local(
        partner_rows_kernel,
        row_table,
        "partner_rows",
        2,
        in_specs=[vmem(), vmem(), vmem(), hbm()],
        scratch=[pltpu.VMEM((slots, band, degrees), jnp.bfloat16), pltpu.SemaphoreType.DMA(())],
    )(chosen_x, south_x, live, in_hbm(legendre_x))
    outgoing = local(
        legendre_forward_kernel, fourier_shape, "legendre_forward", 4, 16, in_specs=[vmem()] * 3, scratch=[float_rows]
    )(gathered, table, table_x)
    outgoing, lat_weight = lax.optimization_barrier((outgoing, lat_weight))
    arrived = lax.all_to_all(outgoing, "wave", split_axis=0, concat_axis=0, tiled=True)

    tables = (
        ((row_count, BLOCK, 2 * all_slots), jnp.bfloat16),
        ((row_count, 2 * all_slots, BLOCK), jnp.bfloat16),
        ((row_count, 16, 2 * all_slots), jnp.float32),
        ((row_count, 16, 2 * all_slots), jnp.float32),
        ((2, LANES, LANES), jnp.bfloat16),
        ((row_count, 8, LANES), jnp.float32),
    )
    tables_vmem = [pltpu.VMEM(shape, kind) for shape, kind in tables]
    prepared = local(
        functools.partial(fourier_tables_kernel, fields=fields, zs=zs),
        [pltpu.HBM(shape, kind) for shape, kind in tables],
        "fourier_tables",
        4,
        16,
        in_specs=[smem()] * 5 + [vmem()],
        out_specs=[hbm()] * 6,
        scratch=tables_vmem + [pltpu.SemaphoreType.DMA((6,))],
    )(
        wave_id, field_id, lat_of_row, lon_count, lat_weight,
        wave_of_slot.astype(jnp.float32).reshape(1, all_slots),
    )
    arrived, prepared = lax.optimization_barrier((arrived, prepared))
    prepared = [in_hbm(x) for x in prepared]

    grid_field, sent = local(
        fourier_kernel,
        (jax.ShapeDtypeStruct((row_count, levels, LONPAD), jnp.bfloat16), fourier_shape),
        "fourier",
        6,
        32,
        in_specs=[vmem()] * 2 + [hbm()] * 6,
        out_specs=(hbm(), vmem()),
        scratch=tables_vmem + [
            float_rows,
            float_rows,
            pltpu.VMEM((row_count, BLOCKS * levels, 2 * all_slots), jnp.bfloat16),
            pltpu.VMEM((row_count, BLOCKS * levels, BLOCK), jnp.bfloat16),
            pltpu.VMEM((row_count, levels, LONPAD), jnp.bfloat16),
            pltpu.SemaphoreType.DMA((6,)),
            pltpu.SemaphoreType.DMA((row_count,)),
        ],
    )(arrived, swap(arrived), *prepared)

    returned = lax.all_to_all(sent, "wave", split_axis=0, concat_axis=0, tiled=True)

    chunk = jax.ShapeDtypeStruct((coded, degrees), jnp.bfloat16)
    own, one, one_x, two, two_x, three, four = local(
        legendre_inverse_kernel,
        (
            jax.ShapeDtypeStruct((coded, degrees), jnp.float32),
            chunk, chunk, chunk, chunk, jax.ShapeDtypeStruct((2, coded, degrees), jnp.bfloat16), chunk,
        ),
        "legendre_inverse",
        2,
        16,
        in_specs=[vmem()] * 4,
        scratch=[float_rows, float_rows],
    )(returned, swap(returned), table, table_x)
    three, four = hop(three, -1), hop(four, -2)
    two, two_x = local(add_three_kernel, (chunk, chunk), "add_three", 1, in_specs=[vmem()] * 4)(
        two, two_x, three, four
    )
    two, two_x, one_x = lax.optimization_barrier((two, two_x, one_x))
    two, two_x = hop(two, -2), hop(two_x, -2, 1)
    one, one_x = hop(one, -1), hop(one_x, -1, 1)
    total = local(
        add_own_kernel,
        jax.ShapeDtypeStruct((2 * slots, cols, degrees), jnp.float32),
        "add_own",
        1,
        in_specs=[vmem()] * 5,
    )(own, one, one_x, two, two_x)
    spectral = jnp.transpose(total.reshape(slots, 2, cols, degrees), (0, 1, 3, 2))
    return grid_field, spectral


def solution(mesh):
    in_specs = (P("wave", None, None, "field"), P("wave", None, "field"), P("field"), P(), P(), P())
    out_specs = (P(("wave", "field"), None, None), P("wave", None, None, "field"))
    return jax.shard_map(shards, mesh=mesh, in_specs=in_specs, out_specs=out_specs, check_vma=False)
```

```python
import functools
import math

import jax
import jax.numpy as jnp
from jax import lax
from jax.experimental import pallas as pl
from jax.experimental.pallas import tpu as pltpu
from jax.sharding import PartitionSpec as P

LONPAD = 3200
LANES = 128
BLOCK = 256
BLOCKS = -(-LONPAD // BLOCK)

NT = (((1,), (1,)), ((), ()))
NN = (((1,), (0,)), ((), ()))
TN = (((0,), (0,)), ((), ()))


def dot(a, b, dims):
    return lax.dot_general(a, b, dims, preferred_element_type=jnp.float32)


def params(mebibytes):
    return pltpu.CompilerParams(vmem_limit_bytes=mebibytes * 1024 * 1024)


def in_hbm(x):
    return pltpu.with_memory_space_constraint(x, pltpu.HBM)


def cost(micros):
    return pl.CostEstimate(flops=0, bytes_accessed=int(micros * 3.7e6), transcendentals=0)


def smem():
    return pl.BlockSpec(memory_space=pltpu.SMEM)


def vmem():
    return pl.BlockSpec(memory_space=pltpu.VMEM)


def hbm():
    return pl.BlockSpec(memory_space=pltpu.HBM)


def side_of(core):
    return 1 - 2 * core


def ordered_rows(chosen, south, live, legendre, out):
    slots, band, degrees = legendre.shape
    odd = (lax.broadcasted_iota(jnp.int32, (1, degrees), 1) & 1).astype(jnp.float32)
    sign = 1.0 - 2.0 * (south[:, :1] * odd)
    for slot in range(slots):
        table = dot(chosen[:, :band], legendre[slot], NN) * sign
        out[slot] = (table * live[slot : slot + 1, :]).astype(jnp.bfloat16)


def own_rows_kernel(
    wave_id, field_id, wave_of_slot, lat_of_row, legendre,
    out, chosen_x, south_x, live,
    slot_waves, row_lats, held, pick, south, sems, *, waves, fields,
):
    copies = [
        pltpu.make_async_copy(source, target, sems.at[i])
        for i, (source, target) in enumerate(((lat_of_row, row_lats), (wave_of_slot, slot_waves), (legendre, held)))
    ]
    for copy in copies:
        copy.start()
    slots, band, degrees = held.shape
    rows = out.shape[1]
    row_count = rows // waves
    half = row_lats.shape[0] // 2
    own, field = wave_id[0], field_id[0]
    lane = lax.broadcasted_iota(jnp.int32, (1, LANES), 1)
    copies[0].wait()
    for at in range(2):
        this = field ^ at
        for row in range(rows):
            member, wave = divmod(row, waves)
            lat = row_lats[(wave * fields + this) * row_count + member]
            is_south = lat >= half
            hemi = jnp.where(is_south, 2 * half - 1 - lat, lat) - this * band
            pick[at, row : row + 1, :] = (lane == hemi).astype(jnp.float32)
            south[at, row : row + 1, :] = jnp.broadcast_to(is_south.astype(jnp.float32), (1, LANES))
    chosen_x[...] = pick[1].astype(jnp.bfloat16)
    south_x[...] = south[1]
    offsets = lax.broadcasted_iota(jnp.int32, (1, degrees), 1)
    copies[1].wait()
    live[...] = jnp.zeros(live.shape, jnp.float32)
    for slot in range(slots):
        live[slot : slot + 1, :] = (offsets < degrees - slot_waves[own * slots + slot]).astype(jnp.float32)
    copies[2].wait()
    ordered_rows(pick[0].astype(jnp.bfloat16), south[0], live, held, out)


def partner_rows_kernel(chosen, south, live, legendre, out, held, sem):
    copy = pltpu.make_async_copy(legendre, held, sem)
    copy.start()
    copy.wait()
    ordered_rows(chosen[...], south[...], live, held, out)


def sin_cos(phase, period):
    inverse = 1.0 / period
    turns = (phase - jnp.floor(phase * inverse + 0.5) * period) * inverse
    quarter = jnp.floor(4.0 * turns + 0.5)
    w = (2.0 * math.pi) * (turns - 0.25 * quarter)
    w2 = w * w
    sine = w * (1.0 + w2 * (-1.0 / 6 + w2 * (1.0 / 120 + w2 * (-1.0 / 5040 + w2 * (1.0 / 362880)))))
    cosine = 1.0 + w2 * (-0.5 + w2 * (1.0 / 24 + w2 * (-1.0 / 720 + w2 * (1.0 / 40320))))
    size = jnp.abs(quarter)
    odd = size == 1.0
    flipped = size >= 2.0
    cos_out = jnp.where(odd, sine, cosine)
    sin_out = jnp.where(odd, cosine, sine)
    cos_out = jnp.where(flipped | (quarter == 1.0), -cos_out, cos_out)
    sin_out = jnp.where(flipped | (quarter == -1.0), -sin_out, sin_out)
    return cos_out, sin_out


def fourier_tables_kernel(
    wave_id, field_id, lat_of_row, lon_count, lat_weight, waves_row,
    inner_out, inner_t_out, outer_fwd_out, outer_inv_out, place_out, limits_out,
    inner, inner_t, outer_fwd, outer_inv, place, limits, sems, *, fields, zs,
):
    row_count = inner.shape[0]
    band = lat_weight.shape[0]
    half = lon_count.shape[0]
    slots = waves_row.shape[1]
    steps = outer_fwd.shape[1]
    wave, field = wave_id[0], field_id[0]
    for member in range(row_count):
        lat = lat_of_row[(wave * fields + field) * row_count + member]
        hemi = jnp.where(lat >= half, 2 * half - 1 - lat, lat)
        points = lon_count[hemi].astype(jnp.float32)
        period = jnp.broadcast_to(points, (1, LANES))
        limits[member] = jnp.broadcast_to(points, limits.shape[1:])
        weight = lat_weight[hemi - field * band] / jnp.sqrt(period)
        for part in range(slots // LANES):
            m = waves_row[:, part * LANES : (part + 1) * LANES]
            at = part * 2 * LANES
            x = lax.broadcasted_iota(jnp.int32, (BLOCK, LANES), 0).astype(jnp.float32)
            cosine, sine = sin_cos(x * m, period)
            both = jnp.concatenate([cosine, -sine], axis=1)
            inner[member, :, at : at + 2 * LANES] = both.astype(jnp.bfloat16)
            inner_t[member, at : at + 2 * LANES, :] = both.T.astype(jnp.bfloat16)
            x = (BLOCK * lax.broadcasted_iota(jnp.int32, (steps, LANES), 0)).astype(jnp.float32)
            cosine, sine = sin_cos(x * m, period)
            both = jnp.concatenate([cosine, sine], axis=1)
            outer_fwd[member, :, at : at + 2 * LANES] = both * (1.0 / math.sqrt(slots))
            outer_inv[member, :, at : at + 2 * LANES] = both * jnp.concatenate([weight, weight], axis=1)
    at = lax.broadcasted_iota(jnp.int32, (LANES, LANES), 1)
    core, chunk, part, low = (field & 1) ^ (at >> 6), (at >> 3) & 7, (at >> 2) & 1, at & 3
    away = (chunk + 1) >> 1
    cross = ((chunk & 1) ^ 1) & (chunk > 0).astype(jnp.int32)
    z = ((field >> 1) - side_of(core) * away + zs) & (zs - 1)
    row = lax.broadcasted_iota(jnp.int32, (LANES, LANES), 0)
    gathered_z = chunk + core * (zs - 1 - 2 * chunk)
    for way, shard in enumerate((2 * gathered_z + core, 2 * z + (core ^ cross))):
        place[way] = (row == part * 64 + shard * 4 + low).astype(jnp.bfloat16)
    results = (
        (inner, inner_out), (inner_t, inner_t_out), (outer_fwd, outer_fwd_out),
        (outer_inv, outer_inv_out), (place, place_out), (limits, limits_out),
    )
    copies = [pltpu.make_async_copy(source, target, sems.at[i]) for i, (source, target) in enumerate(results)]
    for copy in copies:
        copy.start()
    for copy in copies:
        copy.wait()


def legendre_forward_kernel(gathered, gathered_x, table, out, held):
    slots, rows, degrees = table.shape
    waves = out.shape[0]
    row_count = rows // waves
    each = slots * row_count
    for pair in range(slots // 2):
        at = pl.ds(16 * pair, 16)
        both = [source[z, at, :].astype(jnp.float32) for source in (gathered, gathered_x) for z in range(source.shape[0])]
        for half in range(2):
            slot = 2 * pair + half
            spec = jnp.concatenate([b[8 * half : 8 * half + 8] for b in both], axis=0).astype(jnp.bfloat16)
            sums = dot(table[slot], spec, NT)
            for member in range(row_count):
                held[pl.ds(slot * row_count + member, waves, stride=each), :] = sums[
                    waves * member : waves * (member + 1)
                ]
    for wave in range(waves):
        out[wave] = held[wave * each : (wave + 1) * each, :].astype(jnp.bfloat16)


def legendre_inverse_kernel(
    arrived, swapped, table, table_swapped, own, one, one_x, two, two_x, three, four, held, held_swapped
):
    slots, rows, degrees = table.shape
    waves = arrived.shape[0]
    row_count = rows // waves
    each = slots * row_count
    for wave in range(waves):
        held[wave * each : (wave + 1) * each, :] = arrived[wave].astype(jnp.float32)
        held_swapped[wave * each : (wave + 1) * each, :] = pltpu.roll(swapped[wave].astype(jnp.float32), 64, 1)

    def share(ref, slot, legendre):
        weighted = jnp.concatenate(
            [ref[pl.ds(slot * row_count + member, waves, stride=each), :] for member in range(row_count)], axis=0
        )
        return dot(weighted[:, :64].astype(jnp.bfloat16), legendre[slot], TN)

    for pair in range(slots // 2):
        at = pl.ds(16 * pair, 16)
        sums = [
            share(held, slot, table) + share(held_swapped, slot, table_swapped) for slot in (2 * pair, 2 * pair + 1)
        ]
        pieces = [jnp.concatenate([s[8 * chunk : 8 * chunk + 8] for s in sums], axis=0) for chunk in range(8)]
        own[at, :] = pieces[0]
        targets = (one, one_x, two, two_x, three.at[0], three.at[1], four)
        for target, piece in zip(targets, pieces[1:]):
            target[at, :] = piece.astype(jnp.bfloat16)


def fourier_kernel(
    arrived, inner_in, inner_t_in, outer_fwd_in, outer_inv_in, place_in, limits_in,
    grid_out, sent,
    inner, inner_t, outer_fwd, outer_inv, place, limits, held, back, turned, products, lines_out, sems, out_sems,
):
    inputs = (
        (place_in, place), (outer_fwd_in, outer_fwd), (limits_in, limits),
        (inner_t_in, inner_t), (inner_in, inner), (outer_inv_in, outer_inv),
    )
    copies = [pltpu.make_async_copy(source, target, sems.at[i]) for i, (source, target) in enumerate(inputs)]
    for copy in copies:
        copy.start()
    row_count = inner.shape[0]
    waves, each, _ = arrived.shape
    slots = waves * each // row_count
    parts = slots // LANES
    levels = grid_out.shape[1]
    for source in range(waves):
        held[source * each : (source + 1) * each, :] = arrived[source].astype(jnp.float32)
    for copy in copies[:3]:
        copy.wait()
    column = lax.broadcasted_iota(jnp.int32, (1, BLOCK), 1).astype(jnp.float32)
    results = []
    for member in range(row_count):
        points = jnp.concatenate([limits[member, :1, :]] * (BLOCK // LANES), axis=1)
        lines = held[pl.ds(member, slots, stride=row_count), :].astype(jnp.bfloat16)
        coef = dot(place[0], lines, NT)
        for step in range(BLOCKS):
            rows = pl.ds(step * levels, levels)
            for part in range(parts):
                real = coef[:levels, part * LANES : (part + 1) * LANES]
                imag = coef[levels:, part * LANES : (part + 1) * LANES]
                at = part * 2 * LANES
                cosine = outer_fwd[member, step : step + 1, at : at + LANES]
                sine = outer_fwd[member, step : step + 1, at + LANES : at + 2 * LANES]
                turned[member, rows, at : at + LANES] = (real * cosine - imag * sine).astype(jnp.bfloat16)
                turned[member, rows, at + LANES : at + 2 * LANES] = (real * sine + imag * cosine).astype(jnp.bfloat16)
        if member == 0:
            copies[3].wait()
        values = dot(turned[member], inner_t[member], NN)
        for step in range(BLOCKS):
            width = min(BLOCK, LONPAD - step * BLOCK)
            line = values[step * levels : (step + 1) * levels]
            line = jnp.where(column + step * BLOCK < points, line, 0.0).astype(jnp.bfloat16)
            lines_out[member, :, step * BLOCK : step * BLOCK + width] = line[:, :width]
            line = line.astype(jnp.float32)
            partner = pltpu.roll(line, levels - 1, 0)
            products[member, step * levels : (step + 1) * levels, :] = (line * partner).astype(jnp.bfloat16)
        result = pltpu.make_async_copy(lines_out.at[member], grid_out.at[member], out_sems.at[member])
        result.start()
        results.append(result)
        if member == 0:
            copies[4].wait()
            copies[5].wait()
        reals, imags = [], []
        for part in range(parts):
            at = part * 2 * LANES
            sums = dot(products[member], inner[member, :, at : at + 2 * LANES], NN)
            real = jnp.zeros((levels, LANES), jnp.float32)
            imag = jnp.zeros((levels, LANES), jnp.float32)
            for step in range(BLOCKS):
                rows = slice(step * levels, (step + 1) * levels)
                cosine = outer_inv[member, step : step + 1, at : at + LANES]
                sine = outer_inv[member, step : step + 1, at + LANES : at + 2 * LANES]
                real += sums[rows, :LANES] * cosine + sums[rows, LANES:] * sine
                imag += sums[rows, LANES:] * cosine - sums[rows, :LANES] * sine
            reals.append(real)
            imags.append(imag)
        analysed = jnp.concatenate([jnp.concatenate(reals, axis=1), jnp.concatenate(imags, axis=1)], axis=0)
        back[pl.ds(member, slots, stride=row_count), :] = dot(
            analysed.T.astype(jnp.bfloat16), place[1], NN
        )
    for source in range(waves):
        sent[source] = back[source * each : (source + 1) * each, :].astype(jnp.bfloat16)
    for result in results:
        result.wait()


def add_three_kernel(two, two_x, three, four, out, out_x):
    out[...] = (
        two[...].astype(jnp.float32) + three[0].astype(jnp.float32) + four[...].astype(jnp.float32)
    ).astype(jnp.bfloat16)
    out_x[...] = (two_x[...].astype(jnp.float32) + three[1].astype(jnp.float32)).astype(jnp.bfloat16)


def add_own_kernel(own, one, one_x, two, two_x, out):
    total = own[...]
    for landed in (one, one_x, two, two_x):
        total = total + landed[...].astype(jnp.float32)
    groups, cols, _ = out.shape
    for group in range(groups):
        out[group] = total[group * cols : (group + 1) * cols]


def shards(spectra, legendre, lat_weight, wave_of_slot, lat_of_row, lon_count):
    waves = lax.axis_size("wave")
    fields = lax.axis_size("field")
    zs = fields // 2
    wave_id = lax.axis_index("wave").astype(jnp.int32).reshape(1)
    field_id = lax.axis_index("field").astype(jnp.int32).reshape(1)
    slots, _, degrees, cols = spectra.shape
    band = legendre.shape[2]
    rows = 2 * band
    row_count = rows // waves
    all_slots = wave_of_slot.shape[0]
    levels = cols * fields
    each = row_count * slots
    coded = slots * 2 * cols

    like_cores = [list(range(0, fields, 2)), list(range(fields - 1, 0, -2))]

    def hop(x, by, cross=0):
        pairs = [
            (i, (2 * (i // 2 + side_of(i % 2) * by) + (i % 2 ^ cross)) % fields) for i in range(fields)
        ]
        return lax.ppermute(x, "field", pairs)

    def swap(x):
        return hop(x, 0, 1)

    def local(kernel, out_shape, name, micros, mebibytes=8, in_specs=None, out_specs=None, scratch=()):
        if in_specs is None:
            in_specs = pl.BlockSpec(memory_space=pltpu.VMEM)
        return pl.pallas_call(
            kernel,
            out_shape=out_shape,
            in_specs=in_specs,
            out_specs=jax.tree.map(lambda _: vmem(), out_shape) if out_specs is None else out_specs,
            scratch_shapes=list(scratch),
            compiler_params=params(mebibytes),
            cost_estimate=cost(micros),
            name=name,
        )

    row_table = jax.ShapeDtypeStruct((slots, rows, degrees), jnp.bfloat16)
    fourier_shape = jax.ShapeDtypeStruct((waves, each, LANES), jnp.bfloat16)
    float_rows = pltpu.VMEM((waves * each, LANES), jnp.float32)

    own = jnp.transpose(spectra, (0, 1, 3, 2)).reshape(coded, degrees)
    gathered = lax.all_gather(own, "field", axis_index_groups=like_cores)
    gathered, legendre = lax.optimization_barrier((gathered, jnp.transpose(legendre, (0, 2, 1))))
    gathered_x = swap(gathered)
    table, chosen_x, south_x, live = local(
        functools.partial(own_rows_kernel, waves=waves, fields=fields),
        (
            row_table,
            jax.ShapeDtypeStruct((rows, LANES), jnp.bfloat16),
            jax.ShapeDtypeStruct((rows, LANES), jnp.float32),
            jax.ShapeDtypeStruct((-(-slots // 8) * 8, degrees), jnp.float32),
        ),
        "own_rows",
        2,
        in_specs=[smem(), smem(), hbm(), hbm(), hbm()],
        scratch=[
            pltpu.SMEM(wave_of_slot.shape, jnp.int32),
            pltpu.SMEM(lat_of_row.shape, jnp.int32),
            pltpu.VMEM((slots, band, degrees), jnp.bfloat16),
            pltpu.VMEM((2, rows, LANES), jnp.float32),
            pltpu.VMEM((2, rows, LANES), jnp.float32),
            pltpu.SemaphoreType.DMA((3,)),
        ],
    )(wave_id, field_id, in_hbm(wave_of_slot), in_hbm(lat_of_row), in_hbm(legendre))
    outgoing = local(
        legendre_forward_kernel, fourier_shape, "legendre_forward", 4, 16, in_specs=[vmem()] * 3, scratch=[float_rows]
    )(gathered, gathered_x, table)
    outgoing, lat_weight = lax.optimization_barrier((outgoing, lat_weight))
    arrived = lax.all_to_all(outgoing, "wave", split_axis=0, concat_axis=0, tiled=True)
    tables = (
        ((row_count, BLOCK, 2 * all_slots), jnp.bfloat16),
        ((row_count, 2 * all_slots, BLOCK), jnp.bfloat16),
        ((row_count, 16, 2 * all_slots), jnp.float32),
        ((row_count, 16, 2 * all_slots), jnp.float32),
        ((2, LANES, LANES), jnp.bfloat16),
        ((row_count, 8, LANES), jnp.float32),
    )
    tables_vmem = [pltpu.VMEM(shape, kind) for shape, kind in tables]
    prepared = local(
        functools.partial(fourier_tables_kernel, fields=fields, zs=zs),
        [pltpu.HBM(shape, kind) for shape, kind in tables],
        "fourier_tables",
        4,
        16,
        in_specs=[smem()] * 5 + [vmem()],
        out_specs=[hbm()] * 6,
        scratch=tables_vmem + [pltpu.SemaphoreType.DMA((6,))],
    )(
        wave_id, field_id, lat_of_row, lon_count, lat_weight,
        wave_of_slot.astype(jnp.float32).reshape(1, all_slots),
    )
    prepared, legendre = lax.optimization_barrier((prepared, legendre))
    legendre_x = swap(legendre)
    arrived, prepared = lax.optimization_barrier((arrived, prepared))
    prepared = [in_hbm(x) for x in prepared]

    grid_field, sent = local(
        fourier_kernel,
        (jax.ShapeDtypeStruct((row_count, levels, LONPAD), jnp.bfloat16), fourier_shape),
        "fourier",
        6,
        32,
        in_specs=[vmem()] + [hbm()] * 6,
        out_specs=(hbm(), vmem()),
        scratch=tables_vmem + [
            float_rows,
            float_rows,
            pltpu.VMEM((row_count, BLOCKS * levels, 2 * all_slots), jnp.bfloat16),
            pltpu.VMEM((row_count, BLOCKS * levels, BLOCK), jnp.bfloat16),
            pltpu.VMEM((row_count, levels, LONPAD), jnp.bfloat16),
            pltpu.SemaphoreType.DMA((6,)),
            pltpu.SemaphoreType.DMA((row_count,)),
        ],
    )(arrived, *prepared)

    sent, legendre_x = lax.optimization_barrier((sent, legendre_x))
    returned = lax.all_to_all(sent, "wave", split_axis=0, concat_axis=0, tiled=True)

    table_x = local(
        partner_rows_kernel,
        row_table,
        "partner_rows",
        2,
        in_specs=[vmem(), vmem(), vmem(), hbm()],
        scratch=[pltpu.VMEM((slots, band, degrees), jnp.bfloat16), pltpu.SemaphoreType.DMA(())],
    )(chosen_x, south_x, live, in_hbm(legendre_x))
    returned, table_x = lax.optimization_barrier((returned, table_x))

    chunk = jax.ShapeDtypeStruct((coded, degrees), jnp.bfloat16)
    own, one, one_x, two, two_x, three, four = local(
        legendre_inverse_kernel,
        (
            jax.ShapeDtypeStruct((coded, degrees), jnp.float32),
            chunk, chunk, chunk, chunk, jax.ShapeDtypeStruct((2, coded, degrees), jnp.bfloat16), chunk,
        ),
        "legendre_inverse",
        2,
        16,
        in_specs=[vmem()] * 4,
        scratch=[float_rows, float_rows],
    )(returned, swap(returned), table, table_x)
    three, four = hop(three, -1), hop(four, -2)
    two, two_x = local(add_three_kernel, (chunk, chunk), "add_three", 1, in_specs=[vmem()] * 4)(
        two, two_x, three, four
    )
    one, one_x = hop(one, -1), hop(one_x, -1, 1)
    two, two_x = hop(two, -2), hop(two_x, -2, 1)
    total = local(
        add_own_kernel,
        jax.ShapeDtypeStruct((2 * slots, cols, degrees), jnp.float32),
        "add_own",
        1,
        in_specs=[vmem()] * 5,
    )(own, one, one_x, two, two_x)
    spectral = jnp.transpose(total.reshape(slots, 2, cols, degrees), (0, 1, 3, 2))
    return grid_field, spectral


def solution(mesh):
    in_specs = (P("wave", None, None, "field"), P("wave", None, "field"), P("field"), P(), P(), P())
    out_specs = (P(("wave", "field"), None, None), P("wave", None, None, "field"))
    return jax.shard_map(shards, mesh=mesh, in_specs=in_specs, out_specs=out_specs, check_vma=False)
```

```python
import functools
import math

import jax
import jax.numpy as jnp
from jax import lax
from jax.experimental import pallas as pl
from jax.experimental.pallas import tpu as pltpu
from jax.sharding import PartitionSpec as P

LONPAD = 3200
LANES = 128
BLOCK = 256
BLOCKS = -(-LONPAD // BLOCK)

NT = (((1,), (1,)), ((), ()))
NN = (((1,), (0,)), ((), ()))
TN = (((0,), (0,)), ((), ()))


def dot(a, b, dims):
    return lax.dot_general(a, b, dims, preferred_element_type=jnp.float32)


def params(mebibytes):
    return pltpu.CompilerParams(vmem_limit_bytes=mebibytes * 1024 * 1024)


def in_hbm(x):
    return pltpu.with_memory_space_constraint(x, pltpu.HBM)


def cost(micros):
    return pl.CostEstimate(flops=0, bytes_accessed=int(micros * 3.7e6), transcendentals=0)


def smem():
    return pl.BlockSpec(memory_space=pltpu.SMEM)


def vmem():
    return pl.BlockSpec(memory_space=pltpu.VMEM)


def hbm():
    return pl.BlockSpec(memory_space=pltpu.HBM)


def side_of(core):
    return 1 - 2 * core


def ordered_rows(chosen, south, live, legendre, out):
    slots, band, degrees = legendre.shape
    odd = (lax.broadcasted_iota(jnp.int32, (1, degrees), 1) & 1).astype(jnp.float32)
    sign = 1.0 - 2.0 * (south[:, :1] * odd)
    for slot in range(slots):
        table = dot(chosen[:, :band], legendre[slot], NN) * sign
        out[slot] = (table * live[slot : slot + 1, :]).astype(jnp.bfloat16)


def own_rows_kernel(
    wave_id, field_id, wave_of_slot, lat_of_row, legendre,
    out, chosen_x, south_x, live,
    slot_waves, row_lats, held, pick, south, sems, *, waves, fields,
):
    copies = [
        pltpu.make_async_copy(source, target, sems.at[i])
        for i, (source, target) in enumerate(((lat_of_row, row_lats), (wave_of_slot, slot_waves), (legendre, held)))
    ]
    for copy in copies:
        copy.start()
    slots, band, degrees = held.shape
    rows = out.shape[1]
    row_count = rows // waves
    half = row_lats.shape[0] // 2
    own, field = wave_id[0], field_id[0]
    lane = lax.broadcasted_iota(jnp.int32, (1, LANES), 1)
    copies[0].wait()
    for at in range(2):
        this = field ^ at
        for row in range(rows):
            member, wave = divmod(row, waves)
            lat = row_lats[(wave * fields + this) * row_count + member]
            is_south = lat >= half
            hemi = jnp.where(is_south, 2 * half - 1 - lat, lat) - this * band
            pick[at, row : row + 1, :] = (lane == hemi).astype(jnp.float32)
            south[at, row : row + 1, :] = jnp.broadcast_to(is_south.astype(jnp.float32), (1, LANES))
    chosen_x[...] = pick[1].astype(jnp.bfloat16)
    south_x[...] = south[1]
    offsets = lax.broadcasted_iota(jnp.int32, (1, degrees), 1)
    copies[1].wait()
    live[...] = jnp.zeros(live.shape, jnp.float32)
    for slot in range(slots):
        live[slot : slot + 1, :] = (offsets < degrees - slot_waves[own * slots + slot]).astype(jnp.float32)
    copies[2].wait()
    ordered_rows(pick[0].astype(jnp.bfloat16), south[0], live, held, out)


def partner_rows_kernel(chosen, south, live, legendre, out, held, sem):
    copy = pltpu.make_async_copy(legendre, held, sem)
    copy.start()
    copy.wait()
    ordered_rows(chosen[...], south[...], live, held, out)


def sin_cos(phase, period):
    inverse = 1.0 / period
    turns = (phase - jnp.floor(phase * inverse + 0.5) * period) * inverse
    quarter = jnp.floor(4.0 * turns + 0.5)
    w = (2.0 * math.pi) * (turns - 0.25 * quarter)
    w2 = w * w
    sine = w * (1.0 + w2 * (-1.0 / 6 + w2 * (1.0 / 120 + w2 * (-1.0 / 5040 + w2 * (1.0 / 362880)))))
    cosine = 1.0 + w2 * (-0.5 + w2 * (1.0 / 24 + w2 * (-1.0 / 720 + w2 * (1.0 / 40320))))
    size = jnp.abs(quarter)
    odd = size == 1.0
    flipped = size >= 2.0
    cos_out = jnp.where(odd, sine, cosine)
    sin_out = jnp.where(odd, cosine, sine)
    cos_out = jnp.where(flipped | (quarter == 1.0), -cos_out, cos_out)
    sin_out = jnp.where(flipped | (quarter == -1.0), -sin_out, sin_out)
    return cos_out, sin_out


def fourier_tables_kernel(
    wave_id, field_id, lat_of_row, lon_count, lat_weight, waves_row,
    inner_out, inner_t_out, outer_fwd_out, outer_inv_out, place_out, limits_out,
    inner, inner_t, outer_fwd, outer_inv, place, limits, sems, *, fields, zs,
):
    row_count = inner.shape[0]
    band = lat_weight.shape[0]
    half = lon_count.shape[0]
    slots = waves_row.shape[1]
    steps = outer_fwd.shape[1]
    wave, field = wave_id[0], field_id[0]
    for member in range(row_count):
        lat = lat_of_row[(wave * fields + field) * row_count + member]
        hemi = jnp.where(lat >= half, 2 * half - 1 - lat, lat)
        points = lon_count[hemi].astype(jnp.float32)
        period = jnp.broadcast_to(points, (1, LANES))
        limits[member] = jnp.broadcast_to(points, limits.shape[1:])
        weight = lat_weight[hemi - field * band] / jnp.sqrt(period)
        for part in range(slots // LANES):
            m = waves_row[:, part * LANES : (part + 1) * LANES]
            at = part * 2 * LANES
            x = lax.broadcasted_iota(jnp.int32, (BLOCK, LANES), 0).astype(jnp.float32)
            cosine, sine = sin_cos(x * m, period)
            both = jnp.concatenate([cosine, -sine], axis=1)
            inner[member, :, at : at + 2 * LANES] = both.astype(jnp.bfloat16)
            inner_t[member, at : at + 2 * LANES, :] = both.T.astype(jnp.bfloat16)
            x = (BLOCK * lax.broadcasted_iota(jnp.int32, (steps, LANES), 0)).astype(jnp.float32)
            cosine, sine = sin_cos(x * m, period)
            both = jnp.concatenate([cosine, sine], axis=1)
            outer_fwd[member, :, at : at + 2 * LANES] = both * (1.0 / math.sqrt(slots))
            outer_inv[member, :, at : at + 2 * LANES] = both * jnp.concatenate([weight, weight], axis=1)
    at = lax.broadcasted_iota(jnp.int32, (LANES, LANES), 1)
    core, chunk, part, low = (field & 1) ^ (at >> 6), (at >> 3) & 7, (at >> 2) & 1, at & 3
    away = (chunk + 1) >> 1
    cross = ((chunk & 1) ^ 1) & (chunk > 0).astype(jnp.int32)
    z = ((field >> 1) - side_of(core) * away + zs) & (zs - 1)
    row = lax.broadcasted_iota(jnp.int32, (LANES, LANES), 0)
    gathered_z = chunk + core * (zs - 1 - 2 * chunk)
    for way, shard in enumerate((2 * gathered_z + core, 2 * z + (core ^ cross))):
        place[way] = (row == part * 64 + shard * 4 + low).astype(jnp.bfloat16)
    results = (
        (inner, inner_out), (inner_t, inner_t_out), (outer_fwd, outer_fwd_out),
        (outer_inv, outer_inv_out), (place, place_out), (limits, limits_out),
    )
    copies = [pltpu.make_async_copy(source, target, sems.at[i]) for i, (source, target) in enumerate(results)]
    for copy in copies:
        copy.start()
    for copy in copies:
        copy.wait()


def unpack_lines(messages, held, each):
    for at in range(messages.shape[0]):
        message = messages[at].astype(jnp.float32)
        for group in range(each // 4):
            first = at * each + 4 * group
            held[first : first + 4, :] = message[:, group * LANES : (group + 1) * LANES]


def pack_lines(held, messages, each):
    for at in range(messages.shape[0]):
        groups = [held[at * each + 4 * group : at * each + 4 * group + 4, :] for group in range(each // 4)]
        messages[at] = jnp.concatenate(groups, axis=1).astype(jnp.bfloat16)


def legendre_forward_kernel(gathered, gathered_x, table, out, held):
    slots, rows, degrees = table.shape
    waves = out.shape[0]
    row_count = rows // waves
    each = slots * row_count
    for pair in range(slots // 2):
        at = pl.ds(16 * pair, 16)
        both = [source[z, at, :].astype(jnp.float32) for source in (gathered, gathered_x) for z in range(source.shape[0])]
        for half in range(2):
            slot = 2 * pair + half
            spec = jnp.concatenate([b[8 * half : 8 * half + 8] for b in both], axis=0).astype(jnp.bfloat16)
            sums = dot(table[slot], spec, NT)
            for member in range(row_count):
                held[pl.ds(slot * row_count + member, waves, stride=each), :] = sums[
                    waves * member : waves * (member + 1)
                ]
    pack_lines(held, out, each)


def legendre_inverse_kernel(
    arrived, swapped, table, table_swapped, own, one, one_x, two, two_x, three, four, held, held_swapped
):
    slots, rows, degrees = table.shape
    waves = arrived.shape[0]
    row_count = rows // waves
    each = slots * row_count
    unpack_lines(arrived, held, each)
    unpack_lines(swapped, held_swapped, each)

    def share(ref, slot, legendre, turn=0):
        weighted = jnp.concatenate(
            [ref[pl.ds(slot * row_count + member, waves, stride=each), :] for member in range(row_count)], axis=0
        )
        if turn:
            weighted = pltpu.roll(weighted, turn, 1)
        return dot(weighted[:, :64].astype(jnp.bfloat16), legendre[slot], TN)

    for pair in range(slots // 2):
        at = pl.ds(16 * pair, 16)
        sums = [
            share(held, slot, table) + share(held_swapped, slot, table_swapped, 64) for slot in (2 * pair, 2 * pair + 1)
        ]
        pieces = [jnp.concatenate([s[8 * chunk : 8 * chunk + 8] for s in sums], axis=0) for chunk in range(8)]
        own[at, :] = pieces[0]
        targets = (one, one_x, two, two_x, three.at[0], three.at[1], four)
        for target, piece in zip(targets, pieces[1:]):
            target[at, :] = piece.astype(jnp.bfloat16)


def fourier_kernel(
    arrived, inner_in, inner_t_in, outer_fwd_in, outer_inv_in, place_in, limits_in,
    grid_out, sent,
    inner, inner_t, outer_fwd, outer_inv, place, limits, held, back, turned, products, lines_out, sems, out_sems,
):
    inputs = (
        (place_in, place), (outer_fwd_in, outer_fwd), (limits_in, limits),
        (inner_t_in, inner_t), (inner_in, inner), (outer_inv_in, outer_inv),
    )
    copies = [pltpu.make_async_copy(source, target, sems.at[i]) for i, (source, target) in enumerate(inputs)]
    for copy in copies:
        copy.start()
    row_count = inner.shape[0]
    slots = held.shape[0] // row_count
    each = held.shape[0] // arrived.shape[0]
    parts = slots // LANES
    levels = grid_out.shape[1]
    unpack_lines(arrived, held, each)
    for copy in copies[:3]:
        copy.wait()
    column = lax.broadcasted_iota(jnp.int32, (1, BLOCK), 1).astype(jnp.float32)
    results = []
    for member in range(row_count):
        points = jnp.concatenate([limits[member, :1, :]] * (BLOCK // LANES), axis=1)
        lines = held[pl.ds(member, slots, stride=row_count), :].astype(jnp.bfloat16)
        coef = dot(place[0], lines, NT)
        for step in range(BLOCKS):
            rows = pl.ds(step * levels, levels)
            for part in range(parts):
                real = coef[:levels, part * LANES : (part + 1) * LANES]
                imag = coef[levels:, part * LANES : (part + 1) * LANES]
                at = part * 2 * LANES
                cosine = outer_fwd[member, step : step + 1, at : at + LANES]
                sine = outer_fwd[member, step : step + 1, at + LANES : at + 2 * LANES]
                turned[member, rows, at : at + LANES] = (real * cosine - imag * sine).astype(jnp.bfloat16)
                turned[member, rows, at + LANES : at + 2 * LANES] = (real * sine + imag * cosine).astype(jnp.bfloat16)
        if member == 0:
            copies[3].wait()
        values = dot(turned[member], inner_t[member], NN)
        for step in range(BLOCKS):
            width = min(BLOCK, LONPAD - step * BLOCK)
            line = values[step * levels : (step + 1) * levels]
            line = jnp.where(column + step * BLOCK < points, line, 0.0).astype(jnp.bfloat16)
            lines_out[member, :, step * BLOCK : step * BLOCK + width] = line[:, :width]
            line = line.astype(jnp.float32)
            partner = pltpu.roll(line, levels - 1, 0)
            products[member, step * levels : (step + 1) * levels, :] = (line * partner).astype(jnp.bfloat16)
        result = pltpu.make_async_copy(lines_out.at[member], grid_out.at[member], out_sems.at[member])
        result.start()
        results.append(result)
        if member == 0:
            copies[4].wait()
            copies[5].wait()
        reals, imags = [], []
        for part in range(parts):
            at = part * 2 * LANES
            sums = dot(products[member], inner[member, :, at : at + 2 * LANES], NN)
            real = jnp.zeros((levels, LANES), jnp.float32)
            imag = jnp.zeros((levels, LANES), jnp.float32)
            for step in range(BLOCKS):
                rows = slice(step * levels, (step + 1) * levels)
                cosine = outer_inv[member, step : step + 1, at : at + LANES]
                sine = outer_inv[member, step : step + 1, at + LANES : at + 2 * LANES]
                real += sums[rows, :LANES] * cosine + sums[rows, LANES:] * sine
                imag += sums[rows, LANES:] * cosine - sums[rows, :LANES] * sine
            reals.append(real)
            imags.append(imag)
        analysed = jnp.concatenate([jnp.concatenate(reals, axis=1), jnp.concatenate(imags, axis=1)], axis=0)
        back[pl.ds(member, slots, stride=row_count), :] = dot(
            analysed.T.astype(jnp.bfloat16), place[1], NN
        )
    pack_lines(back, sent, each)
    for result in results:
        result.wait()


def add_three_kernel(two, two_x, three, four, out, out_x):
    out[...] = (
        two[...].astype(jnp.float32) + three[0].astype(jnp.float32) + four[...].astype(jnp.float32)
    ).astype(jnp.bfloat16)
    out_x[...] = (two_x[...].astype(jnp.float32) + three[1].astype(jnp.float32)).astype(jnp.bfloat16)


def add_own_kernel(own, one, one_x, two, two_x, out):
    total = own[...]
    for landed in (one, one_x, two, two_x):
        total = total + landed[...].astype(jnp.float32)
    groups, cols, _ = out.shape
    for group in range(groups):
        out[group] = total[group * cols : (group + 1) * cols]


def shards(spectra, legendre, lat_weight, wave_of_slot, lat_of_row, lon_count):
    waves = lax.axis_size("wave")
    fields = lax.axis_size("field")
    zs = fields // 2
    wave_id = lax.axis_index("wave").astype(jnp.int32).reshape(1)
    field_id = lax.axis_index("field").astype(jnp.int32).reshape(1)
    slots, _, degrees, cols = spectra.shape
    band = legendre.shape[2]
    rows = 2 * band
    row_count = rows // waves
    all_slots = wave_of_slot.shape[0]
    levels = cols * fields
    each = row_count * slots
    coded = slots * 2 * cols

    like_cores = [list(range(0, fields, 2)), list(range(fields - 1, 0, -2))]

    def hop(x, by, cross=0):
        pairs = [
            (i, (2 * (i // 2 + side_of(i % 2) * by) + (i % 2 ^ cross)) % fields) for i in range(fields)
        ]
        return lax.ppermute(x, "field", pairs)

    def swap(x):
        return hop(x, 0, 1)

    def local(kernel, out_shape, name, micros, mebibytes=8, in_specs=None, out_specs=None, scratch=()):
        if in_specs is None:
            in_specs = pl.BlockSpec(memory_space=pltpu.VMEM)
        return pl.pallas_call(
            kernel,
            out_shape=out_shape,
            in_specs=in_specs,
            out_specs=jax.tree.map(lambda _: vmem(), out_shape) if out_specs is None else out_specs,
            scratch_shapes=list(scratch),
            compiler_params=params(mebibytes),
            cost_estimate=cost(micros),
            name=name,
        )

    row_table = jax.ShapeDtypeStruct((slots, rows, degrees), jnp.bfloat16)
    fourier_shape = jax.ShapeDtypeStruct((waves, 4, each // 4 * LANES), jnp.bfloat16)
    float_rows = pltpu.VMEM((waves * each, LANES), jnp.float32)

    own = jnp.transpose(spectra, (0, 1, 3, 2)).reshape(coded, degrees)
    gathered = lax.all_gather(own, "field", axis_index_groups=like_cores)
    gathered, legendre = lax.optimization_barrier((gathered, jnp.transpose(legendre, (0, 2, 1))))
    gathered_x = swap(gathered)
    table, chosen_x, south_x, live = local(
        functools.partial(own_rows_kernel, waves=waves, fields=fields),
        (
            row_table,
            jax.ShapeDtypeStruct((rows, LANES), jnp.bfloat16),
            jax.ShapeDtypeStruct((rows, LANES), jnp.float32),
            jax.ShapeDtypeStruct((-(-slots // 8) * 8, degrees), jnp.float32),
        ),
        "own_rows",
        2,
        in_specs=[smem(), smem(), hbm(), hbm(), hbm()],
        scratch=[
            pltpu.SMEM(wave_of_slot.shape, jnp.int32),
            pltpu.SMEM(lat_of_row.shape, jnp.int32),
            pltpu.VMEM((slots, band, degrees), jnp.bfloat16),
            pltpu.VMEM((2, rows, LANES), jnp.float32),
            pltpu.VMEM((2, rows, LANES), jnp.float32),
            pltpu.SemaphoreType.DMA((3,)),
        ],
    )(wave_id, field_id, in_hbm(wave_of_slot), in_hbm(lat_of_row), in_hbm(legendre))
    outgoing = local(
        legendre_forward_kernel, fourier_shape, "legendre_forward", 4, 16, in_specs=[vmem()] * 3, scratch=[float_rows]
    )(gathered, gathered_x, table)
    outgoing, lat_weight = lax.optimization_barrier((outgoing, lat_weight))
    arrived = lax.all_to_all(outgoing, "wave", split_axis=0, concat_axis=0, tiled=True)
    tables = (
        ((row_count, BLOCK, 2 * all_slots), jnp.bfloat16),
        ((row_count, 2 * all_slots, BLOCK), jnp.bfloat16),
        ((row_count, 16, 2 * all_slots), jnp.float32),
        ((row_count, 16, 2 * all_slots), jnp.float32),
        ((2, LANES, LANES), jnp.bfloat16),
        ((row_count, 8, LANES), jnp.float32),
    )
    tables_vmem = [pltpu.VMEM(shape, kind) for shape, kind in tables]
    prepared = local(
        functools.partial(fourier_tables_kernel, fields=fields, zs=zs),
        [pltpu.HBM(shape, kind) for shape, kind in tables],
        "fourier_tables",
        4,
        16,
        in_specs=[smem()] * 5 + [vmem()],
        out_specs=[hbm()] * 6,
        scratch=tables_vmem + [pltpu.SemaphoreType.DMA((6,))],
    )(
        wave_id, field_id, lat_of_row, lon_count, lat_weight,
        wave_of_slot.astype(jnp.float32).reshape(1, all_slots),
    )
    arrived, prepared = lax.optimization_barrier((arrived, prepared))
    prepared = [in_hbm(x) for x in prepared]

    grid_field, sent = local(
        fourier_kernel,
        (jax.ShapeDtypeStruct((row_count, levels, LONPAD), jnp.bfloat16), fourier_shape),
        "fourier",
        6,
        32,
        in_specs=[vmem()] + [hbm()] * 6,
        out_specs=(hbm(), vmem()),
        scratch=tables_vmem + [
            float_rows,
            float_rows,
            pltpu.VMEM((row_count, BLOCKS * levels, 2 * all_slots), jnp.bfloat16),
            pltpu.VMEM((row_count, BLOCKS * levels, BLOCK), jnp.bfloat16),
            pltpu.VMEM((row_count, levels, LONPAD), jnp.bfloat16),
            pltpu.SemaphoreType.DMA((6,)),
            pltpu.SemaphoreType.DMA((row_count,)),
        ],
    )(arrived, *prepared)

    sent, legendre = lax.optimization_barrier((sent, legendre))
    returned = lax.all_to_all(sent, "wave", split_axis=0, concat_axis=0, tiled=True)
    legendre_x = swap(legendre)

    table_x = local(
        partner_rows_kernel,
        row_table,
        "partner_rows",
        2,
        in_specs=[vmem(), vmem(), vmem(), hbm()],
        scratch=[pltpu.VMEM((slots, band, degrees), jnp.bfloat16), pltpu.SemaphoreType.DMA(())],
    )(chosen_x, south_x, live, in_hbm(legendre_x))
    returned, table_x = lax.optimization_barrier((returned, table_x))

    chunk = jax.ShapeDtypeStruct((coded, degrees), jnp.bfloat16)
    own, one, one_x, two, two_x, three, four = local(
        legendre_inverse_kernel,
        (
            jax.ShapeDtypeStruct((coded, degrees), jnp.float32),
            chunk, chunk, chunk, chunk, jax.ShapeDtypeStruct((2, coded, degrees), jnp.bfloat16), chunk,
        ),
        "legendre_inverse",
        2,
        16,
        in_specs=[vmem()] * 4,
        scratch=[float_rows, float_rows],
    )(returned, swap(returned), table, table_x)
    three, four = hop(three, -1), hop(four, -2)
    two, two_x = local(add_three_kernel, (chunk, chunk), "add_three", 1, in_specs=[vmem()] * 4)(
        two, two_x, three, four
    )
    one, one_x = hop(one, -1), hop(one_x, -1, 1)
    two, two_x = hop(two, -2), hop(two_x, -2, 1)
    total = local(
        add_own_kernel,
        jax.ShapeDtypeStruct((2 * slots, cols, degrees), jnp.float32),
        "add_own",
        1,
        in_specs=[vmem()] * 5,
    )(own, one, one_x, two, two_x)
    spectral = jnp.transpose(total.reshape(slots, 2, cols, degrees), (0, 1, 3, 2))
    return grid_field, spectral


def solution(mesh):
    in_specs = (P("wave", None, None, "field"), P("wave", None, "field"), P("field"), P(), P(), P())
    out_specs = (P(("wave", "field"), None, None), P("wave", None, None, "field"))
    return jax.shard_map(shards, mesh=mesh, in_specs=in_specs, out_specs=out_specs, check_vma=False)
```

```python
import functools
import math

import jax
import jax.numpy as jnp
from jax import lax
from jax.experimental import pallas as pl
from jax.experimental.pallas import tpu as pltpu
from jax.sharding import PartitionSpec as P

LONPAD = 3200
LANES = 128
BLOCK = 256
BLOCKS = -(-LONPAD // BLOCK)

NT = (((1,), (1,)), ((), ()))
NN = (((1,), (0,)), ((), ()))
TN = (((0,), (0,)), ((), ()))


def dot(a, b, dims):
    return lax.dot_general(a, b, dims, preferred_element_type=jnp.float32)


def params(mebibytes):
    return pltpu.CompilerParams(vmem_limit_bytes=mebibytes * 1024 * 1024)


def in_hbm(x):
    return pltpu.with_memory_space_constraint(x, pltpu.HBM)


def cost(micros):
    return pl.CostEstimate(flops=0, bytes_accessed=int(micros * 3.7e6), transcendentals=0)


def smem():
    return pl.BlockSpec(memory_space=pltpu.SMEM)


def vmem():
    return pl.BlockSpec(memory_space=pltpu.VMEM)


def hbm():
    return pl.BlockSpec(memory_space=pltpu.HBM)


def side_of(core):
    return 1 - 2 * core


def ordered_rows(chosen, south, live, legendre, out):
    slots, band, degrees = legendre.shape
    odd = (lax.broadcasted_iota(jnp.int32, (1, degrees), 1) & 1).astype(jnp.float32)
    sign = 1.0 - 2.0 * (south[:, :1] * odd)
    for slot in range(slots):
        table = dot(chosen[:, :band], legendre[slot], NN) * sign
        out[slot] = (table * live[slot : slot + 1, :]).astype(jnp.bfloat16)


def own_rows_kernel(
    wave_id, field_id, wave_of_slot, lat_of_row, legendre,
    out, chosen_x, south_x, live,
    slot_waves, row_lats, held, pick, south, sems, *, waves, fields,
):
    copies = [
        pltpu.make_async_copy(source, target, sems.at[i])
        for i, (source, target) in enumerate(((lat_of_row, row_lats), (wave_of_slot, slot_waves), (legendre, held)))
    ]
    for copy in copies:
        copy.start()
    slots, band, degrees = held.shape
    rows = out.shape[1]
    row_count = rows // waves
    half = row_lats.shape[0] // 2
    own, field = wave_id[0], field_id[0]
    lane = lax.broadcasted_iota(jnp.int32, (1, LANES), 1)
    copies[0].wait()
    for at in range(2):
        this = field ^ at
        for row in range(rows):
            member, wave = divmod(row, waves)
            lat = row_lats[(wave * fields + this) * row_count + member]
            is_south = lat >= half
            hemi = jnp.where(is_south, 2 * half - 1 - lat, lat) - this * band
            pick[at, row : row + 1, :] = (lane == hemi).astype(jnp.float32)
            south[at, row : row + 1, :] = jnp.broadcast_to(is_south.astype(jnp.float32), (1, LANES))
    chosen_x[...] = pick[1].astype(jnp.bfloat16)
    south_x[...] = south[1]
    offsets = lax.broadcasted_iota(jnp.int32, (1, degrees), 1)
    copies[1].wait()
    live[...] = jnp.zeros(live.shape, jnp.float32)
    for slot in range(slots):
        live[slot : slot + 1, :] = (offsets < degrees - slot_waves[own * slots + slot]).astype(jnp.float32)
    copies[2].wait()
    ordered_rows(pick[0].astype(jnp.bfloat16), south[0], live, held, out)


def partner_rows_kernel(chosen, south, live, legendre, out, held, sem):
    copy = pltpu.make_async_copy(legendre, held, sem)
    copy.start()
    copy.wait()
    ordered_rows(chosen[...], south[...], live, held, out)


def sin_cos(phase, period):
    inverse = 1.0 / period
    turns = (phase - jnp.floor(phase * inverse + 0.5) * period) * inverse
    quarter = jnp.floor(4.0 * turns + 0.5)
    w = (2.0 * math.pi) * (turns - 0.25 * quarter)
    w2 = w * w
    sine = w * (1.0 + w2 * (-1.0 / 6 + w2 * (1.0 / 120 + w2 * (-1.0 / 5040 + w2 * (1.0 / 362880)))))
    cosine = 1.0 + w2 * (-0.5 + w2 * (1.0 / 24 + w2 * (-1.0 / 720 + w2 * (1.0 / 40320))))
    size = jnp.abs(quarter)
    odd = size == 1.0
    flipped = size >= 2.0
    cos_out = jnp.where(odd, sine, cosine)
    sin_out = jnp.where(odd, cosine, sine)
    cos_out = jnp.where(flipped | (quarter == 1.0), -cos_out, cos_out)
    sin_out = jnp.where(flipped | (quarter == -1.0), -sin_out, sin_out)
    return cos_out, sin_out


def fourier_tables_kernel(
    wave_id, field_id, lat_of_row, lon_count, lat_weight, waves_row,
    inner_out, inner_t_out, outer_fwd_out, outer_inv_out, place_out, limits_out,
    inner, inner_t, outer_fwd, outer_inv, place, limits, sems, *, fields, zs,
):
    row_count = inner.shape[0]
    band = lat_weight.shape[0]
    half = lon_count.shape[0]
    slots = waves_row.shape[1]
    steps = outer_fwd.shape[1]
    wave, field = wave_id[0], field_id[0]
    for member in range(row_count):
        lat = lat_of_row[(wave * fields + field) * row_count + member]
        hemi = jnp.where(lat >= half, 2 * half - 1 - lat, lat)
        points = lon_count[hemi].astype(jnp.float32)
        period = jnp.broadcast_to(points, (1, LANES))
        limits[member] = jnp.broadcast_to(points, limits.shape[1:])
        weight = lat_weight[hemi - field * band] / jnp.sqrt(period)
        for part in range(slots // LANES):
            m = waves_row[:, part * LANES : (part + 1) * LANES]
            at = part * 2 * LANES
            x = lax.broadcasted_iota(jnp.int32, (BLOCK, LANES), 0).astype(jnp.float32)
            cosine, sine = sin_cos(x * m, period)
            both = jnp.concatenate([cosine, -sine], axis=1)
            inner[member, :, at : at + 2 * LANES] = both.astype(jnp.bfloat16)
            inner_t[member, at : at + 2 * LANES, :] = both.T.astype(jnp.bfloat16)
            x = (BLOCK * lax.broadcasted_iota(jnp.int32, (steps, LANES), 0)).astype(jnp.float32)
            cosine, sine = sin_cos(x * m, period)
            both = jnp.concatenate([cosine, sine], axis=1)
            outer_fwd[member, :, at : at + 2 * LANES] = both * (1.0 / math.sqrt(slots))
            outer_inv[member, :, at : at + 2 * LANES] = both * jnp.concatenate([weight, weight], axis=1)
    at = lax.broadcasted_iota(jnp.int32, (LANES, LANES), 1)
    core, chunk, part, low = (field & 1) ^ (at >> 6), (at >> 3) & 7, (at >> 2) & 1, at & 3
    away = (chunk + 1) >> 1
    cross = ((chunk & 1) ^ 1) & (chunk > 0).astype(jnp.int32)
    z = ((field >> 1) - side_of(core) * away + zs) & (zs - 1)
    row = lax.broadcasted_iota(jnp.int32, (LANES, LANES), 0)
    gathered_z = chunk + core * (zs - 1 - 2 * chunk)
    for way, shard in enumerate((2 * gathered_z + core, 2 * z + (core ^ cross))):
        place[way] = (row == part * 64 + shard * 4 + low).astype(jnp.bfloat16)
    results = (
        (inner, inner_out), (inner_t, inner_t_out), (outer_fwd, outer_fwd_out),
        (outer_inv, outer_inv_out), (place, place_out), (limits, limits_out),
    )
    copies = [pltpu.make_async_copy(source, target, sems.at[i]) for i, (source, target) in enumerate(results)]
    for copy in copies:
        copy.start()
    for copy in copies:
        copy.wait()


def unpack_lines(messages, held, each):
    for at in range(messages.shape[0]):
        message = messages[at].astype(jnp.float32)
        for group in range(each // 4):
            first = at * each + 4 * group
            held[first : first + 4, :] = message[:, group * LANES : (group + 1) * LANES]


def pack_lines(held, messages, each):
    for at in range(messages.shape[0]):
        groups = [held[at * each + 4 * group : at * each + 4 * group + 4, :] for group in range(each // 4)]
        messages[at] = jnp.concatenate(groups, axis=1).astype(jnp.bfloat16)


def legendre_forward_kernel(gathered, gathered_x, table, out, held):
    slots, rows, degrees = table.shape
    waves = out.shape[0]
    row_count = rows // waves
    each = slots * row_count
    for pair in range(slots // 2):
        at = pl.ds(16 * pair, 16)
        both = [source[z, at, :].astype(jnp.float32) for source in (gathered, gathered_x) for z in range(source.shape[0])]
        for half in range(2):
            slot = 2 * pair + half
            spec = jnp.concatenate([b[8 * half : 8 * half + 8] for b in both], axis=0).astype(jnp.bfloat16)
            sums = dot(table[slot], spec, NT)
            for member in range(row_count):
                held[pl.ds(slot * row_count + member, waves, stride=each), :] = sums[
                    waves * member : waves * (member + 1)
                ]
    pack_lines(held, out, each)


def legendre_inverse_kernel(
    arrived, swapped, table, table_swapped, own, one, one_x, two, two_x, three, four, held, held_swapped
):
    slots, rows, degrees = table.shape
    waves = arrived.shape[0]
    row_count = rows // waves
    each = slots * row_count
    unpack_lines(arrived, held, each)
    unpack_lines(swapped, held_swapped, each)

    def share(ref, slot, legendre, turn=0):
        weighted = jnp.concatenate(
            [ref[pl.ds(slot * row_count + member, waves, stride=each), :] for member in range(row_count)], axis=0
        )
        if turn:
            weighted = pltpu.roll(weighted, turn, 1)
        return dot(weighted[:, :64].astype(jnp.bfloat16), legendre[slot], TN)

    for pair in range(slots // 2):
        at = pl.ds(16 * pair, 16)
        sums = [
            share(held, slot, table) + share(held_swapped, slot, table_swapped, 64) for slot in (2 * pair, 2 * pair + 1)
        ]
        pieces = [jnp.concatenate([s[8 * chunk : 8 * chunk + 8] for s in sums], axis=0) for chunk in range(8)]
        own[at, :] = pieces[0]
        targets = (one, one_x, two, two_x, three.at[0], three.at[1], four)
        for target, piece in zip(targets, pieces[1:]):
            target[at, :] = piece.astype(jnp.bfloat16)


def fourier_kernel(
    arrived, inner_in, inner_t_in, outer_fwd_in, outer_inv_in, place_in, limits_in,
    grid_out, sent,
    inner, inner_t, outer_fwd, outer_inv, place, limits, held, back, turned, products, lines_out, sems, out_sems,
):
    inputs = (
        (place_in, place), (outer_fwd_in, outer_fwd), (limits_in, limits),
        (inner_t_in, inner_t), (inner_in, inner), (outer_inv_in, outer_inv),
    )
    copies = [pltpu.make_async_copy(source, target, sems.at[i]) for i, (source, target) in enumerate(inputs)]
    for copy in copies:
        copy.start()
    row_count = inner.shape[0]
    slots = held.shape[0] // row_count
    each = held.shape[0] // arrived.shape[0]
    parts = slots // LANES
    levels = grid_out.shape[1]
    unpack_lines(arrived, held, each)
    for copy in copies[:3]:
        copy.wait()
    column = lax.broadcasted_iota(jnp.int32, (1, BLOCK), 1).astype(jnp.float32)

    def rotate(member):
        lines = held[pl.ds(member, slots, stride=row_count), :].astype(jnp.bfloat16)
        coef = dot(place[0], lines, NT)
        for step in range(BLOCKS):
            rows = pl.ds(step * levels, levels)
            for part in range(parts):
                real = coef[:levels, part * LANES : (part + 1) * LANES]
                imag = coef[levels:, part * LANES : (part + 1) * LANES]
                at = part * 2 * LANES
                cosine = outer_fwd[member, step : step + 1, at : at + LANES]
                sine = outer_fwd[member, step : step + 1, at + LANES : at + 2 * LANES]
                turned[member, rows, at : at + LANES] = (real * cosine - imag * sine).astype(jnp.bfloat16)
                turned[member, rows, at + LANES : at + 2 * LANES] = (real * sine + imag * cosine).astype(jnp.bfloat16)

    def spread(member):
        return dot(turned[member], inner_t[member], NN)

    def multiply(member, values):
        points = jnp.concatenate([limits[member, :1, :]] * (BLOCK // LANES), axis=1)
        for step in range(BLOCKS):
            width = min(BLOCK, LONPAD - step * BLOCK)
            line = values[step * levels : (step + 1) * levels]
            line = jnp.where(column + step * BLOCK < points, line, 0.0).astype(jnp.bfloat16)
            lines_out[member, :, step * BLOCK : step * BLOCK + width] = line[:, :width]
            line = line.astype(jnp.float32)
            partner = pltpu.roll(line, levels - 1, 0)
            products[member, step * levels : (step + 1) * levels, :] = (line * partner).astype(jnp.bfloat16)
        result = pltpu.make_async_copy(lines_out.at[member], grid_out.at[member], out_sems.at[member])
        result.start()
        return result

    def analyse(member):
        return dot(products[member], inner[member], NN)

    def collect(member, sums):
        reals, imags = [], []
        for part in range(parts):
            at = part * 2 * LANES
            real = jnp.zeros((levels, LANES), jnp.float32)
            imag = jnp.zeros((levels, LANES), jnp.float32)
            for step in range(BLOCKS):
                rows = slice(step * levels, (step + 1) * levels)
                cosine = outer_inv[member, step : step + 1, at : at + LANES]
                sine = outer_inv[member, step : step + 1, at + LANES : at + 2 * LANES]
                even, odd = sums[rows, at : at + LANES], sums[rows, at + LANES : at + 2 * LANES]
                real += even * cosine + odd * sine
                imag += odd * cosine - even * sine
            reals.append(real)
            imags.append(imag)
        analysed = jnp.concatenate([jnp.concatenate(reals, axis=1), jnp.concatenate(imags, axis=1)], axis=0)
        back[pl.ds(member, slots, stride=row_count), :] = dot(analysed.T.astype(jnp.bfloat16), place[1], NN)

    rotate(0)
    copies[3].wait()
    copies[4].wait()
    copies[5].wait()
    values, sums, results = {0: spread(0)}, {}, []
    for member in range(row_count):
        if member + 1 < row_count:
            rotate(member + 1)
        if member > 0:
            sums[member - 1] = analyse(member - 1)
        results.append(multiply(member, values.pop(member)))
        if member + 1 < row_count:
            values[member + 1] = spread(member + 1)
        if member > 0:
            collect(member - 1, sums.pop(member - 1))
    collect(row_count - 1, analyse(row_count - 1))
    pack_lines(back, sent, each)
    for result in results:
        result.wait()


def add_three_kernel(two, two_x, three, four, out, out_x):
    out[...] = (
        two[...].astype(jnp.float32) + three[0].astype(jnp.float32) + four[...].astype(jnp.float32)
    ).astype(jnp.bfloat16)
    out_x[...] = (two_x[...].astype(jnp.float32) + three[1].astype(jnp.float32)).astype(jnp.bfloat16)


def add_own_kernel(own, one, one_x, two, two_x, out):
    total = own[...]
    for landed in (one, one_x, two, two_x):
        total = total + landed[...].astype(jnp.float32)
    groups, cols, _ = out.shape
    for group in range(groups):
        out[group] = total[group * cols : (group + 1) * cols]


def shards(spectra, legendre, lat_weight, wave_of_slot, lat_of_row, lon_count):
    waves = lax.axis_size("wave")
    fields = lax.axis_size("field")
    zs = fields // 2
    wave_id = lax.axis_index("wave").astype(jnp.int32).reshape(1)
    field_id = lax.axis_index("field").astype(jnp.int32).reshape(1)
    slots, _, degrees, cols = spectra.shape
    band = legendre.shape[2]
    rows = 2 * band
    row_count = rows // waves
    all_slots = wave_of_slot.shape[0]
    levels = cols * fields
    each = row_count * slots
    coded = slots * 2 * cols

    like_cores = [list(range(0, fields, 2)), list(range(fields - 1, 0, -2))]

    def hop(x, by, cross=0):
        pairs = [
            (i, (2 * (i // 2 + side_of(i % 2) * by) + (i % 2 ^ cross)) % fields) for i in range(fields)
        ]
        return lax.ppermute(x, "field", pairs)

    def swap(x):
        return hop(x, 0, 1)

    def local(kernel, out_shape, name, micros, mebibytes=8, in_specs=None, out_specs=None, scratch=()):
        if in_specs is None:
            in_specs = pl.BlockSpec(memory_space=pltpu.VMEM)
        return pl.pallas_call(
            kernel,
            out_shape=out_shape,
            in_specs=in_specs,
            out_specs=jax.tree.map(lambda _: vmem(), out_shape) if out_specs is None else out_specs,
            scratch_shapes=list(scratch),
            compiler_params=params(mebibytes),
            cost_estimate=cost(micros),
            name=name,
        )

    row_table = jax.ShapeDtypeStruct((slots, rows, degrees), jnp.bfloat16)
    fourier_shape = jax.ShapeDtypeStruct((waves, 4, each // 4 * LANES), jnp.bfloat16)
    float_rows = pltpu.VMEM((waves * each, LANES), jnp.float32)

    own = jnp.transpose(spectra, (0, 1, 3, 2)).reshape(coded, degrees)
    gathered = lax.all_gather(own, "field", axis_index_groups=like_cores)
    gathered, legendre = lax.optimization_barrier((gathered, jnp.transpose(legendre, (0, 2, 1))))
    gathered_x = swap(gathered)
    table, chosen_x, south_x, live = local(
        functools.partial(own_rows_kernel, waves=waves, fields=fields),
        (
            row_table,
            jax.ShapeDtypeStruct((rows, LANES), jnp.bfloat16),
            jax.ShapeDtypeStruct((rows, LANES), jnp.float32),
            jax.ShapeDtypeStruct((-(-slots // 8) * 8, degrees), jnp.float32),
        ),
        "own_rows",
        2,
        in_specs=[smem(), smem(), hbm(), hbm(), hbm()],
        scratch=[
            pltpu.SMEM(wave_of_slot.shape, jnp.int32),
            pltpu.SMEM(lat_of_row.shape, jnp.int32),
            pltpu.VMEM((slots, band, degrees), jnp.bfloat16),
            pltpu.VMEM((2, rows, LANES), jnp.float32),
            pltpu.VMEM((2, rows, LANES), jnp.float32),
            pltpu.SemaphoreType.DMA((3,)),
        ],
    )(wave_id, field_id, in_hbm(wave_of_slot), in_hbm(lat_of_row), in_hbm(legendre))
    outgoing = local(
        legendre_forward_kernel, fourier_shape, "legendre_forward", 4, 16, in_specs=[vmem()] * 3, scratch=[float_rows]
    )(gathered, gathered_x, table)
    outgoing, lat_weight = lax.optimization_barrier((outgoing, lat_weight))
    arrived = lax.all_to_all(outgoing, "wave", split_axis=0, concat_axis=0, tiled=True)
    tables = (
        ((row_count, BLOCK, 2 * all_slots), jnp.bfloat16),
        ((row_count, 2 * all_slots, BLOCK), jnp.bfloat16),
        ((row_count, 16, 2 * all_slots), jnp.float32),
        ((row_count, 16, 2 * all_slots), jnp.float32),
        ((2, LANES, LANES), jnp.bfloat16),
        ((row_count, 8, LANES), jnp.float32),
    )
    tables_vmem = [pltpu.VMEM(shape, kind) for shape, kind in tables]
    prepared = local(
        functools.partial(fourier_tables_kernel, fields=fields, zs=zs),
        [pltpu.HBM(shape, kind) for shape, kind in tables],
        "fourier_tables",
        4,
        16,
        in_specs=[smem()] * 5 + [vmem()],
        out_specs=[hbm()] * 6,
        scratch=tables_vmem + [pltpu.SemaphoreType.DMA((6,))],
    )(
        wave_id, field_id, lat_of_row, lon_count, lat_weight,
        wave_of_slot.astype(jnp.float32).reshape(1, all_slots),
    )
    arrived, prepared = lax.optimization_barrier((arrived, prepared))
    prepared = [in_hbm(x) for x in prepared]

    grid_field, sent = local(
        fourier_kernel,
        (jax.ShapeDtypeStruct((row_count, levels, LONPAD), jnp.bfloat16), fourier_shape),
        "fourier",
        6,
        32,
        in_specs=[vmem()] + [hbm()] * 6,
        out_specs=(hbm(), vmem()),
        scratch=tables_vmem + [
            float_rows,
            float_rows,
            pltpu.VMEM((row_count, BLOCKS * levels, 2 * all_slots), jnp.bfloat16),
            pltpu.VMEM((row_count, BLOCKS * levels, BLOCK), jnp.bfloat16),
            pltpu.VMEM((row_count, levels, LONPAD), jnp.bfloat16),
            pltpu.SemaphoreType.DMA((6,)),
            pltpu.SemaphoreType.DMA((row_count,)),
        ],
    )(arrived, *prepared)

    sent, legendre = lax.optimization_barrier((sent, legendre))
    returned = lax.all_to_all(sent, "wave", split_axis=0, concat_axis=0, tiled=True)
    legendre_x = swap(legendre)

    table_x = local(
        partner_rows_kernel,
        row_table,
        "partner_rows",
        2,
        in_specs=[vmem(), vmem(), vmem(), hbm()],
        scratch=[pltpu.VMEM((slots, band, degrees), jnp.bfloat16), pltpu.SemaphoreType.DMA(())],
    )(chosen_x, south_x, live, in_hbm(legendre_x))
    returned, table_x = lax.optimization_barrier((returned, table_x))

    chunk = jax.ShapeDtypeStruct((coded, degrees), jnp.bfloat16)
    own, one, one_x, two, two_x, three, four = local(
        legendre_inverse_kernel,
        (
            jax.ShapeDtypeStruct((coded, degrees), jnp.float32),
            chunk, chunk, chunk, chunk, jax.ShapeDtypeStruct((2, coded, degrees), jnp.bfloat16), chunk,
        ),
        "legendre_inverse",
        2,
        16,
        in_specs=[vmem()] * 4,
        scratch=[float_rows, float_rows],
    )(returned, swap(returned), table, table_x)
    three, four = hop(three, -1), hop(four, -2)
    two, two_x = local(add_three_kernel, (chunk, chunk), "add_three", 1, in_specs=[vmem()] * 4)(
        two, two_x, three, four
    )
    one, one_x = hop(one, -1), hop(one_x, -1, 1)
    two, two_x = hop(two, -2), hop(two_x, -2, 1)
    total = local(
        add_own_kernel,
        jax.ShapeDtypeStruct((2 * slots, cols, degrees), jnp.float32),
        "add_own",
        1,
        in_specs=[vmem()] * 5,
    )(own, one, one_x, two, two_x)
    spectral = jnp.transpose(total.reshape(slots, 2, cols, degrees), (0, 1, 3, 2))
    return grid_field, spectral


def solution(mesh):
    in_specs = (P("wave", None, None, "field"), P("wave", None, "field"), P("field"), P(), P(), P())
    out_specs = (P(("wave", "field"), None, None), P("wave", None, None, "field"))
    return jax.shard_map(shards, mesh=mesh, in_specs=in_specs, out_specs=out_specs, check_vma=False)
```

```python
import functools
import math

import jax
import jax.numpy as jnp
from jax import lax
from jax.experimental import pallas as pl
from jax.experimental.pallas import tpu as pltpu
from jax.sharding import PartitionSpec as P

LONPAD = 3200
LANES = 128
BLOCK = 256
BLOCKS = -(-LONPAD // BLOCK)

NT = (((1,), (1,)), ((), ()))
NN = (((1,), (0,)), ((), ()))
TN = (((0,), (0,)), ((), ()))


def dot(a, b, dims):
    return lax.dot_general(a, b, dims, preferred_element_type=jnp.float32)


def params(mebibytes):
    return pltpu.CompilerParams(vmem_limit_bytes=mebibytes * 1024 * 1024)


def in_hbm(x):
    return pltpu.with_memory_space_constraint(x, pltpu.HBM)


def cost(micros):
    return pl.CostEstimate(flops=0, bytes_accessed=int(micros * 3.7e6), transcendentals=0)


def smem():
    return pl.BlockSpec(memory_space=pltpu.SMEM)


def vmem():
    return pl.BlockSpec(memory_space=pltpu.VMEM)


def hbm():
    return pl.BlockSpec(memory_space=pltpu.HBM)


def side_of(core):
    return 1 - 2 * core


def legendre_rows_kernel(
    wave_id, field_id, wave_of_slot, lat_of_row, legendre, out,
    slot_waves, row_lats, held, pick, south, sems, *, waves, fields,
):
    sources = ((lat_of_row, row_lats), (wave_of_slot, slot_waves), (legendre, held))
    copies = [pltpu.make_async_copy(source, target, sems.at[i]) for i, (source, target) in enumerate(sources)]
    for copy in copies:
        copy.start()
    slots, band, degrees = held.shape
    rows = out.shape[1]
    row_count = rows // waves
    half = row_lats.shape[0] // 2
    own, field = wave_id[0], field_id[0]
    lane = lax.broadcasted_iota(jnp.int32, (1, LANES), 1)
    copies[0].wait()
    for row in range(rows):
        member, wave = divmod(row, waves)
        lat = row_lats[(wave * fields + field) * row_count + member]
        is_south = lat >= half
        hemi = jnp.where(is_south, 2 * half - 1 - lat, lat) - field * band
        pick[row : row + 1, :] = (lane == hemi).astype(jnp.float32)
        south[row : row + 1, :] = jnp.broadcast_to(is_south.astype(jnp.float32), (1, LANES))
    copies[1].wait()
    copies[2].wait()
    offsets = lax.broadcasted_iota(jnp.int32, (1, degrees), 1)
    sign = 1.0 - 2.0 * (south[:, :1] * (offsets & 1).astype(jnp.float32))
    chosen = pick[:, :band].astype(jnp.bfloat16)
    for slot in range(slots):
        live = offsets < degrees - slot_waves[own * slots + slot]
        out[slot] = jnp.where(live, dot(chosen, held[slot], NN) * sign, 0.0).astype(jnp.bfloat16)


def sin_cos(phase, period):
    inverse = 1.0 / period
    turns = (phase - jnp.floor(phase * inverse + 0.5) * period) * inverse
    quarter = jnp.floor(4.0 * turns + 0.5)
    w = (2.0 * math.pi) * (turns - 0.25 * quarter)
    w2 = w * w
    sine = w * (1.0 + w2 * (-1.0 / 6 + w2 * (1.0 / 120 + w2 * (-1.0 / 5040 + w2 * (1.0 / 362880)))))
    cosine = 1.0 + w2 * (-0.5 + w2 * (1.0 / 24 + w2 * (-1.0 / 720 + w2 * (1.0 / 40320))))
    size = jnp.abs(quarter)
    odd = size == 1.0
    flipped = size >= 2.0
    cos_out = jnp.where(odd, sine, cosine)
    sin_out = jnp.where(odd, cosine, sine)
    cos_out = jnp.where(flipped | (quarter == 1.0), -cos_out, cos_out)
    sin_out = jnp.where(flipped | (quarter == -1.0), -sin_out, sin_out)
    return cos_out, sin_out


def fourier_tables_kernel(
    wave_id, field_id, lat_of_row, lon_count, lat_weight, waves_row,
    inner_out, inner_t_out, outer_fwd_out, outer_inv_out, place_out, limits_out,
    inner, inner_t, outer_fwd, outer_inv, place, limits, sems, *, fields, zs,
):
    row_count = inner.shape[0]
    band = lat_weight.shape[0]
    half = lon_count.shape[0]
    slots = waves_row.shape[1]
    steps = outer_fwd.shape[1]
    wave, field = wave_id[0], field_id[0]
    for member in range(row_count):
        lat = lat_of_row[(wave * fields + field) * row_count + member]
        hemi = jnp.where(lat >= half, 2 * half - 1 - lat, lat)
        points = lon_count[hemi].astype(jnp.float32)
        period = jnp.broadcast_to(points, (1, LANES))
        limits[member] = jnp.broadcast_to(points, limits.shape[1:])
        weight = lat_weight[hemi - field * band] / jnp.sqrt(period)
        for part in range(slots // LANES):
            m = waves_row[:, part * LANES : (part + 1) * LANES]
            at = part * 2 * LANES
            x = lax.broadcasted_iota(jnp.int32, (BLOCK, LANES), 0).astype(jnp.float32)
            cosine, sine = sin_cos(x * m, period)
            both = jnp.concatenate([cosine, -sine], axis=1)
            inner[member, :, at : at + 2 * LANES] = both.astype(jnp.bfloat16)
            inner_t[member, at : at + 2 * LANES, :] = both.T.astype(jnp.bfloat16)
            x = (BLOCK * lax.broadcasted_iota(jnp.int32, (steps, LANES), 0)).astype(jnp.float32)
            cosine, sine = sin_cos(x * m, period)
            both = jnp.concatenate([cosine, sine], axis=1)
            outer_fwd[member, :, at : at + 2 * LANES] = both * (1.0 / math.sqrt(slots))
            outer_inv[member, :, at : at + 2 * LANES] = both * jnp.concatenate([weight, weight], axis=1)
    at = lax.broadcasted_iota(jnp.int32, (LANES, LANES), 1)
    core, chunk, part, low = (field & 1) ^ (at >> 6), (at >> 3) & 7, (at >> 2) & 1, at & 3
    away = (chunk + 1) >> 1
    cross = ((chunk & 1) ^ 1) & (chunk > 0).astype(jnp.int32)
    z = ((field >> 1) - side_of(core) * away + zs) & (zs - 1)
    row = lax.broadcasted_iota(jnp.int32, (LANES, LANES), 0)
    gathered_z = chunk + core * (zs - 1 - 2 * chunk)
    for way, shard in enumerate((2 * gathered_z + core, 2 * z + (core ^ cross))):
        place[way] = (row == part * 64 + shard * 4 + low).astype(jnp.bfloat16)
    results = (
        (inner, inner_out), (inner_t, inner_t_out), (outer_fwd, outer_fwd_out),
        (outer_inv, outer_inv_out), (place, place_out), (limits, limits_out),
    )
    copies = [pltpu.make_async_copy(source, target, sems.at[i]) for i, (source, target) in enumerate(results)]
    for copy in copies:
        copy.start()
    for copy in copies:
        copy.wait()


def unpack_lines(messages, held, each):
    for at in range(messages.shape[0]):
        held[at * each : (at + 1) * each, :] = messages[at].astype(jnp.float32)


def pack_lines(held, messages, each):
    for at in range(messages.shape[0]):
        messages[at] = held[at * each : (at + 1) * each, :].astype(jnp.bfloat16)


def legendre_forward_kernel(gathered, gathered_x, table, out, held):
    slots, rows, degrees = table.shape
    waves = out.shape[0]
    row_count = rows // waves
    each = slots * row_count
    for pair in range(slots // 2):
        at = pl.ds(16 * pair, 16)
        both = [source[z, at, :].astype(jnp.float32) for source in (gathered, gathered_x) for z in range(source.shape[0])]
        for half in range(2):
            slot = 2 * pair + half
            spec = jnp.concatenate([b[8 * half : 8 * half + 8] for b in both], axis=0).astype(jnp.bfloat16)
            sums = dot(table[slot], spec, NT)
            for member in range(row_count):
                held[pl.ds(slot * row_count + member, waves, stride=each), :] = sums[
                    waves * member : waves * (member + 1)
                ]
    pack_lines(held, out, each)


def legendre_inverse_kernel(
    arrived, swapped, table, table_swapped, own, one, one_x, two, two_x, three, four, held, held_swapped
):
    slots, rows, degrees = table.shape
    waves = arrived.shape[0]
    row_count = rows // waves
    each = slots * row_count
    unpack_lines(arrived, held, each)
    unpack_lines(swapped, held_swapped, each)

    def share(ref, slot, legendre, turn=0):
        weighted = jnp.concatenate(
            [ref[pl.ds(slot * row_count + member, waves, stride=each), :] for member in range(row_count)], axis=0
        )
        if turn:
            weighted = pltpu.roll(weighted, turn, 1)
        return dot(weighted[:, :64].astype(jnp.bfloat16), legendre[slot], TN)

    for pair in range(slots // 2):
        at = pl.ds(16 * pair, 16)
        sums = [
            share(held, slot, table) + share(held_swapped, slot, table_swapped, 64) for slot in (2 * pair, 2 * pair + 1)
        ]
        pieces = [jnp.concatenate([s[8 * chunk : 8 * chunk + 8] for s in sums], axis=0) for chunk in range(8)]
        own[at, :] = pieces[0]
        targets = (one, one_x, two, two_x, three.at[0], three.at[1], four)
        for target, piece in zip(targets, pieces[1:]):
            target[at, :] = piece.astype(jnp.bfloat16)


def fourier_kernel(
    arrived, inner_in, inner_t_in, outer_fwd_in, outer_inv_in, place_in, limits_in,
    grid_out, sent,
    inner, inner_t, outer_fwd, outer_inv, place, limits, held, back, turned, products, lines_out, sems, out_sems,
):
    inputs = (
        (place_in, place), (outer_fwd_in, outer_fwd), (limits_in, limits),
        (inner_t_in, inner_t), (inner_in, inner), (outer_inv_in, outer_inv),
    )
    copies = [pltpu.make_async_copy(source, target, sems.at[i]) for i, (source, target) in enumerate(inputs)]
    for copy in copies:
        copy.start()
    row_count = inner.shape[0]
    slots = held.shape[0] // row_count
    each = held.shape[0] // arrived.shape[0]
    parts = slots // LANES
    levels = grid_out.shape[1]
    unpack_lines(arrived, held, each)
    for copy in copies[:3]:
        copy.wait()
    column = lax.broadcasted_iota(jnp.int32, (1, BLOCK), 1).astype(jnp.float32)

    def rotate(member):
        lines = held[pl.ds(member, slots, stride=row_count), :].astype(jnp.bfloat16)
        coef = dot(place[0], lines, NT)
        for step in range(BLOCKS):
            rows = pl.ds(step * levels, levels)
            for part in range(parts):
                real = coef[:levels, part * LANES : (part + 1) * LANES]
                imag = coef[levels:, part * LANES : (part + 1) * LANES]
                at = part * 2 * LANES
                cosine = outer_fwd[member, step : step + 1, at : at + LANES]
                sine = outer_fwd[member, step : step + 1, at + LANES : at + 2 * LANES]
                turned[member, rows, at : at + LANES] = (real * cosine - imag * sine).astype(jnp.bfloat16)
                turned[member, rows, at + LANES : at + 2 * LANES] = (real * sine + imag * cosine).astype(jnp.bfloat16)

    def spread(member):
        return dot(turned[member], inner_t[member], NN)

    def multiply(member, values):
        points = jnp.concatenate([limits[member, :1, :]] * (BLOCK // LANES), axis=1)
        for step in range(BLOCKS):
            width = min(BLOCK, LONPAD - step * BLOCK)
            line = values[step * levels : (step + 1) * levels]
            line = jnp.where(column + step * BLOCK < points, line, 0.0).astype(jnp.bfloat16)
            lines_out[member, :, step * BLOCK : step * BLOCK + width] = line[:, :width]
            line = line.astype(jnp.float32)
            partner = pltpu.roll(line, levels - 1, 0)
            products[member, step * levels : (step + 1) * levels, :] = (line * partner).astype(jnp.bfloat16)
        result = pltpu.make_async_copy(lines_out.at[member], grid_out.at[member], out_sems.at[member])
        result.start()
        return result

    def analyse(member):
        return dot(products[member], inner[member], NN)

    def collect(member, sums):
        reals, imags = [], []
        for part in range(parts):
            at = part * 2 * LANES
            real = jnp.zeros((levels, LANES), jnp.float32)
            imag = jnp.zeros((levels, LANES), jnp.float32)
            for step in range(BLOCKS):
                rows = slice(step * levels, (step + 1) * levels)
                cosine = outer_inv[member, step : step + 1, at : at + LANES]
                sine = outer_inv[member, step : step + 1, at + LANES : at + 2 * LANES]
                even, odd = sums[rows, at : at + LANES], sums[rows, at + LANES : at + 2 * LANES]
                real += even * cosine + odd * sine
                imag += odd * cosine - even * sine
            reals.append(real)
            imags.append(imag)
        analysed = jnp.concatenate([jnp.concatenate(reals, axis=1), jnp.concatenate(imags, axis=1)], axis=0)
        back[pl.ds(member, slots, stride=row_count), :] = dot(analysed.T.astype(jnp.bfloat16), place[1], NN)

    rotate(0)
    copies[3].wait()
    copies[4].wait()
    copies[5].wait()
    values, sums, results = {0: spread(0)}, {}, []
    for member in range(row_count):
        if member + 1 < row_count:
            rotate(member + 1)
        if member > 0:
            sums[member - 1] = analyse(member - 1)
        results.append(multiply(member, values.pop(member)))
        if member + 1 < row_count:
            values[member + 1] = spread(member + 1)
        if member > 0:
            collect(member - 1, sums.pop(member - 1))
    collect(row_count - 1, analyse(row_count - 1))
    pack_lines(back, sent, each)
    for result in results:
        result.wait()


def add_three_kernel(two, two_x, three, four, out, out_x):
    out[...] = (
        two[...].astype(jnp.float32) + three[0].astype(jnp.float32) + four[...].astype(jnp.float32)
    ).astype(jnp.bfloat16)
    out_x[...] = (two_x[...].astype(jnp.float32) + three[1].astype(jnp.float32)).astype(jnp.bfloat16)


def add_own_kernel(own, one, one_x, two, two_x, out):
    total = own[...]
    for landed in (one, one_x, two, two_x):
        total = total + landed[...].astype(jnp.float32)
    groups, cols, _ = out.shape
    for group in range(groups):
        out[group] = total[group * cols : (group + 1) * cols]


def shards(spectra, legendre, lat_weight, wave_of_slot, lat_of_row, lon_count):
    waves = lax.axis_size("wave")
    fields = lax.axis_size("field")
    zs = fields // 2
    wave_id = lax.axis_index("wave").astype(jnp.int32).reshape(1)
    field_id = lax.axis_index("field").astype(jnp.int32).reshape(1)
    slots, _, degrees, cols = spectra.shape
    band = legendre.shape[2]
    rows = 2 * band
    row_count = rows // waves
    all_slots = wave_of_slot.shape[0]
    levels = cols * fields
    each = row_count * slots
    coded = slots * 2 * cols

    like_cores = [list(range(0, fields, 2)), list(range(fields - 1, 0, -2))]

    def hop(x, by, cross=0):
        pairs = [
            (i, (2 * (i // 2 + side_of(i % 2) * by) + (i % 2 ^ cross)) % fields) for i in range(fields)
        ]
        return lax.ppermute(x, "field", pairs)

    def swap(x):
        return hop(x, 0, 1)

    def local(kernel, out_shape, name, micros, mebibytes=8, in_specs=None, out_specs=None, scratch=()):
        if in_specs is None:
            in_specs = pl.BlockSpec(memory_space=pltpu.VMEM)
        return pl.pallas_call(
            kernel,
            out_shape=out_shape,
            in_specs=in_specs,
            out_specs=jax.tree.map(lambda _: vmem(), out_shape) if out_specs is None else out_specs,
            scratch_shapes=list(scratch),
            compiler_params=params(mebibytes),
            cost_estimate=cost(micros),
            name=name,
        )

    row_table = jax.ShapeDtypeStruct((slots, rows, degrees), jnp.bfloat16)
    fourier_shape = jax.ShapeDtypeStruct((waves, each, LANES), jnp.bfloat16)
    float_rows = pltpu.VMEM((waves * each, LANES), jnp.float32)

    own = jnp.transpose(spectra, (0, 1, 3, 2)).reshape(coded, degrees)
    gathered = lax.all_gather(own, "field", axis_index_groups=like_cores)
    gathered, legendre = lax.optimization_barrier((gathered, jnp.transpose(legendre, (0, 2, 1))))
    gathered_x = swap(gathered)

    def ordered_rows(values, band_of):
        return local(
            functools.partial(legendre_rows_kernel, waves=waves, fields=fields),
            row_table,
            "legendre_rows",
            2,
            in_specs=[smem(), smem(), hbm(), hbm(), hbm()],
            scratch=[
                pltpu.SMEM(wave_of_slot.shape, jnp.int32),
                pltpu.SMEM(lat_of_row.shape, jnp.int32),
                pltpu.VMEM((slots, band, degrees), jnp.bfloat16),
                pltpu.VMEM((rows, LANES), jnp.float32),
                pltpu.VMEM((rows, LANES), jnp.float32),
                pltpu.SemaphoreType.DMA((3,)),
            ],
        )(wave_id, band_of, in_hbm(wave_of_slot), in_hbm(lat_of_row), in_hbm(values))

    table = ordered_rows(legendre, field_id)
    outgoing = local(
        legendre_forward_kernel, fourier_shape, "legendre_forward", 4, 16, in_specs=[vmem()] * 3, scratch=[float_rows]
    )(gathered, gathered_x, table)
    outgoing, lat_weight = lax.optimization_barrier((outgoing, lat_weight))
    arrived = lax.all_to_all(outgoing, "wave", split_axis=0, concat_axis=0, tiled=True)
    tables = (
        ((row_count, BLOCK, 2 * all_slots), jnp.bfloat16),
        ((row_count, 2 * all_slots, BLOCK), jnp.bfloat16),
        ((row_count, 16, 2 * all_slots), jnp.float32),
        ((row_count, 16, 2 * all_slots), jnp.float32),
        ((2, LANES, LANES), jnp.bfloat16),
        ((row_count, 8, LANES), jnp.float32),
    )
    tables_vmem = [pltpu.VMEM(shape, kind) for shape, kind in tables]
    prepared = local(
        functools.partial(fourier_tables_kernel, fields=fields, zs=zs),
        [pltpu.HBM(shape, kind) for shape, kind in tables],
        "fourier_tables",
        4,
        16,
        in_specs=[smem()] * 5 + [vmem()],
        out_specs=[hbm()] * 6,
        scratch=tables_vmem + [pltpu.SemaphoreType.DMA((6,))],
    )(
        wave_id, field_id, lat_of_row, lon_count, lat_weight,
        wave_of_slot.astype(jnp.float32).reshape(1, all_slots),
    )
    arrived, prepared = lax.optimization_barrier((arrived, prepared))
    prepared = [in_hbm(x) for x in prepared]

    grid_field, sent = local(
        fourier_kernel,
        (jax.ShapeDtypeStruct((row_count, levels, LONPAD), jnp.bfloat16), fourier_shape),
        "fourier",
        6,
        32,
        in_specs=[vmem()] + [hbm()] * 6,
        out_specs=(hbm(), vmem()),
        scratch=tables_vmem + [
            float_rows,
            float_rows,
            pltpu.VMEM((row_count, BLOCKS * levels, 2 * all_slots), jnp.bfloat16),
            pltpu.VMEM((row_count, BLOCKS * levels, BLOCK), jnp.bfloat16),
            pltpu.VMEM((row_count, levels, LONPAD), jnp.bfloat16),
            pltpu.SemaphoreType.DMA((6,)),
            pltpu.SemaphoreType.DMA((row_count,)),
        ],
    )(arrived, *prepared)

    sent, legendre = lax.optimization_barrier((sent, legendre))
    returned = lax.all_to_all(sent, "wave", split_axis=0, concat_axis=0, tiled=True)
    legendre_x = swap(legendre)

    table_x = ordered_rows(legendre_x, field_id ^ 1)
    returned, table_x = lax.optimization_barrier((returned, table_x))

    chunk = jax.ShapeDtypeStruct((coded, degrees), jnp.bfloat16)
    own, one, one_x, two, two_x, three, four = local(
        legendre_inverse_kernel,
        (
            jax.ShapeDtypeStruct((coded, degrees), jnp.float32),
            chunk, chunk, chunk, chunk, jax.ShapeDtypeStruct((2, coded, degrees), jnp.bfloat16), chunk,
        ),
        "legendre_inverse",
        2,
        16,
        in_specs=[vmem()] * 4,
        scratch=[float_rows, float_rows],
    )(returned, swap(returned), table, table_x)
    three, four = hop(three, -1), hop(four, -2)
    two, two_x = local(add_three_kernel, (chunk, chunk), "add_three", 1, in_specs=[vmem()] * 4)(
        two, two_x, three, four
    )
    one, one_x = hop(one, -1), hop(one_x, -1, 1)
    two, two_x = hop(two, -2), hop(two_x, -2, 1)
    total = local(
        add_own_kernel,
        jax.ShapeDtypeStruct((2 * slots, cols, degrees), jnp.float32),
        "add_own",
        1,
        in_specs=[vmem()] * 5,
    )(own, one, one_x, two, two_x)
    spectral = jnp.transpose(total.reshape(slots, 2, cols, degrees), (0, 1, 3, 2))
    return grid_field, spectral


def solution(mesh):
    in_specs = (P("wave", None, None, "field"), P("wave", None, "field"), P("field"), P(), P(), P())
    out_specs = (P(("wave", "field"), None, None), P("wave", None, None, "field"))
    return jax.shard_map(shards, mesh=mesh, in_specs=in_specs, out_specs=out_specs, check_vma=False)
```

```python
import functools
import math

import jax
import jax.numpy as jnp
from jax import lax
from jax.experimental import pallas as pl
from jax.experimental.pallas import tpu as pltpu
from jax.sharding import PartitionSpec as P

LONPAD = 3200
LANES = 128
BLOCK = 256
BLOCKS = -(-LONPAD // BLOCK)

NT = (((1,), (1,)), ((), ()))
NN = (((1,), (0,)), ((), ()))
TN = (((0,), (0,)), ((), ()))


def dot(a, b, dims):
    return lax.dot_general(a, b, dims, preferred_element_type=jnp.float32)


def params(mebibytes):
    return pltpu.CompilerParams(vmem_limit_bytes=mebibytes * 1024 * 1024)


def in_hbm(x):
    return pltpu.with_memory_space_constraint(x, pltpu.HBM)


def cost(micros):
    return pl.CostEstimate(flops=0, bytes_accessed=int(micros * 3.7e6), transcendentals=0)


def smem():
    return pl.BlockSpec(memory_space=pltpu.SMEM)


def vmem():
    return pl.BlockSpec(memory_space=pltpu.VMEM)


def hbm():
    return pl.BlockSpec(memory_space=pltpu.HBM)


def side_of(core):
    return 1 - 2 * core


def legendre_rows_kernel(
    wave_id, field_id, wave_of_slot, lat_of_row, legendre, out,
    slot_waves, row_lats, held, pick, south, sems, *, waves, fields,
):
    sources = ((lat_of_row, row_lats), (wave_of_slot, slot_waves), (legendre, held))
    copies = [pltpu.make_async_copy(source, target, sems.at[i]) for i, (source, target) in enumerate(sources)]
    for copy in copies:
        copy.start()
    slots, band, degrees = held.shape
    rows = out.shape[1]
    row_count = rows // waves
    half = row_lats.shape[0] // 2
    own, field = wave_id[0], field_id[0]
    lane = lax.broadcasted_iota(jnp.int32, (1, LANES), 1)
    copies[0].wait()
    for row in range(rows):
        member, wave = divmod(row, waves)
        lat = row_lats[(wave * fields + field) * row_count + member]
        is_south = lat >= half
        hemi = jnp.where(is_south, 2 * half - 1 - lat, lat) - field * band
        pick[row : row + 1, :] = (lane == hemi).astype(jnp.float32)
        south[row : row + 1, :] = jnp.broadcast_to(is_south.astype(jnp.float32), (1, LANES))
    copies[1].wait()
    copies[2].wait()
    offsets = lax.broadcasted_iota(jnp.int32, (1, degrees), 1)
    sign = 1.0 - 2.0 * (south[:, :1] * (offsets & 1).astype(jnp.float32))
    chosen = pick[:, :band].astype(jnp.bfloat16)
    for slot in range(slots):
        live = offsets < degrees - slot_waves[own * slots + slot]
        out[slot] = jnp.where(live, dot(chosen, held[slot], NN) * sign, 0.0).astype(jnp.bfloat16)


def sin_cos(phase, period):
    inverse = 1.0 / period
    turns = (phase - jnp.floor(phase * inverse + 0.5) * period) * inverse
    quarter = jnp.floor(4.0 * turns + 0.5)
    w = (2.0 * math.pi) * (turns - 0.25 * quarter)
    w2 = w * w
    sine = w * (1.0 + w2 * (-1.0 / 6 + w2 * (1.0 / 120 + w2 * (-1.0 / 5040 + w2 * (1.0 / 362880)))))
    cosine = 1.0 + w2 * (-0.5 + w2 * (1.0 / 24 + w2 * (-1.0 / 720 + w2 * (1.0 / 40320))))
    size = jnp.abs(quarter)
    odd = size == 1.0
    flipped = size >= 2.0
    cos_out = jnp.where(odd, sine, cosine)
    sin_out = jnp.where(odd, cosine, sine)
    cos_out = jnp.where(flipped | (quarter == 1.0), -cos_out, cos_out)
    sin_out = jnp.where(flipped | (quarter == -1.0), -sin_out, sin_out)
    return cos_out, sin_out


def fourier_tables_kernel(
    wave_id, field_id, lat_of_row, lon_count, lat_weight, waves_row,
    inner_out, inner_t_out, outer_fwd_out, outer_inv_out, place_out, limits_out,
    inner, inner_t, outer_fwd, outer_inv, place, limits, sems, *, fields, zs,
):
    row_count = inner.shape[0]
    band = lat_weight.shape[0]
    half = lon_count.shape[0]
    slots = waves_row.shape[1]
    steps = outer_fwd.shape[1]
    wave, field = wave_id[0], field_id[0]
    for member in range(row_count):
        lat = lat_of_row[(wave * fields + field) * row_count + member]
        hemi = jnp.where(lat >= half, 2 * half - 1 - lat, lat)
        points = lon_count[hemi].astype(jnp.float32)
        period = jnp.broadcast_to(points, (1, LANES))
        limits[member] = jnp.broadcast_to(points, limits.shape[1:])
        weight = lat_weight[hemi - field * band] / jnp.sqrt(period)
        for part in range(slots // LANES):
            m = waves_row[:, part * LANES : (part + 1) * LANES]
            at = part * 2 * LANES
            x = lax.broadcasted_iota(jnp.int32, (BLOCK, LANES), 0).astype(jnp.float32)
            cosine, sine = sin_cos(x * m, period)
            both = jnp.concatenate([cosine, -sine], axis=1)
            inner[member, :, at : at + 2 * LANES] = both.astype(jnp.bfloat16)
            inner_t[member, at : at + 2 * LANES, :] = both.T.astype(jnp.bfloat16)
            x = (BLOCK * lax.broadcasted_iota(jnp.int32, (steps, LANES), 0)).astype(jnp.float32)
            cosine, sine = sin_cos(x * m, period)
            both = jnp.concatenate([cosine, sine], axis=1)
            outer_fwd[member, :, at : at + 2 * LANES] = both * (1.0 / math.sqrt(slots))
            outer_inv[member, :, at : at + 2 * LANES] = both * jnp.concatenate([weight, weight], axis=1)
    at = lax.broadcasted_iota(jnp.int32, (LANES, LANES), 1)
    core, chunk, part, low = (field & 1) ^ (at >> 6), (at >> 3) & 7, (at >> 2) & 1, at & 3
    away = (chunk + 1) >> 1
    cross = ((chunk & 1) ^ 1) & (chunk > 0).astype(jnp.int32)
    z = ((field >> 1) - side_of(core) * away + zs) & (zs - 1)
    row = lax.broadcasted_iota(jnp.int32, (LANES, LANES), 0)
    gathered_z = chunk + core * (zs - 1 - 2 * chunk)
    for way, shard in enumerate((2 * gathered_z + core, 2 * z + (core ^ cross))):
        place[way] = (row == part * 64 + shard * 4 + low).astype(jnp.bfloat16)
    results = (
        (inner, inner_out), (inner_t, inner_t_out), (outer_fwd, outer_fwd_out),
        (outer_inv, outer_inv_out), (place, place_out), (limits, limits_out),
    )
    copies = [pltpu.make_async_copy(source, target, sems.at[i]) for i, (source, target) in enumerate(results)]
    for copy in copies:
        copy.start()
    for copy in copies:
        copy.wait()


def unpack_lines(messages, held, each):
    for at in range(messages.shape[0]):
        message = messages[at].astype(jnp.float32)
        for group in range(each // 4):
            first = at * each + 4 * group
            held[first : first + 4, :] = message[:, group * LANES : (group + 1) * LANES]


def pack_lines(held, messages, each):
    for at in range(messages.shape[0]):
        groups = [held[at * each + 4 * group : at * each + 4 * group + 4, :] for group in range(each // 4)]
        messages[at] = jnp.concatenate(groups, axis=1).astype(jnp.bfloat16)


def legendre_forward_kernel(gathered, gathered_x, table, out, held):
    slots, rows, degrees = table.shape
    waves = out.shape[0]
    row_count = rows // waves
    each = slots * row_count
    for pair in range(slots // 2):
        at = pl.ds(16 * pair, 16)
        both = [source[z, at, :].astype(jnp.float32) for source in (gathered, gathered_x) for z in range(source.shape[0])]
        for half in range(2):
            slot = 2 * pair + half
            spec = jnp.concatenate([b[8 * half : 8 * half + 8] for b in both], axis=0).astype(jnp.bfloat16)
            sums = dot(table[slot], spec, NT)
            for member in range(row_count):
                held[pl.ds(slot * row_count + member, waves, stride=each), :] = sums[
                    waves * member : waves * (member + 1)
                ]
    pack_lines(held, out, each)


def legendre_inverse_kernel(
    arrived, swapped, table, table_swapped, own, one, one_x, two, two_x, three, four, held, held_swapped
):
    slots, rows, degrees = table.shape
    waves = arrived.shape[0]
    row_count = rows // waves
    each = slots * row_count
    unpack_lines(arrived, held, each)
    unpack_lines(swapped, held_swapped, each)

    def share(ref, slot, legendre, turn=0):
        weighted = jnp.concatenate(
            [ref[pl.ds(slot * row_count + member, waves, stride=each), :] for member in range(row_count)], axis=0
        )
        if turn:
            weighted = pltpu.roll(weighted, turn, 1)
        return dot(weighted[:, :64].astype(jnp.bfloat16), legendre[slot], TN)

    for pair in range(slots // 2):
        at = pl.ds(16 * pair, 16)
        sums = [
            share(held, slot, table) + share(held_swapped, slot, table_swapped, 64) for slot in (2 * pair, 2 * pair + 1)
        ]
        pieces = [jnp.concatenate([s[8 * chunk : 8 * chunk + 8] for s in sums], axis=0) for chunk in range(8)]
        own[at, :] = pieces[0]
        targets = (one, one_x, two, two_x, three.at[0], three.at[1], four)
        for target, piece in zip(targets, pieces[1:]):
            target[at, :] = piece.astype(jnp.bfloat16)


def fourier_kernel(
    arrived, inner_in, inner_t_in, outer_fwd_in, outer_inv_in, place_in, limits_in,
    grid_out, sent,
    inner, inner_t, outer_fwd, outer_inv, place, limits, held, back, turned, products, lines_out, sems, out_sems,
):
    inputs = (
        (place_in, place), (outer_fwd_in, outer_fwd), (limits_in, limits),
        (inner_t_in, inner_t), (inner_in, inner), (outer_inv_in, outer_inv),
    )
    copies = [pltpu.make_async_copy(source, target, sems.at[i]) for i, (source, target) in enumerate(inputs)]
    for copy in copies:
        copy.start()
    row_count = inner.shape[0]
    slots = held.shape[0] // row_count
    each = held.shape[0] // arrived.shape[0]
    parts = slots // LANES
    levels = grid_out.shape[1]
    unpack_lines(arrived, held, each)
    for copy in copies[:3]:
        copy.wait()
    column = lax.broadcasted_iota(jnp.int32, (1, BLOCK), 1).astype(jnp.float32)

    def rotate(member):
        lines = held[pl.ds(member, slots, stride=row_count), :].astype(jnp.bfloat16)
        coef = dot(place[0], lines, NT)
        for step in range(BLOCKS):
            rows = pl.ds(step * levels, levels)
            for part in range(parts):
                real = coef[:levels, part * LANES : (part + 1) * LANES]
                imag = coef[levels:, part * LANES : (part + 1) * LANES]
                at = part * 2 * LANES
                cosine = outer_fwd[member, step : step + 1, at : at + LANES]
                sine = outer_fwd[member, step : step + 1, at + LANES : at + 2 * LANES]
                turned[member, rows, at : at + LANES] = (real * cosine - imag * sine).astype(jnp.bfloat16)
                turned[member, rows, at + LANES : at + 2 * LANES] = (real * sine + imag * cosine).astype(jnp.bfloat16)

    def spread(member):
        return dot(turned[member], inner_t[member], NN)

    def multiply(member, values):
        points = jnp.concatenate([limits[member, :1, :]] * (BLOCK // LANES), axis=1)
        for step in range(BLOCKS):
            width = min(BLOCK, LONPAD - step * BLOCK)
            line = values[step * levels : (step + 1) * levels]
            line = jnp.where(column + step * BLOCK < points, line, 0.0).astype(jnp.bfloat16)
            lines_out[member, :, step * BLOCK : step * BLOCK + width] = line[:, :width]
            line = line.astype(jnp.float32)
            partner = pltpu.roll(line, levels - 1, 0)
            products[member, step * levels : (step + 1) * levels, :] = (line * partner).astype(jnp.bfloat16)
        result = pltpu.make_async_copy(lines_out.at[member], grid_out.at[member], out_sems.at[member])
        result.start()
        return result

    def analyse(member):
        return dot(products[member], inner[member], NN)

    def collect(member, sums):
        reals, imags = [], []
        for part in range(parts):
            at = part * 2 * LANES
            real = jnp.zeros((levels, LANES), jnp.float32)
            imag = jnp.zeros((levels, LANES), jnp.float32)
            for step in range(BLOCKS):
                rows = slice(step * levels, (step + 1) * levels)
                cosine = outer_inv[member, step : step + 1, at : at + LANES]
                sine = outer_inv[member, step : step + 1, at + LANES : at + 2 * LANES]
                even, odd = sums[rows, at : at + LANES], sums[rows, at + LANES : at + 2 * LANES]
                real += even * cosine + odd * sine
                imag += odd * cosine - even * sine
            reals.append(real)
            imags.append(imag)
        analysed = jnp.concatenate([jnp.concatenate(reals, axis=1), jnp.concatenate(imags, axis=1)], axis=0)
        back[pl.ds(member, slots, stride=row_count), :] = dot(analysed.T.astype(jnp.bfloat16), place[1], NN)

    rotate(0)
    copies[3].wait()
    copies[4].wait()
    copies[5].wait()
    values, sums, results = {0: spread(0)}, {}, []
    for member in range(row_count):
        if member + 1 < row_count:
            rotate(member + 1)
        if member > 0:
            sums[member - 1] = analyse(member - 1)
        results.append(multiply(member, values.pop(member)))
        if member + 1 < row_count:
            values[member + 1] = spread(member + 1)
        if member > 0:
            collect(member - 1, sums.pop(member - 1))
    collect(row_count - 1, analyse(row_count - 1))
    pack_lines(back, sent, each)
    for result in results:
        result.wait()


def add_three_kernel(two, two_x, three, four, out, out_x):
    out[...] = (
        two[...].astype(jnp.float32) + three[0].astype(jnp.float32) + four[...].astype(jnp.float32)
    ).astype(jnp.bfloat16)
    out_x[...] = (two_x[...].astype(jnp.float32) + three[1].astype(jnp.float32)).astype(jnp.bfloat16)


def add_own_kernel(own, one, one_x, two, two_x, out):
    total = own[...]
    for landed in (one, one_x, two, two_x):
        total = total + landed[...].astype(jnp.float32)
    groups, cols, _ = out.shape
    for group in range(groups):
        out[group] = total[group * cols : (group + 1) * cols]


def shards(spectra, legendre, lat_weight, wave_of_slot, lat_of_row, lon_count):
    waves = lax.axis_size("wave")
    fields = lax.axis_size("field")
    zs = fields // 2
    wave_id = lax.axis_index("wave").astype(jnp.int32).reshape(1)
    field_id = lax.axis_index("field").astype(jnp.int32).reshape(1)
    slots, _, degrees, cols = spectra.shape
    band = legendre.shape[2]
    rows = 2 * band
    row_count = rows // waves
    all_slots = wave_of_slot.shape[0]
    levels = cols * fields
    each = row_count * slots
    coded = slots * 2 * cols

    like_cores = [list(range(0, fields, 2)), list(range(fields - 1, 0, -2))]

    def hop(x, by, cross=0):
        pairs = [
            (i, (2 * (i // 2 + side_of(i % 2) * by) + (i % 2 ^ cross)) % fields) for i in range(fields)
        ]
        return lax.ppermute(x, "field", pairs)

    def swap(x):
        return hop(x, 0, 1)

    def local(kernel, out_shape, name, micros, mebibytes=8, in_specs=None, out_specs=None, scratch=()):
        if in_specs is None:
            in_specs = pl.BlockSpec(memory_space=pltpu.VMEM)
        return pl.pallas_call(
            kernel,
            out_shape=out_shape,
            in_specs=in_specs,
            out_specs=jax.tree.map(lambda _: vmem(), out_shape) if out_specs is None else out_specs,
            scratch_shapes=list(scratch),
            compiler_params=params(mebibytes),
            cost_estimate=cost(micros),
            name=name,
        )

    row_table = jax.ShapeDtypeStruct((slots, rows, degrees), jnp.bfloat16)
    fourier_shape = jax.ShapeDtypeStruct((waves, 4, each // 4 * LANES), jnp.bfloat16)
    float_rows = pltpu.VMEM((waves * each, LANES), jnp.float32)

    own = jnp.transpose(spectra, (0, 1, 3, 2)).reshape(coded, degrees)
    gathered = lax.all_gather(own, "field", axis_index_groups=like_cores)
    gathered, legendre = lax.optimization_barrier((gathered, jnp.transpose(legendre, (0, 2, 1))))
    gathered_x = swap(gathered)
    legendre_x = swap(legendre)

    def ordered_rows(values, band_of):
        return local(
            functools.partial(legendre_rows_kernel, waves=waves, fields=fields),
            row_table,
            "legendre_rows",
            2,
            in_specs=[smem(), smem(), hbm(), hbm(), hbm()],
            scratch=[
                pltpu.SMEM(wave_of_slot.shape, jnp.int32),
                pltpu.SMEM(lat_of_row.shape, jnp.int32),
                pltpu.VMEM((slots, band, degrees), jnp.bfloat16),
                pltpu.VMEM((rows, LANES), jnp.float32),
                pltpu.VMEM((rows, LANES), jnp.float32),
                pltpu.SemaphoreType.DMA((3,)),
            ],
        )(wave_id, band_of, in_hbm(wave_of_slot), in_hbm(lat_of_row), in_hbm(values))

    table = ordered_rows(legendre, field_id)
    gathered_x, legendre_x = lax.optimization_barrier((gathered_x, legendre_x))
    outgoing = local(
        legendre_forward_kernel, fourier_shape, "legendre_forward", 4, 16, in_specs=[vmem()] * 3, scratch=[float_rows]
    )(gathered, gathered_x, table)
    outgoing, lat_weight = lax.optimization_barrier((outgoing, lat_weight))
    arrived = lax.all_to_all(outgoing, "wave", split_axis=0, concat_axis=0, tiled=True)
    tables = (
        ((row_count, BLOCK, 2 * all_slots), jnp.bfloat16),
        ((row_count, 2 * all_slots, BLOCK), jnp.bfloat16),
        ((row_count, 16, 2 * all_slots), jnp.float32),
        ((row_count, 16, 2 * all_slots), jnp.float32),
        ((2, LANES, LANES), jnp.bfloat16),
        ((row_count, 8, LANES), jnp.float32),
    )
    tables_vmem = [pltpu.VMEM(shape, kind) for shape, kind in tables]
    prepared = local(
        functools.partial(fourier_tables_kernel, fields=fields, zs=zs),
        [pltpu.HBM(shape, kind) for shape, kind in tables],
        "fourier_tables",
        4,
        16,
        in_specs=[smem()] * 5 + [vmem()],
        out_specs=[hbm()] * 6,
        scratch=tables_vmem + [pltpu.SemaphoreType.DMA((6,))],
    )(
        wave_id, field_id, lat_of_row, lon_count, lat_weight,
        wave_of_slot.astype(jnp.float32).reshape(1, all_slots),
    )
    arrived, prepared = lax.optimization_barrier((arrived, prepared))
    prepared = [in_hbm(x) for x in prepared]

    grid_field, sent = local(
        fourier_kernel,
        (jax.ShapeDtypeStruct((row_count, levels, LONPAD), jnp.bfloat16), fourier_shape),
        "fourier",
        6,
        32,
        in_specs=[vmem()] + [hbm()] * 6,
        out_specs=(hbm(), vmem()),
        scratch=tables_vmem + [
            float_rows,
            float_rows,
            pltpu.VMEM((row_count, BLOCKS * levels, 2 * all_slots), jnp.bfloat16),
            pltpu.VMEM((row_count, BLOCKS * levels, BLOCK), jnp.bfloat16),
            pltpu.VMEM((row_count, levels, LONPAD), jnp.bfloat16),
            pltpu.SemaphoreType.DMA((6,)),
            pltpu.SemaphoreType.DMA((row_count,)),
        ],
    )(arrived, *prepared)

    sent, legendre_x = lax.optimization_barrier((sent, legendre_x))
    returned = lax.all_to_all(sent, "wave", split_axis=0, concat_axis=0, tiled=True)

    table_x = ordered_rows(legendre_x, field_id ^ 1)
    returned, table_x = lax.optimization_barrier((returned, table_x))

    chunk = jax.ShapeDtypeStruct((coded, degrees), jnp.bfloat16)
    own, one, one_x, two, two_x, three, four = local(
        legendre_inverse_kernel,
        (
            jax.ShapeDtypeStruct((coded, degrees), jnp.float32),
            chunk, chunk, chunk, chunk, jax.ShapeDtypeStruct((2, coded, degrees), jnp.bfloat16), chunk,
        ),
        "legendre_inverse",
        2,
        16,
        in_specs=[vmem()] * 4,
        scratch=[float_rows, float_rows],
    )(returned, swap(returned), table, table_x)
    three, four = hop(three, -1), hop(four, -2)
    two, two_x = local(add_three_kernel, (chunk, chunk), "add_three", 1, in_specs=[vmem()] * 4)(
        two, two_x, three, four
    )
    one, one_x = hop(one, -1), hop(one_x, -1, 1)
    two, two_x = hop(two, -2), hop(two_x, -2, 1)
    total = local(
        add_own_kernel,
        jax.ShapeDtypeStruct((2 * slots, cols, degrees), jnp.float32),
        "add_own",
        1,
        in_specs=[vmem()] * 5,
    )(own, one, one_x, two, two_x)
    spectral = jnp.transpose(total.reshape(slots, 2, cols, degrees), (0, 1, 3, 2))
    return grid_field, spectral


def solution(mesh):
    in_specs = (P("wave", None, None, "field"), P("wave", None, "field"), P("field"), P(), P(), P())
    out_specs = (P(("wave", "field"), None, None), P("wave", None, None, "field"))
    return jax.shard_map(shards, mesh=mesh, in_specs=in_specs, out_specs=out_specs, check_vma=False)
```

```python
import functools
import math

import jax
import jax.numpy as jnp
from jax import lax
from jax.experimental import pallas as pl
from jax.experimental.pallas import tpu as pltpu
from jax.sharding import PartitionSpec as P

LONPAD = 3200
LANES = 128
BLOCK = 512
BLOCKS = -(-LONPAD // BLOCK)

NT = (((1,), (1,)), ((), ()))
NN = (((1,), (0,)), ((), ()))
TN = (((0,), (0,)), ((), ()))


def dot(a, b, dims):
    return lax.dot_general(a, b, dims, preferred_element_type=jnp.float32)


def params(mebibytes):
    return pltpu.CompilerParams(vmem_limit_bytes=mebibytes * 1024 * 1024)


def in_hbm(x):
    return pltpu.with_memory_space_constraint(x, pltpu.HBM)


def cost(micros):
    return pl.CostEstimate(flops=0, bytes_accessed=int(micros * 3.7e6), transcendentals=0)


def smem():
    return pl.BlockSpec(memory_space=pltpu.SMEM)


def vmem():
    return pl.BlockSpec(memory_space=pltpu.VMEM)


def hbm():
    return pl.BlockSpec(memory_space=pltpu.HBM)


def side_of(core):
    return 1 - 2 * core


def legendre_rows_kernel(
    wave_id, field_id, wave_of_slot, lat_of_row, legendre, out,
    slot_waves, row_lats, held, pick, south, sems, *, waves, fields,
):
    sources = ((lat_of_row, row_lats), (wave_of_slot, slot_waves), (legendre, held))
    copies = [pltpu.make_async_copy(source, target, sems.at[i]) for i, (source, target) in enumerate(sources)]
    for copy in copies:
        copy.start()
    slots, band, degrees = held.shape
    rows = out.shape[1]
    row_count = rows // waves
    half = row_lats.shape[0] // 2
    own, field = wave_id[0], field_id[0]
    lane = lax.broadcasted_iota(jnp.int32, (1, LANES), 1)
    copies[0].wait()
    for row in range(rows):
        member, wave = divmod(row, waves)
        lat = row_lats[(wave * fields + field) * row_count + member]
        is_south = lat >= half
        hemi = jnp.where(is_south, 2 * half - 1 - lat, lat) - field * band
        pick[row : row + 1, :] = (lane == hemi).astype(jnp.float32)
        south[row : row + 1, :] = jnp.broadcast_to(is_south.astype(jnp.float32), (1, LANES))
    copies[1].wait()
    copies[2].wait()
    offsets = lax.broadcasted_iota(jnp.int32, (1, degrees), 1)
    sign = 1.0 - 2.0 * (south[:, :1] * (offsets & 1).astype(jnp.float32))
    chosen = pick[:, :band].astype(jnp.bfloat16)
    for slot in range(slots):
        live = offsets < degrees - slot_waves[own * slots + slot]
        out[slot] = jnp.where(live, dot(chosen, held[slot], NN) * sign, 0.0).astype(jnp.bfloat16)


def sin_cos(phase, period):
    inverse = 1.0 / period
    turns = (phase - jnp.floor(phase * inverse + 0.5) * period) * inverse
    quarter = jnp.floor(4.0 * turns + 0.5)
    w = (2.0 * math.pi) * (turns - 0.25 * quarter)
    w2 = w * w
    sine = w * (1.0 + w2 * (-1.0 / 6 + w2 * (1.0 / 120 + w2 * (-1.0 / 5040 + w2 * (1.0 / 362880)))))
    cosine = 1.0 + w2 * (-0.5 + w2 * (1.0 / 24 + w2 * (-1.0 / 720 + w2 * (1.0 / 40320))))
    size = jnp.abs(quarter)
    odd = size == 1.0
    flipped = size >= 2.0
    cos_out = jnp.where(odd, sine, cosine)
    sin_out = jnp.where(odd, cosine, sine)
    cos_out = jnp.where(flipped | (quarter == 1.0), -cos_out, cos_out)
    sin_out = jnp.where(flipped | (quarter == -1.0), -sin_out, sin_out)
    return cos_out, sin_out


def fourier_tables_kernel(
    wave_id, field_id, lat_of_row, lon_count, lat_weight, waves_row,
    inner_out, inner_t_out, outer_fwd_out, outer_inv_out, place_out, limits_out,
    inner, inner_t, outer_fwd, outer_inv, place, limits, sems, *, fields, zs,
):
    row_count = inner.shape[0]
    band = lat_weight.shape[0]
    half = lon_count.shape[0]
    slots = waves_row.shape[1]
    steps = outer_fwd.shape[1]
    wave, field = wave_id[0], field_id[0]
    for member in range(row_count):
        lat = lat_of_row[(wave * fields + field) * row_count + member]
        hemi = jnp.where(lat >= half, 2 * half - 1 - lat, lat)
        points = lon_count[hemi].astype(jnp.float32)
        period = jnp.broadcast_to(points, (1, LANES))
        limits[member] = jnp.broadcast_to(points, limits.shape[1:])
        weight = lat_weight[hemi - field * band] / jnp.sqrt(period)
        for part in range(slots // LANES):
            m = waves_row[:, part * LANES : (part + 1) * LANES]
            at = part * 2 * LANES
            x = lax.broadcasted_iota(jnp.int32, (BLOCK, LANES), 0).astype(jnp.float32)
            cosine, sine = sin_cos(x * m, period)
            both = jnp.concatenate([cosine, -sine], axis=1)
            inner[member, :, at : at + 2 * LANES] = both.astype(jnp.bfloat16)
            inner_t[member, at : at + 2 * LANES, :] = both.T.astype(jnp.bfloat16)
            x = (BLOCK * lax.broadcasted_iota(jnp.int32, (steps, LANES), 0)).astype(jnp.float32)
            cosine, sine = sin_cos(x * m, period)
            both = jnp.concatenate([cosine, sine], axis=1)
            outer_fwd[member, :, at : at + 2 * LANES] = both * (1.0 / math.sqrt(slots))
            outer_inv[member, :, at : at + 2 * LANES] = both * jnp.concatenate([weight, weight], axis=1)
    at = lax.broadcasted_iota(jnp.int32, (LANES, LANES), 1)
    core, chunk, part, low = (field & 1) ^ (at >> 6), (at >> 3) & 7, (at >> 2) & 1, at & 3
    away = (chunk + 1) >> 1
    cross = ((chunk & 1) ^ 1) & (chunk > 0).astype(jnp.int32)
    z = ((field >> 1) - side_of(core) * away + zs) & (zs - 1)
    row = lax.broadcasted_iota(jnp.int32, (LANES, LANES), 0)
    gathered_z = chunk + core * (zs - 1 - 2 * chunk)
    for way, shard in enumerate((2 * gathered_z + core, 2 * z + (core ^ cross))):
        place[way] = (row == part * 64 + shard * 4 + low).astype(jnp.bfloat16)
    results = (
        (inner, inner_out), (inner_t, inner_t_out), (outer_fwd, outer_fwd_out),
        (outer_inv, outer_inv_out), (place, place_out), (limits, limits_out),
    )
    copies = [pltpu.make_async_copy(source, target, sems.at[i]) for i, (source, target) in enumerate(results)]
    for copy in copies:
        copy.start()
    for copy in copies:
        copy.wait()


def unpack_lines(messages, held, each):
    for at in range(messages.shape[0]):
        message = messages[at].astype(jnp.float32)
        for group in range(each // 4):
            first = at * each + 4 * group
            held[first : first + 4, :] = message[:, group * LANES : (group + 1) * LANES]


def pack_lines(held, messages, each):
    for at in range(messages.shape[0]):
        groups = [held[at * each + 4 * group : at * each + 4 * group + 4, :] for group in range(each // 4)]
        messages[at] = jnp.concatenate(groups, axis=1).astype(jnp.bfloat16)


def legendre_forward_kernel(gathered, gathered_x, table, out, held):
    slots, rows, degrees = table.shape
    waves = out.shape[0]
    row_count = rows // waves
    each = slots * row_count
    for pair in range(slots // 2):
        at = pl.ds(16 * pair, 16)
        both = [source[z, at, :].astype(jnp.float32) for source in (gathered, gathered_x) for z in range(source.shape[0])]
        for half in range(2):
            slot = 2 * pair + half
            spec = jnp.concatenate([b[8 * half : 8 * half + 8] for b in both], axis=0).astype(jnp.bfloat16)
            sums = dot(table[slot], spec, NT)
            for member in range(row_count):
                held[pl.ds(slot * row_count + member, waves, stride=each), :] = sums[
                    waves * member : waves * (member + 1)
                ]
    pack_lines(held, out, each)


def legendre_inverse_kernel(
    arrived, swapped, table, table_swapped, own, one, one_x, two, two_x, three, four, held, held_swapped
):
    slots, rows, degrees = table.shape
    waves = arrived.shape[0]
    row_count = rows // waves
    each = slots * row_count
    unpack_lines(arrived, held, each)
    unpack_lines(swapped, held_swapped, each)

    def share(ref, slot, legendre, turn=0):
        weighted = jnp.concatenate(
            [ref[pl.ds(slot * row_count + member, waves, stride=each), :] for member in range(row_count)], axis=0
        )
        if turn:
            weighted = pltpu.roll(weighted, turn, 1)
        return dot(weighted[:, :64].astype(jnp.bfloat16), legendre[slot], TN)

    for pair in range(slots // 2):
        at = pl.ds(16 * pair, 16)
        sums = [
            share(held, slot, table) + share(held_swapped, slot, table_swapped, 64) for slot in (2 * pair, 2 * pair + 1)
        ]
        pieces = [jnp.concatenate([s[8 * chunk : 8 * chunk + 8] for s in sums], axis=0) for chunk in range(8)]
        own[at, :] = pieces[0]
        targets = (one, one_x, two, two_x, three.at[0], three.at[1], four)
        for target, piece in zip(targets, pieces[1:]):
            target[at, :] = piece.astype(jnp.bfloat16)


def fourier_kernel(
    arrived, inner_in, inner_t_in, outer_fwd_in, outer_inv_in, place_in, limits_in,
    grid_out, sent,
    inner, inner_t, outer_fwd, outer_inv, place, limits, held, back, turned, products, lines_out, sems, out_sems,
):
    inputs = (
        (place_in, place), (outer_fwd_in, outer_fwd), (limits_in, limits),
        (inner_t_in, inner_t), (inner_in, inner), (outer_inv_in, outer_inv),
    )
    copies = [pltpu.make_async_copy(source, target, sems.at[i]) for i, (source, target) in enumerate(inputs)]
    for copy in copies:
        copy.start()
    row_count = inner.shape[0]
    slots = held.shape[0] // row_count
    each = held.shape[0] // arrived.shape[0]
    parts = slots // LANES
    levels = grid_out.shape[1]
    unpack_lines(arrived, held, each)
    for copy in copies[:3]:
        copy.wait()
    column = lax.broadcasted_iota(jnp.int32, (1, BLOCK), 1).astype(jnp.float32)

    def rotate(member):
        lines = held[pl.ds(member, slots, stride=row_count), :].astype(jnp.bfloat16)
        coef = dot(place[0], lines, NT)
        for step in range(BLOCKS):
            rows = pl.ds(step * levels, levels)
            for part in range(parts):
                real = coef[:levels, part * LANES : (part + 1) * LANES]
                imag = coef[levels:, part * LANES : (part + 1) * LANES]
                at = part * 2 * LANES
                cosine = outer_fwd[member, step : step + 1, at : at + LANES]
                sine = outer_fwd[member, step : step + 1, at + LANES : at + 2 * LANES]
                turned[member, rows, at : at + LANES] = (real * cosine - imag * sine).astype(jnp.bfloat16)
                turned[member, rows, at + LANES : at + 2 * LANES] = (real * sine + imag * cosine).astype(jnp.bfloat16)

    def spread(member):
        return dot(turned[member], inner_t[member], NN)

    def multiply(member, values):
        points = jnp.concatenate([limits[member, :1, :]] * (BLOCK // LANES), axis=1)
        for step in range(BLOCKS):
            width = min(BLOCK, LONPAD - step * BLOCK)
            line = values[step * levels : (step + 1) * levels]
            line = jnp.where(column + step * BLOCK < points, line, 0.0).astype(jnp.bfloat16)
            lines_out[member, :, step * BLOCK : step * BLOCK + width] = line[:, :width]
            line = line.astype(jnp.float32)
            partner = pltpu.roll(line, levels - 1, 0)
            products[member, step * levels : (step + 1) * levels, :] = (line * partner).astype(jnp.bfloat16)
        result = pltpu.make_async_copy(lines_out.at[member], grid_out.at[member], out_sems.at[member])
        result.start()
        return result

    def analyse(member):
        return dot(products[member], inner[member], NN)

    def collect(member, sums):
        reals, imags = [], []
        for part in range(parts):
            at = part * 2 * LANES
            real = jnp.zeros((levels, LANES), jnp.float32)
            imag = jnp.zeros((levels, LANES), jnp.float32)
            for step in range(BLOCKS):
                rows = slice(step * levels, (step + 1) * levels)
                cosine = outer_inv[member, step : step + 1, at : at + LANES]
                sine = outer_inv[member, step : step + 1, at + LANES : at + 2 * LANES]
                even, odd = sums[rows, at : at + LANES], sums[rows, at + LANES : at + 2 * LANES]
                real += even * cosine + odd * sine
                imag += odd * cosine - even * sine
            reals.append(real)
            imags.append(imag)
        analysed = jnp.concatenate([jnp.concatenate(reals, axis=1), jnp.concatenate(imags, axis=1)], axis=0)
        back[pl.ds(member, slots, stride=row_count), :] = dot(analysed.T.astype(jnp.bfloat16), place[1], NN)

    rotate(0)
    copies[3].wait()
    values, sums, results = {0: spread(0)}, {}, []
    for member in range(row_count):
        if member + 1 < row_count:
            rotate(member + 1)
        if member == 1:
            copies[4].wait()
            copies[5].wait()
        if member > 0:
            sums[member - 1] = analyse(member - 1)
        results.append(multiply(member, values.pop(member)))
        if member + 1 < row_count:
            values[member + 1] = spread(member + 1)
        if member > 0:
            collect(member - 1, sums.pop(member - 1))
    collect(row_count - 1, analyse(row_count - 1))
    pack_lines(back, sent, each)
    for result in results:
        result.wait()


def add_three_kernel(two, two_x, three, four, out, out_x):
    out[...] = (
        two[...].astype(jnp.float32) + three[0].astype(jnp.float32) + four[...].astype(jnp.float32)
    ).astype(jnp.bfloat16)
    out_x[...] = (two_x[...].astype(jnp.float32) + three[1].astype(jnp.float32)).astype(jnp.bfloat16)


def add_own_kernel(own, one, one_x, two, two_x, out):
    total = own[...]
    for landed in (one, one_x, two, two_x):
        total = total + landed[...].astype(jnp.float32)
    groups, cols, _ = out.shape
    for group in range(groups):
        out[group] = total[group * cols : (group + 1) * cols]


def shards(spectra, legendre, lat_weight, wave_of_slot, lat_of_row, lon_count):
    waves = lax.axis_size("wave")
    fields = lax.axis_size("field")
    zs = fields // 2
    wave_id = lax.axis_index("wave").astype(jnp.int32).reshape(1)
    field_id = lax.axis_index("field").astype(jnp.int32).reshape(1)
    slots, _, degrees, cols = spectra.shape
    band = legendre.shape[2]
    rows = 2 * band
    row_count = rows // waves
    all_slots = wave_of_slot.shape[0]
    levels = cols * fields
    each = row_count * slots
    coded = slots * 2 * cols

    like_cores = [list(range(0, fields, 2)), list(range(fields - 1, 0, -2))]

    def hop(x, by, cross=0):
        pairs = [
            (i, (2 * (i // 2 + side_of(i % 2) * by) + (i % 2 ^ cross)) % fields) for i in range(fields)
        ]
        return lax.ppermute(x, "field", pairs)

    def swap(x):
        return hop(x, 0, 1)

    def local(kernel, out_shape, name, micros, mebibytes=8, in_specs=None, out_specs=None, scratch=()):
        if in_specs is None:
            in_specs = pl.BlockSpec(memory_space=pltpu.VMEM)
        return pl.pallas_call(
            kernel,
            out_shape=out_shape,
            in_specs=in_specs,
            out_specs=jax.tree.map(lambda _: vmem(), out_shape) if out_specs is None else out_specs,
            scratch_shapes=list(scratch),
            compiler_params=params(mebibytes),
            cost_estimate=cost(micros),
            name=name,
        )

    row_table = jax.ShapeDtypeStruct((slots, rows, degrees), jnp.bfloat16)
    fourier_shape = jax.ShapeDtypeStruct((waves, 4, each // 4 * LANES), jnp.bfloat16)
    float_rows = pltpu.VMEM((waves * each, LANES), jnp.float32)

    own = jnp.transpose(spectra, (0, 1, 3, 2)).reshape(coded, degrees)
    gathered = lax.all_gather(own, "field", axis_index_groups=like_cores)
    gathered, legendre = lax.optimization_barrier((gathered, jnp.transpose(legendre, (0, 2, 1))))
    gathered_x = swap(gathered)
    legendre_x = swap(legendre)

    def ordered_rows(values, band_of):
        return local(
            functools.partial(legendre_rows_kernel, waves=waves, fields=fields),
            row_table,
            "legendre_rows",
            2,
            in_specs=[smem(), smem(), hbm(), hbm(), hbm()],
            scratch=[
                pltpu.SMEM(wave_of_slot.shape, jnp.int32),
                pltpu.SMEM(lat_of_row.shape, jnp.int32),
                pltpu.VMEM((slots, band, degrees), jnp.bfloat16),
                pltpu.VMEM((rows, LANES), jnp.float32),
                pltpu.VMEM((rows, LANES), jnp.float32),
                pltpu.SemaphoreType.DMA((3,)),
            ],
        )(wave_id, band_of, in_hbm(wave_of_slot), in_hbm(lat_of_row), in_hbm(values))

    table = ordered_rows(legendre, field_id)
    gathered_x, legendre_x = lax.optimization_barrier((gathered_x, legendre_x))
    outgoing = local(
        legendre_forward_kernel, fourier_shape, "legendre_forward", 4, 16, in_specs=[vmem()] * 3, scratch=[float_rows]
    )(gathered, gathered_x, table)
    outgoing, lat_weight = lax.optimization_barrier((outgoing, lat_weight))
    arrived = lax.all_to_all(outgoing, "wave", split_axis=0, concat_axis=0, tiled=True)
    tables = (
        ((row_count, BLOCK, 2 * all_slots), jnp.bfloat16),
        ((row_count, 2 * all_slots, BLOCK), jnp.bfloat16),
        ((row_count, 16, 2 * all_slots), jnp.float32),
        ((row_count, 16, 2 * all_slots), jnp.float32),
        ((2, LANES, LANES), jnp.bfloat16),
        ((row_count, 8, LANES), jnp.float32),
    )
    tables_vmem = [pltpu.VMEM(shape, kind) for shape, kind in tables]
    prepared = local(
        functools.partial(fourier_tables_kernel, fields=fields, zs=zs),
        [pltpu.HBM(shape, kind) for shape, kind in tables],
        "fourier_tables",
        4,
        24,
        in_specs=[smem()] * 5 + [vmem()],
        out_specs=[hbm()] * 6,
        scratch=tables_vmem + [pltpu.SemaphoreType.DMA((6,))],
    )(
        wave_id, field_id, lat_of_row, lon_count, lat_weight,
        wave_of_slot.astype(jnp.float32).reshape(1, all_slots),
    )
    arrived, prepared = lax.optimization_barrier((arrived, prepared))
    prepared = [in_hbm(x) for x in prepared]

    grid_field, sent = local(
        fourier_kernel,
        (jax.ShapeDtypeStruct((row_count, levels, LONPAD), jnp.bfloat16), fourier_shape),
        "fourier",
        6,
        40,
        in_specs=[vmem()] + [hbm()] * 6,
        out_specs=(hbm(), vmem()),
        scratch=tables_vmem + [
            float_rows,
            float_rows,
            pltpu.VMEM((row_count, BLOCKS * levels, 2 * all_slots), jnp.bfloat16),
            pltpu.VMEM((row_count, BLOCKS * levels, BLOCK), jnp.bfloat16),
            pltpu.VMEM((row_count, levels, LONPAD), jnp.bfloat16),
            pltpu.SemaphoreType.DMA((6,)),
            pltpu.SemaphoreType.DMA((row_count,)),
        ],
    )(arrived, *prepared)

    sent, legendre_x = lax.optimization_barrier((sent, legendre_x))
    returned = lax.all_to_all(sent, "wave", split_axis=0, concat_axis=0, tiled=True)

    table_x = ordered_rows(legendre_x, field_id ^ 1)
    returned, table_x = lax.optimization_barrier((returned, table_x))

    chunk = jax.ShapeDtypeStruct((coded, degrees), jnp.bfloat16)
    own, one, one_x, two, two_x, three, four = local(
        legendre_inverse_kernel,
        (
            jax.ShapeDtypeStruct((coded, degrees), jnp.float32),
            chunk, chunk, chunk, chunk, jax.ShapeDtypeStruct((2, coded, degrees), jnp.bfloat16), chunk,
        ),
        "legendre_inverse",
        2,
        16,
        in_specs=[vmem()] * 4,
        scratch=[float_rows, float_rows],
    )(returned, swap(returned), table, table_x)
    three, four = hop(three, -1), hop(four, -2)
    two, two_x = local(add_three_kernel, (chunk, chunk), "add_three", 1, in_specs=[vmem()] * 4)(
        two, two_x, three, four
    )
    one, one_x = hop(one, -1), hop(one_x, -1, 1)
    two, two_x = hop(two, -2), hop(two_x, -2, 1)
    total = local(
        add_own_kernel,
        jax.ShapeDtypeStruct((2 * slots, cols, degrees), jnp.float32),
        "add_own",
        1,
        in_specs=[vmem()] * 5,
    )(own, one, one_x, two, two_x)
    spectral = jnp.transpose(total.reshape(slots, 2, cols, degrees), (0, 1, 3, 2))
    return grid_field, spectral


def solution(mesh):
    in_specs = (P("wave", None, None, "field"), P("wave", None, "field"), P("field"), P(), P(), P())
    out_specs = (P(("wave", "field"), None, None), P("wave", None, None, "field"))
    return jax.shard_map(shards, mesh=mesh, in_specs=in_specs, out_specs=out_specs, check_vma=False)
```

```python
import functools
import math

import jax
import jax.numpy as jnp
from jax import lax
from jax.experimental import pallas as pl
from jax.experimental.pallas import tpu as pltpu
from jax.sharding import PartitionSpec as P

LONPAD = 3200
LANES = 128
BLOCK = 256
BLOCKS = -(-LONPAD // BLOCK)

NT = (((1,), (1,)), ((), ()))
NN = (((1,), (0,)), ((), ()))
TN = (((0,), (0,)), ((), ()))


def dot(a, b, dims):
    return lax.dot_general(a, b, dims, preferred_element_type=jnp.float32)


def params(mebibytes):
    return pltpu.CompilerParams(vmem_limit_bytes=mebibytes * 1024 * 1024)


def in_hbm(x):
    return pltpu.with_memory_space_constraint(x, pltpu.HBM)


def cost(micros):
    return pl.CostEstimate(flops=0, bytes_accessed=int(micros * 3.7e6), transcendentals=0)


def smem():
    return pl.BlockSpec(memory_space=pltpu.SMEM)


def vmem():
    return pl.BlockSpec(memory_space=pltpu.VMEM)


def hbm():
    return pl.BlockSpec(memory_space=pltpu.HBM)


def side_of(core):
    return 1 - 2 * core


def legendre_rows_kernel(
    wave_id, field_id, wave_of_slot, lat_of_row, legendre, out,
    slot_waves, row_lats, held, pick, south, sems, *, waves, fields,
):
    sources = ((lat_of_row, row_lats), (wave_of_slot, slot_waves), (legendre, held))
    copies = [pltpu.make_async_copy(source, target, sems.at[i]) for i, (source, target) in enumerate(sources)]
    for copy in copies:
        copy.start()
    slots, band, degrees = held.shape
    rows = out.shape[1]
    row_count = rows // waves
    half = row_lats.shape[0] // 2
    own, field = wave_id[0], field_id[0]
    lane = lax.broadcasted_iota(jnp.int32, (1, LANES), 1)
    copies[0].wait()
    for row in range(rows):
        member, wave = divmod(row, waves)
        lat = row_lats[(wave * fields + field) * row_count + member]
        is_south = lat >= half
        hemi = jnp.where(is_south, 2 * half - 1 - lat, lat) - field * band
        pick[row : row + 1, :] = (lane == hemi).astype(jnp.float32)
        south[row : row + 1, :] = jnp.broadcast_to(is_south.astype(jnp.float32), (1, LANES))
    copies[1].wait()
    copies[2].wait()
    offsets = lax.broadcasted_iota(jnp.int32, (1, degrees), 1)
    sign = 1.0 - 2.0 * (south[:, :1] * (offsets & 1).astype(jnp.float32))
    chosen = pick[:, :band].astype(jnp.bfloat16)
    for slot in range(slots):
        live = offsets < degrees - slot_waves[own * slots + slot]
        out[slot] = jnp.where(live, dot(chosen, held[slot], NN) * sign, 0.0).astype(jnp.bfloat16)


def sin_cos(phase, period):
    inverse = 1.0 / period
    turns = (phase - jnp.floor(phase * inverse + 0.5) * period) * inverse
    quarter = jnp.floor(4.0 * turns + 0.5)
    w = (2.0 * math.pi) * (turns - 0.25 * quarter)
    w2 = w * w
    sine = w * (1.0 + w2 * (-1.0 / 6 + w2 * (1.0 / 120 + w2 * (-1.0 / 5040 + w2 * (1.0 / 362880)))))
    cosine = 1.0 + w2 * (-0.5 + w2 * (1.0 / 24 + w2 * (-1.0 / 720 + w2 * (1.0 / 40320))))
    size = jnp.abs(quarter)
    odd = size == 1.0
    flipped = size >= 2.0
    cos_out = jnp.where(odd, sine, cosine)
    sin_out = jnp.where(odd, cosine, sine)
    cos_out = jnp.where(flipped | (quarter == 1.0), -cos_out, cos_out)
    sin_out = jnp.where(flipped | (quarter == -1.0), -sin_out, sin_out)
    return cos_out, sin_out


def fourier_tables_kernel(
    wave_id, field_id, lat_of_row, lon_count, lat_weight, waves_row,
    inner_out, inner_t_out, outer_fwd_out, outer_inv_out, place_out, limits_out,
    inner, inner_t, outer_fwd, outer_inv, place, limits, sems, *, fields, zs,
):
    row_count = inner.shape[0]
    band = lat_weight.shape[0]
    half = lon_count.shape[0]
    slots = waves_row.shape[1]
    steps = outer_fwd.shape[1]
    wave, field = wave_id[0], field_id[0]
    for member in range(row_count):
        lat = lat_of_row[(wave * fields + field) * row_count + member]
        hemi = jnp.where(lat >= half, 2 * half - 1 - lat, lat)
        points = lon_count[hemi].astype(jnp.float32)
        period = jnp.broadcast_to(points, (1, LANES))
        limits[member] = jnp.broadcast_to(points, limits.shape[1:])
        weight = lat_weight[hemi - field * band] / jnp.sqrt(period)
        for part in range(slots // LANES):
            m = waves_row[:, part * LANES : (part + 1) * LANES]
            at = part * 2 * LANES
            x = lax.broadcasted_iota(jnp.int32, (BLOCK, LANES), 0).astype(jnp.float32)
            cosine, sine = sin_cos(x * m, period)
            both = jnp.concatenate([cosine, -sine], axis=1)
            inner[member, :, at : at + 2 * LANES] = both.astype(jnp.bfloat16)
            inner_t[member, at : at + 2 * LANES, :] = both.T.astype(jnp.bfloat16)
            x = (BLOCK * lax.broadcasted_iota(jnp.int32, (steps, LANES), 0)).astype(jnp.float32)
            cosine, sine = sin_cos(x * m, period)
            both = jnp.concatenate([cosine, sine], axis=1)
            outer_fwd[member, :, at : at + 2 * LANES] = both * (1.0 / math.sqrt(slots))
            outer_inv[member, :, at : at + 2 * LANES] = both * jnp.concatenate([weight, weight], axis=1)
    at = lax.broadcasted_iota(jnp.int32, (LANES, LANES), 1)
    core, chunk, part, low = (field & 1) ^ (at >> 6), (at >> 3) & 7, (at >> 2) & 1, at & 3
    away = (chunk + 1) >> 1
    cross = ((chunk & 1) ^ 1) & (chunk > 0).astype(jnp.int32)
    z = ((field >> 1) - side_of(core) * away + zs) & (zs - 1)
    row = lax.broadcasted_iota(jnp.int32, (LANES, LANES), 0)
    gathered_z = chunk + core * (zs - 1 - 2 * chunk)
    for way, shard in enumerate((2 * gathered_z + core, 2 * z + (core ^ cross))):
        place[way] = (row == part * 64 + shard * 4 + low).astype(jnp.bfloat16)
    results = (
        (inner, inner_out), (inner_t, inner_t_out), (outer_fwd, outer_fwd_out),
        (outer_inv, outer_inv_out), (place, place_out), (limits, limits_out),
    )
    copies = [pltpu.make_async_copy(source, target, sems.at[i]) for i, (source, target) in enumerate(results)]
    for copy in copies:
        copy.start()
    for copy in copies:
        copy.wait()


def unpack_lines(messages, held, each):
    for at in range(messages.shape[0]):
        message = messages[at].astype(jnp.float32)
        for group in range(each // 4):
            first = at * each + 4 * group
            held[first : first + 4, :] = message[:, group * LANES : (group + 1) * LANES]


def pack_lines(held, messages, each):
    for at in range(messages.shape[0]):
        groups = [held[at * each + 4 * group : at * each + 4 * group + 4, :] for group in range(each // 4)]
        messages[at] = jnp.concatenate(groups, axis=1).astype(jnp.bfloat16)


def legendre_forward_kernel(gathered, gathered_x, table, out, held):
    slots, rows, degrees = table.shape
    waves = out.shape[0]
    row_count = rows // waves
    each = slots * row_count
    for pair in range(slots // 2):
        at = pl.ds(16 * pair, 16)
        both = [source[z, at, :].astype(jnp.float32) for source in (gathered, gathered_x) for z in range(source.shape[0])]
        for half in range(2):
            slot = 2 * pair + half
            spec = jnp.concatenate([b[8 * half : 8 * half + 8] for b in both], axis=0).astype(jnp.bfloat16)
            sums = dot(table[slot], spec, NT)
            for member in range(row_count):
                held[pl.ds(slot * row_count + member, waves, stride=each), :] = sums[
                    waves * member : waves * (member + 1)
                ]
    pack_lines(held, out, each)


def legendre_inverse_kernel(
    arrived, swapped, table, table_swapped, own, one, one_x, two, two_x, three, four, held, held_swapped
):
    slots, rows, degrees = table.shape
    waves = arrived.shape[0]
    row_count = rows // waves
    each = slots * row_count
    unpack_lines(arrived, held, each)
    unpack_lines(swapped, held_swapped, each)

    def share(ref, slot, legendre, turn=0):
        weighted = jnp.concatenate(
            [ref[pl.ds(slot * row_count + member, waves, stride=each), :] for member in range(row_count)], axis=0
        )
        if turn:
            weighted = pltpu.roll(weighted, turn, 1)
        return dot(weighted[:, :64].astype(jnp.bfloat16), legendre[slot], TN)

    for pair in range(slots // 2):
        at = pl.ds(16 * pair, 16)
        sums = [
            share(held, slot, table) + share(held_swapped, slot, table_swapped, 64) for slot in (2 * pair, 2 * pair + 1)
        ]
        pieces = [jnp.concatenate([s[8 * chunk : 8 * chunk + 8] for s in sums], axis=0) for chunk in range(8)]
        own[at, :] = pieces[0]
        targets = (one, one_x, two, two_x, three.at[0], three.at[1], four)
        for target, piece in zip(targets, pieces[1:]):
            target[at, :] = piece.astype(jnp.bfloat16)


def fourier_kernel(
    arrived, inner_in, inner_t_in, outer_fwd_in, outer_inv_in, place_in, limits_in,
    grid_out, sent,
    inner, inner_t, outer_fwd, outer_inv, place, limits, held, back, turned, products, lines_out, sems, out_sems,
):
    inputs = (
        (place_in, place), (outer_fwd_in, outer_fwd), (limits_in, limits),
        (inner_t_in, inner_t), (inner_in, inner), (outer_inv_in, outer_inv),
    )
    copies = [pltpu.make_async_copy(source, target, sems.at[i]) for i, (source, target) in enumerate(inputs)]
    for copy in copies:
        copy.start()
    row_count = inner.shape[0]
    each = arrived.shape[1] * arrived.shape[2] // LANES
    slots = arrived.shape[0] * each // row_count
    parts = slots // LANES
    levels = grid_out.shape[1]
    unpack_lines(arrived, held, each)
    for copy in copies[:3]:
        copy.wait()
    column = lax.broadcasted_iota(jnp.int32, (1, BLOCK), 1).astype(jnp.float32)

    def rotate(member):
        lines = held[pl.ds(member, slots, stride=row_count), :].astype(jnp.bfloat16)
        coef = dot(place[0], lines, NT)
        for step in range(BLOCKS):
            rows = pl.ds(step * levels, levels)
            for part in range(parts):
                real = coef[:levels, part * LANES : (part + 1) * LANES]
                imag = coef[levels:, part * LANES : (part + 1) * LANES]
                at = part * 2 * LANES
                cosine = outer_fwd[member, step : step + 1, at : at + LANES]
                sine = outer_fwd[member, step : step + 1, at + LANES : at + 2 * LANES]
                turned[member, rows, at : at + LANES] = (real * cosine - imag * sine).astype(jnp.bfloat16)
                turned[member, rows, at + LANES : at + 2 * LANES] = (real * sine + imag * cosine).astype(jnp.bfloat16)

    def spread(member):
        return dot(turned[member], inner_t[member], NN)

    def multiply(member, values):
        points = jnp.concatenate([limits[member, :1, :]] * (BLOCK // LANES), axis=1)
        for step in range(BLOCKS):
            width = min(BLOCK, LONPAD - step * BLOCK)
            line = values[step * levels : (step + 1) * levels]
            line = jnp.where(column + step * BLOCK < points, line, 0.0).astype(jnp.bfloat16)
            lines_out[member, :, step * BLOCK : step * BLOCK + width] = line[:, :width]
            line = line.astype(jnp.float32)
            partner = pltpu.roll(line, levels - 1, 0)
            products[member, step * levels : (step + 1) * levels, :] = (line * partner).astype(jnp.bfloat16)
        result = pltpu.make_async_copy(lines_out.at[member], grid_out.at[member], out_sems.at[member])
        result.start()
        return result

    def analyse(member):
        return dot(products[member], inner[member], NN)

    def collect(member, sums):
        reals, imags = [], []
        for part in range(parts):
            at = part * 2 * LANES
            real = jnp.zeros((levels, LANES), jnp.float32)
            imag = jnp.zeros((levels, LANES), jnp.float32)
            for step in range(BLOCKS):
                rows = slice(step * levels, (step + 1) * levels)
                cosine = outer_inv[member, step : step + 1, at : at + LANES]
                sine = outer_inv[member, step : step + 1, at + LANES : at + 2 * LANES]
                even, odd = sums[rows, at : at + LANES], sums[rows, at + LANES : at + 2 * LANES]
                real += even * cosine + odd * sine
                imag += odd * cosine - even * sine
            reals.append(real)
            imags.append(imag)
        analysed = jnp.concatenate([jnp.concatenate(reals, axis=1), jnp.concatenate(imags, axis=1)], axis=0)
        back[pl.ds(member, slots, stride=row_count), :] = dot(analysed.T.astype(jnp.bfloat16), place[1], NN)

    rotate(0)
    copies[3].wait()
    values, sums, results = {0: spread(0)}, {}, []
    for member in range(row_count):
        if member + 1 < row_count:
            rotate(member + 1)
        if member == 1:
            copies[4].wait()
            copies[5].wait()
        if member > 0:
            sums[member - 1] = analyse(member - 1)
        results.append(multiply(member, values.pop(member)))
        if member + 1 < row_count:
            values[member + 1] = spread(member + 1)
        if member > 0:
            collect(member - 1, sums.pop(member - 1))
    collect(row_count - 1, analyse(row_count - 1))
    pack_lines(back, sent, each)
    for result in results:
        result.wait()


def add_three_kernel(two, two_x, three, four, out, out_x):
    out[...] = (
        two[...].astype(jnp.float32) + three[0].astype(jnp.float32) + four[...].astype(jnp.float32)
    ).astype(jnp.bfloat16)
    out_x[...] = (two_x[...].astype(jnp.float32) + three[1].astype(jnp.float32)).astype(jnp.bfloat16)


def add_own_kernel(own, one, one_x, two, two_x, out):
    total = own[...]
    for landed in (one, one_x, two, two_x):
        total = total + landed[...].astype(jnp.float32)
    groups, cols, _ = out.shape
    for group in range(groups):
        out[group] = total[group * cols : (group + 1) * cols]


def shards(spectra, legendre, lat_weight, wave_of_slot, lat_of_row, lon_count):
    waves = lax.axis_size("wave")
    fields = lax.axis_size("field")
    zs = fields // 2
    wave_id = lax.axis_index("wave").astype(jnp.int32).reshape(1)
    field_id = lax.axis_index("field").astype(jnp.int32).reshape(1)
    slots, _, degrees, cols = spectra.shape
    band = legendre.shape[2]
    rows = 2 * band
    row_count = rows // waves
    all_slots = wave_of_slot.shape[0]
    levels = cols * fields
    each = row_count * slots
    coded = slots * 2 * cols

    like_cores = [list(range(0, fields, 2)), list(range(fields - 1, 0, -2))]

    def hop(x, by, cross=0):
        pairs = [
            (i, (2 * (i // 2 + side_of(i % 2) * by) + (i % 2 ^ cross)) % fields) for i in range(fields)
        ]
        return lax.ppermute(x, "field", pairs)

    def swap(x):
        return hop(x, 0, 1)

    def local(kernel, out_shape, name, micros, mebibytes=8, in_specs=None, out_specs=None, scratch=()):
        if in_specs is None:
            in_specs = pl.BlockSpec(memory_space=pltpu.VMEM)
        return pl.pallas_call(
            kernel,
            out_shape=out_shape,
            in_specs=in_specs,
            out_specs=jax.tree.map(lambda _: vmem(), out_shape) if out_specs is None else out_specs,
            scratch_shapes=list(scratch),
            compiler_params=params(mebibytes),
            cost_estimate=cost(micros),
            name=name,
        )

    row_table = jax.ShapeDtypeStruct((slots, rows, degrees), jnp.bfloat16)
    fourier_shape = jax.ShapeDtypeStruct((waves, 4, each // 4 * LANES), jnp.bfloat16)
    float_rows = pltpu.VMEM(((waves + 1) * each, LANES), jnp.float32)

    own = jnp.transpose(spectra, (0, 1, 3, 2)).reshape(coded, degrees)
    gathered = lax.all_gather(own, "field", axis_index_groups=like_cores)
    gathered, legendre = lax.optimization_barrier((gathered, jnp.transpose(legendre, (0, 2, 1))))
    gathered_x = swap(gathered)
    legendre_x = swap(legendre)

    def ordered_rows(values, band_of):
        return local(
            functools.partial(legendre_rows_kernel, waves=waves, fields=fields),
            row_table,
            "legendre_rows",
            2,
            in_specs=[smem(), smem(), hbm(), hbm(), hbm()],
            scratch=[
                pltpu.SMEM(wave_of_slot.shape, jnp.int32),
                pltpu.SMEM(lat_of_row.shape, jnp.int32),
                pltpu.VMEM((slots, band, degrees), jnp.bfloat16),
                pltpu.VMEM((rows, LANES), jnp.float32),
                pltpu.VMEM((rows, LANES), jnp.float32),
                pltpu.SemaphoreType.DMA((3,)),
            ],
        )(wave_id, band_of, in_hbm(wave_of_slot), in_hbm(lat_of_row), in_hbm(values))

    table = ordered_rows(legendre, field_id)
    gathered_x, legendre_x = lax.optimization_barrier((gathered_x, legendre_x))
    outgoing = local(
        legendre_forward_kernel, fourier_shape, "legendre_forward", 4, 16, in_specs=[vmem()] * 3, scratch=[float_rows]
    )(gathered, gathered_x, table)
    outgoing, lat_weight = lax.optimization_barrier((outgoing, lat_weight))
    arrived = lax.all_to_all(outgoing, "wave", split_axis=0, concat_axis=0, tiled=True)
    tables = (
        ((row_count, BLOCK, 2 * all_slots), jnp.bfloat16),
        ((row_count, 2 * all_slots, BLOCK), jnp.bfloat16),
        ((row_count, 16, 2 * all_slots), jnp.float32),
        ((row_count, 16, 2 * all_slots), jnp.float32),
        ((2, LANES, LANES), jnp.bfloat16),
        ((row_count, 8, LANES), jnp.float32),
    )
    tables_vmem = [pltpu.VMEM(shape, kind) for shape, kind in tables]
    prepared = local(
        functools.partial(fourier_tables_kernel, fields=fields, zs=zs),
        [pltpu.HBM(shape, kind) for shape, kind in tables],
        "fourier_tables",
        4,
        16,
        in_specs=[smem()] * 5 + [vmem()],
        out_specs=[hbm()] * 6,
        scratch=tables_vmem + [pltpu.SemaphoreType.DMA((6,))],
    )(
        wave_id, field_id, lat_of_row, lon_count, lat_weight,
        wave_of_slot.astype(jnp.float32).reshape(1, all_slots),
    )
    arrived, prepared = lax.optimization_barrier((arrived, prepared))
    prepared = [in_hbm(x) for x in prepared]

    grid_field, sent = local(
        fourier_kernel,
        (jax.ShapeDtypeStruct((row_count, levels, LONPAD), jnp.bfloat16), fourier_shape),
        "fourier",
        6,
        32,
        in_specs=[vmem()] + [hbm()] * 6,
        out_specs=(hbm(), vmem()),
        scratch=tables_vmem + [
            float_rows,
            float_rows,
            pltpu.VMEM((row_count, BLOCKS * levels, 2 * all_slots), jnp.bfloat16),
            pltpu.VMEM((row_count, BLOCKS * levels, BLOCK), jnp.bfloat16),
            pltpu.VMEM((row_count, levels, LONPAD), jnp.bfloat16),
            pltpu.SemaphoreType.DMA((6,)),
            pltpu.SemaphoreType.DMA((row_count,)),
        ],
    )(arrived, *prepared)

    sent, legendre_x = lax.optimization_barrier((sent, legendre_x))
    returned = lax.all_to_all(sent, "wave", split_axis=0, concat_axis=0, tiled=True)

    table_x = ordered_rows(legendre_x, field_id ^ 1)
    returned, table_x = lax.optimization_barrier((returned, table_x))

    chunk = jax.ShapeDtypeStruct((coded, degrees), jnp.bfloat16)
    own, one, one_x, two, two_x, three, four = local(
        legendre_inverse_kernel,
        (
            jax.ShapeDtypeStruct((coded, degrees), jnp.float32),
            chunk, chunk, chunk, chunk, jax.ShapeDtypeStruct((2, coded, degrees), jnp.bfloat16), chunk,
        ),
        "legendre_inverse",
        2,
        16,
        in_specs=[vmem()] * 4,
        scratch=[float_rows, float_rows],
    )(returned, swap(returned), table, table_x)
    three, four = hop(three, -1), hop(four, -2)
    two, two_x = local(add_three_kernel, (chunk, chunk), "add_three", 1, in_specs=[vmem()] * 4)(
        two, two_x, three, four
    )
    one, one_x = hop(one, -1), hop(one_x, -1, 1)
    two, two_x = hop(two, -2), hop(two_x, -2, 1)
    total = local(
        add_own_kernel,
        jax.ShapeDtypeStruct((2 * slots, cols, degrees), jnp.float32),
        "add_own",
        1,
        in_specs=[vmem()] * 5,
    )(own, one, one_x, two, two_x)
    spectral = jnp.transpose(total.reshape(slots, 2, cols, degrees), (0, 1, 3, 2))
    return grid_field, spectral


def solution(mesh):
    in_specs = (P("wave", None, None, "field"), P("wave", None, "field"), P("field"), P(), P(), P())
    out_specs = (P(("wave", "field"), None, None), P("wave", None, None, "field"))
    return jax.shard_map(shards, mesh=mesh, in_specs=in_specs, out_specs=out_specs, check_vma=False)
```

```python
import functools
import math

import jax
import jax.numpy as jnp
from jax import lax
from jax.experimental import pallas as pl
from jax.experimental.pallas import tpu as pltpu
from jax.sharding import PartitionSpec as P

LONPAD = 3200
LANES = 128
BLOCK = 256
BLOCKS = -(-LONPAD // BLOCK)

NT = (((1,), (1,)), ((), ()))
NN = (((1,), (0,)), ((), ()))
TN = (((0,), (0,)), ((), ()))


def dot(a, b, dims):
    return lax.dot_general(a, b, dims, preferred_element_type=jnp.float32)


def params(mebibytes):
    return pltpu.CompilerParams(vmem_limit_bytes=mebibytes * 1024 * 1024)


def in_hbm(x):
    return pltpu.with_memory_space_constraint(x, pltpu.HBM)


def cost(micros):
    return pl.CostEstimate(flops=0, bytes_accessed=int(micros * 3.7e6), transcendentals=0)


def smem():
    return pl.BlockSpec(memory_space=pltpu.SMEM)


def vmem():
    return pl.BlockSpec(memory_space=pltpu.VMEM)


def hbm():
    return pl.BlockSpec(memory_space=pltpu.HBM)


def side_of(core):
    return 1 - 2 * core


def legendre_rows_kernel(
    wave_id, field_id, wave_of_slot, lat_of_row, legendre, out,
    slot_waves, row_lats, held, pick, south, sems, *, waves, fields,
):
    sources = ((lat_of_row, row_lats), (wave_of_slot, slot_waves), (legendre, held))
    copies = [pltpu.make_async_copy(source, target, sems.at[i]) for i, (source, target) in enumerate(sources)]
    for copy in copies:
        copy.start()
    slots, band, degrees = held.shape
    rows = out.shape[1]
    row_count = rows // waves
    half = row_lats.shape[0] // 2
    own, field = wave_id[0], field_id[0]
    lane = lax.broadcasted_iota(jnp.int32, (1, LANES), 1)
    copies[0].wait()
    for row in range(rows):
        member, wave = divmod(row, waves)
        lat = row_lats[(wave * fields + field) * row_count + member]
        is_south = lat >= half
        hemi = jnp.where(is_south, 2 * half - 1 - lat, lat) - field * band
        pick[row : row + 1, :] = (lane == hemi).astype(jnp.float32)
        south[row : row + 1, :] = jnp.broadcast_to(is_south.astype(jnp.float32), (1, LANES))
    copies[1].wait()
    copies[2].wait()
    offsets = lax.broadcasted_iota(jnp.int32, (1, degrees), 1)
    sign = 1.0 - 2.0 * (south[:, :1] * (offsets & 1).astype(jnp.float32))
    chosen = pick[:, :band].astype(jnp.bfloat16)
    for slot in range(slots):
        live = offsets < degrees - slot_waves[own * slots + slot]
        out[slot] = jnp.where(live, dot(chosen, held[slot], NN) * sign, 0.0).astype(jnp.bfloat16)


def sin_cos(phase, period):
    inverse = 1.0 / period
    turns = (phase - jnp.floor(phase * inverse + 0.5) * period) * inverse
    quarter = jnp.floor(4.0 * turns + 0.5)
    w = (2.0 * math.pi) * (turns - 0.25 * quarter)
    w2 = w * w
    sine = w * (1.0 + w2 * (-1.0 / 6 + w2 * (1.0 / 120 + w2 * (-1.0 / 5040 + w2 * (1.0 / 362880)))))
    cosine = 1.0 + w2 * (-0.5 + w2 * (1.0 / 24 + w2 * (-1.0 / 720 + w2 * (1.0 / 40320))))
    size = jnp.abs(quarter)
    odd = size == 1.0
    flipped = size >= 2.0
    cos_out = jnp.where(odd, sine, cosine)
    sin_out = jnp.where(odd, cosine, sine)
    cos_out = jnp.where(flipped | (quarter == 1.0), -cos_out, cos_out)
    sin_out = jnp.where(flipped | (quarter == -1.0), -sin_out, sin_out)
    return cos_out, sin_out


def fourier_tables_kernel(
    wave_id, field_id, lat_of_row, lon_count, lat_weight, waves_row,
    inner_out, inner_t_out, outer_fwd_out, outer_inv_out, place_out, limits_out,
    inner, inner_t, outer_fwd, outer_inv, place, limits, sems, *, fields, zs,
):
    row_count = inner.shape[0]
    band = lat_weight.shape[0]
    half = lon_count.shape[0]
    slots = waves_row.shape[1]
    steps = outer_fwd.shape[1]
    wave, field = wave_id[0], field_id[0]
    for member in range(row_count):
        lat = lat_of_row[(wave * fields + field) * row_count + member]
        hemi = jnp.where(lat >= half, 2 * half - 1 - lat, lat)
        points = lon_count[hemi].astype(jnp.float32)
        period = jnp.broadcast_to(points, (1, LANES))
        limits[member] = jnp.broadcast_to(points, limits.shape[1:])
        weight = lat_weight[hemi - field * band] / jnp.sqrt(period)
        for part in range(slots // LANES):
            m = waves_row[:, part * LANES : (part + 1) * LANES]
            at = part * 2 * LANES
            x = lax.broadcasted_iota(jnp.int32, (BLOCK, LANES), 0).astype(jnp.float32)
            cosine, sine = sin_cos(x * m, period)
            both = jnp.concatenate([cosine, -sine], axis=1)
            inner[member, :, at : at + 2 * LANES] = both.astype(jnp.bfloat16)
            inner_t[member, at : at + 2 * LANES, :] = both.T.astype(jnp.bfloat16)
            x = (BLOCK * lax.broadcasted_iota(jnp.int32, (steps, LANES), 0)).astype(jnp.float32)
            cosine, sine = sin_cos(x * m, period)
            both = jnp.concatenate([cosine, sine], axis=1)
            outer_fwd[member, :, at : at + 2 * LANES] = both * (1.0 / math.sqrt(slots))
            outer_inv[member, :, at : at + 2 * LANES] = both * jnp.concatenate([weight, weight], axis=1)
    at = lax.broadcasted_iota(jnp.int32, (LANES, LANES), 1)
    core, chunk, part, low = (field & 1) ^ (at >> 6), (at >> 3) & 7, (at >> 2) & 1, at & 3
    away = (chunk + 1) >> 1
    cross = ((chunk & 1) ^ 1) & (chunk > 0).astype(jnp.int32)
    z = ((field >> 1) - side_of(core) * away + zs) & (zs - 1)
    row = lax.broadcasted_iota(jnp.int32, (LANES, LANES), 0)
    gathered_z = chunk + core * (zs - 1 - 2 * chunk)
    for way, shard in enumerate((2 * gathered_z + core, 2 * z + (core ^ cross))):
        place[way] = (row == part * 64 + shard * 4 + low).astype(jnp.bfloat16)
    results = (
        (inner, inner_out), (inner_t, inner_t_out), (outer_fwd, outer_fwd_out),
        (outer_inv, outer_inv_out), (place, place_out), (limits, limits_out),
    )
    copies = [pltpu.make_async_copy(source, target, sems.at[i]) for i, (source, target) in enumerate(results)]
    for copy in copies:
        copy.start()
    for copy in copies:
        copy.wait()


def unpack_lines(messages, held, each):
    for at in range(messages.shape[0]):
        message = messages[at].astype(jnp.float32)
        for group in range(each // 4):
            first = at * each + 4 * group
            held[first : first + 4, :] = message[:, group * LANES : (group + 1) * LANES]


def pack_lines(held, messages, each):
    for at in range(messages.shape[0]):
        groups = [held[at * each + 4 * group : at * each + 4 * group + 4, :] for group in range(each // 4)]
        messages[at] = jnp.concatenate(groups, axis=1).astype(jnp.bfloat16)


def legendre_forward_kernel(gathered, gathered_x, table, out, held):
    slots, rows, degrees = table.shape
    waves = out.shape[0]
    row_count = rows // waves
    each = slots * row_count
    for pair in range(slots // 2):
        at = pl.ds(16 * pair, 16)
        both = [source[z, at, :].astype(jnp.float32) for source in (gathered, gathered_x) for z in range(source.shape[0])]
        for half in range(2):
            slot = 2 * pair + half
            spec = jnp.concatenate([b[8 * half : 8 * half + 8] for b in both], axis=0).astype(jnp.bfloat16)
            sums = dot(table[slot], spec, NT)
            for member in range(row_count):
                held[pl.ds(slot * row_count + member, waves, stride=each), :] = sums[
                    waves * member : waves * (member + 1)
                ]
    pack_lines(held, out, each)


def legendre_inverse_kernel(
    arrived, swapped, table, table_swapped, own, one, one_x, two, two_x, three, four, held, held_swapped
):
    slots, rows, degrees = table.shape
    waves = arrived.shape[0]
    row_count = rows // waves
    each = slots * row_count
    unpack_lines(arrived, held, each)
    unpack_lines(swapped, held_swapped, each)

    def share(ref, slot, legendre, turn=0):
        weighted = jnp.concatenate(
            [ref[pl.ds(slot * row_count + member, waves, stride=each), :] for member in range(row_count)], axis=0
        )
        if turn:
            weighted = pltpu.roll(weighted, turn, 1)
        return dot(weighted[:, :64].astype(jnp.bfloat16), legendre[slot], TN)

    for pair in range(slots // 2):
        at = pl.ds(16 * pair, 16)
        sums = [
            share(held, slot, table) + share(held_swapped, slot, table_swapped, 64) for slot in (2 * pair, 2 * pair + 1)
        ]
        pieces = [jnp.concatenate([s[8 * chunk : 8 * chunk + 8] for s in sums], axis=0) for chunk in range(8)]
        own[at, :] = pieces[0]
        targets = (one, one_x, two, two_x, three.at[0], three.at[1], four)
        for target, piece in zip(targets, pieces[1:]):
            target[at, :] = piece.astype(jnp.bfloat16)


def fourier_kernel(
    arrived, inner_in, inner_t_in, outer_fwd_in, outer_inv_in, place_in, limits_in,
    grid_out, sent,
    inner, inner_t, outer_fwd, outer_inv, place, limits, held, back, turned, products, lines_out, sems, out_sems,
):
    inputs = (
        (place_in, place), (outer_fwd_in, outer_fwd), (limits_in, limits),
        (inner_t_in, inner_t), (inner_in, inner), (outer_inv_in, outer_inv),
    )
    copies = [pltpu.make_async_copy(source, target, sems.at[i]) for i, (source, target) in enumerate(inputs)]
    for copy in copies:
        copy.start()
    row_count = inner.shape[0]
    each = arrived.shape[1] * arrived.shape[2] // LANES
    slots = arrived.shape[0] * each // row_count
    parts = slots // LANES
    levels = grid_out.shape[1]
    unpack_lines(arrived, held, each)
    for copy in copies[:3]:
        copy.wait()
    column = lax.broadcasted_iota(jnp.int32, (1, BLOCK), 1).astype(jnp.float32)

    def rotate(member):
        lines = held[pl.ds(member, slots, stride=row_count), :].astype(jnp.bfloat16)
        coef = dot(place[0], lines, NT)
        for step in range(BLOCKS):
            rows = pl.ds(step * levels, levels)
            for part in range(parts):
                real = coef[:levels, part * LANES : (part + 1) * LANES]
                imag = coef[levels:, part * LANES : (part + 1) * LANES]
                at = part * 2 * LANES
                cosine = outer_fwd[member, step : step + 1, at : at + LANES]
                sine = outer_fwd[member, step : step + 1, at + LANES : at + 2 * LANES]
                turned[member, rows, at : at + LANES] = (real * cosine - imag * sine).astype(jnp.bfloat16)
                turned[member, rows, at + LANES : at + 2 * LANES] = (real * sine + imag * cosine).astype(jnp.bfloat16)

    def spread(member):
        return dot(turned[member], inner_t[member], NN)

    def multiply(member, values):
        points = jnp.concatenate([limits[member, :1, :]] * (BLOCK // LANES), axis=1)
        for step in range(BLOCKS):
            width = min(BLOCK, LONPAD - step * BLOCK)
            line = values[step * levels : (step + 1) * levels]
            line = jnp.where(column + step * BLOCK < points, line, 0.0).astype(jnp.bfloat16)
            lines_out[member, :, step * BLOCK : step * BLOCK + width] = line[:, :width]
            line = line.astype(jnp.float32)
            partner = pltpu.roll(line, levels - 1, 0)
            products[member, step * levels : (step + 1) * levels, :] = (line * partner).astype(jnp.bfloat16)
        result = pltpu.make_async_copy(lines_out.at[member], grid_out.at[member], out_sems.at[member])
        result.start()
        return result

    def analyse(member):
        return dot(products[member], inner[member], NN)

    def collect(member, sums):
        reals, imags = [], []
        for part in range(parts):
            at = part * 2 * LANES
            real = jnp.zeros((levels, LANES), jnp.float32)
            imag = jnp.zeros((levels, LANES), jnp.float32)
            for step in range(BLOCKS):
                rows = slice(step * levels, (step + 1) * levels)
                cosine = outer_inv[member, step : step + 1, at : at + LANES]
                sine = outer_inv[member, step : step + 1, at + LANES : at + 2 * LANES]
                even, odd = sums[rows, at : at + LANES], sums[rows, at + LANES : at + 2 * LANES]
                real += even * cosine + odd * sine
                imag += odd * cosine - even * sine
            reals.append(real)
            imags.append(imag)
        analysed = jnp.concatenate([jnp.concatenate(reals, axis=1), jnp.concatenate(imags, axis=1)], axis=0)
        back[pl.ds(member, slots, stride=row_count), :] = dot(analysed.T.astype(jnp.bfloat16), place[1], NN)

    rotate(0)
    copies[3].wait()
    values, sums, results = {0: spread(0)}, {}, []
    for member in range(row_count):
        if member + 1 < row_count:
            rotate(member + 1)
        if member == 1:
            copies[4].wait()
            copies[5].wait()
        if member > 0:
            sums[member - 1] = analyse(member - 1)
        results.append(multiply(member, values.pop(member)))
        if member + 1 < row_count:
            values[member + 1] = spread(member + 1)
        if member > 0:
            collect(member - 1, sums.pop(member - 1))
    collect(row_count - 1, analyse(row_count - 1))
    pack_lines(back, sent, each)
    for result in results:
        result.wait()


def add_three_kernel(two, two_x, three, four, out, out_x):
    out[...] = (
        two[...].astype(jnp.float32) + three[0].astype(jnp.float32) + four[...].astype(jnp.float32)
    ).astype(jnp.bfloat16)
    out_x[...] = (two_x[...].astype(jnp.float32) + three[1].astype(jnp.float32)).astype(jnp.bfloat16)


def add_own_kernel(own, one, one_x, two, two_x, out):
    total = own[...]
    for landed in (one, one_x, two, two_x):
        total = total + landed[...].astype(jnp.float32)
    groups, cols, _ = out.shape
    for group in range(groups):
        out[group] = total[group * cols : (group + 1) * cols]


def shards(spectra, legendre, lat_weight, wave_of_slot, lat_of_row, lon_count):
    waves = lax.axis_size("wave")
    fields = lax.axis_size("field")
    zs = fields // 2
    wave_id = lax.axis_index("wave").astype(jnp.int32).reshape(1)
    field_id = lax.axis_index("field").astype(jnp.int32).reshape(1)
    slots, _, degrees, cols = spectra.shape
    band = legendre.shape[2]
    rows = 2 * band
    row_count = rows // waves
    all_slots = wave_of_slot.shape[0]
    levels = cols * fields
    each = row_count * slots
    coded = slots * 2 * cols

    like_cores = [list(range(0, fields, 2)), list(range(fields - 1, 0, -2))]

    def hop(x, by, cross=0):
        pairs = [
            (i, (2 * (i // 2 + side_of(i % 2) * by) + (i % 2 ^ cross)) % fields) for i in range(fields)
        ]
        return lax.ppermute(x, "field", pairs)

    def swap(x):
        return hop(x, 0, 1)

    def local(kernel, out_shape, name, micros, mebibytes=8, in_specs=None, out_specs=None, scratch=()):
        if in_specs is None:
            in_specs = pl.BlockSpec(memory_space=pltpu.VMEM)
        return pl.pallas_call(
            kernel,
            out_shape=out_shape,
            in_specs=in_specs,
            out_specs=jax.tree.map(lambda _: vmem(), out_shape) if out_specs is None else out_specs,
            scratch_shapes=list(scratch),
            compiler_params=params(mebibytes),
            cost_estimate=cost(micros),
            name=name,
        )

    row_table = jax.ShapeDtypeStruct((slots, rows, degrees), jnp.bfloat16)
    fourier_shape = jax.ShapeDtypeStruct((waves, 4, each // 4 * LANES), jnp.bfloat16)
    float_rows = pltpu.VMEM(((waves + 1) * each, LANES), jnp.float32)

    own = jnp.transpose(spectra, (0, 1, 3, 2)).reshape(coded, degrees)
    gathered = lax.all_gather(own, "field", axis_index_groups=like_cores)
    gathered, legendre = lax.optimization_barrier((gathered, jnp.transpose(legendre, (0, 2, 1))))
    gathered_x = swap(gathered)
    legendre_x = swap(legendre)

    def ordered_rows(values, band_of):
        return local(
            functools.partial(legendre_rows_kernel, waves=waves, fields=fields),
            row_table,
            "legendre_rows",
            2,
            in_specs=[smem(), smem(), hbm(), hbm(), hbm()],
            scratch=[
                pltpu.SMEM(wave_of_slot.shape, jnp.int32),
                pltpu.SMEM(lat_of_row.shape, jnp.int32),
                pltpu.VMEM((slots, band, degrees), jnp.bfloat16),
                pltpu.VMEM((rows, LANES), jnp.float32),
                pltpu.VMEM((rows, LANES), jnp.float32),
                pltpu.SemaphoreType.DMA((3,)),
            ],
        )(wave_id, band_of, in_hbm(wave_of_slot), in_hbm(lat_of_row), in_hbm(values))

    table = ordered_rows(legendre, field_id)
    outgoing = local(
        legendre_forward_kernel, fourier_shape, "legendre_forward", 4, 16, in_specs=[vmem()] * 3, scratch=[float_rows]
    )(gathered, gathered_x, table)
    outgoing, lat_weight, legendre_x = lax.optimization_barrier((outgoing, lat_weight, legendre_x))
    arrived = lax.all_to_all(outgoing, "wave", split_axis=0, concat_axis=0, tiled=True)
    tables = (
        ((row_count, BLOCK, 2 * all_slots), jnp.bfloat16),
        ((row_count, 2 * all_slots, BLOCK), jnp.bfloat16),
        ((row_count, 16, 2 * all_slots), jnp.float32),
        ((row_count, 16, 2 * all_slots), jnp.float32),
        ((2, LANES, LANES), jnp.bfloat16),
        ((row_count, 8, LANES), jnp.float32),
    )
    tables_vmem = [pltpu.VMEM(shape, kind) for shape, kind in tables]
    prepared = local(
        functools.partial(fourier_tables_kernel, fields=fields, zs=zs),
        [pltpu.HBM(shape, kind) for shape, kind in tables],
        "fourier_tables",
        4,
        16,
        in_specs=[smem()] * 5 + [vmem()],
        out_specs=[hbm()] * 6,
        scratch=tables_vmem + [pltpu.SemaphoreType.DMA((6,))],
    )(
        wave_id, field_id, lat_of_row, lon_count, lat_weight,
        wave_of_slot.astype(jnp.float32).reshape(1, all_slots),
    )
    arrived, prepared = lax.optimization_barrier((arrived, prepared))
    prepared = [in_hbm(x) for x in prepared]

    grid_field, sent = local(
        fourier_kernel,
        (jax.ShapeDtypeStruct((row_count, levels, LONPAD), jnp.bfloat16), fourier_shape),
        "fourier",
        6,
        32,
        in_specs=[vmem()] + [hbm()] * 6,
        out_specs=(hbm(), vmem()),
        scratch=tables_vmem + [
            float_rows,
            float_rows,
            pltpu.VMEM((row_count, BLOCKS * levels, 2 * all_slots), jnp.bfloat16),
            pltpu.VMEM((row_count, BLOCKS * levels, BLOCK), jnp.bfloat16),
            pltpu.VMEM((row_count, levels, LONPAD), jnp.bfloat16),
            pltpu.SemaphoreType.DMA((6,)),
            pltpu.SemaphoreType.DMA((row_count,)),
        ],
    )(arrived, *prepared)

    sent, legendre_x = lax.optimization_barrier((sent, legendre_x))
    returned = lax.all_to_all(sent, "wave", split_axis=0, concat_axis=0, tiled=True)

    table_x = ordered_rows(legendre_x, field_id ^ 1)
    returned, table_x = lax.optimization_barrier((returned, table_x))

    chunk = jax.ShapeDtypeStruct((coded, degrees), jnp.bfloat16)
    own, one, one_x, two, two_x, three, four = local(
        legendre_inverse_kernel,
        (
            jax.ShapeDtypeStruct((coded, degrees), jnp.float32),
            chunk, chunk, chunk, chunk, jax.ShapeDtypeStruct((2, coded, degrees), jnp.bfloat16), chunk,
        ),
        "legendre_inverse",
        2,
        16,
        in_specs=[vmem()] * 4,
        scratch=[float_rows, float_rows],
    )(returned, swap(returned), table, table_x)
    three, four = hop(three, -1), hop(four, -2)
    two, two_x = local(add_three_kernel, (chunk, chunk), "add_three", 1, in_specs=[vmem()] * 4)(
        two, two_x, three, four
    )
    one, one_x = hop(one, -1), hop(one_x, -1, 1)
    two, two_x = hop(two, -2), hop(two_x, -2, 1)
    total = local(
        add_own_kernel,
        jax.ShapeDtypeStruct((2 * slots, cols, degrees), jnp.float32),
        "add_own",
        1,
        in_specs=[vmem()] * 5,
    )(own, one, one_x, two, two_x)
    spectral = jnp.transpose(total.reshape(slots, 2, cols, degrees), (0, 1, 3, 2))
    return grid_field, spectral


def solution(mesh):
    in_specs = (P("wave", None, None, "field"), P("wave", None, "field"), P("field"), P(), P(), P())
    out_specs = (P(("wave", "field"), None, None), P("wave", None, None, "field"))
    return jax.shard_map(shards, mesh=mesh, in_specs=in_specs, out_specs=out_specs, check_vma=False)
```
